32 devices in a mesh: replica: 8 (over z, core), tensor: 4 (over y, x).
Axes of the slice: x: 2, y: 2, z: 4, core: 2. Of those that a mesh axis runs over, the one named last changes fastest.
Arguments:
- x_input: bfloat16 [2048, 4096], P('replica', 'tensor'), may hold values from -6 to 6
- z_input: bfloat16 [2048, 4096], P('replica', 'tensor'), may hold values from -6 to 6
- bc_input: bfloat16 [2048, 1024], P('replica'), may hold values from -6 to 6
- dt_raw: float32 [2048, 128], P('replica', 'tensor'), may hold values from -6 to 6
- dt_bias: float32 [128], P('tensor'), may hold values from -3 to -1
- decay_rates: float32 [128], P('tensor'), may hold values from 0.005 to 0.5
- skip_gain: float32 [128], P('tensor'), may hold values from 0.5 to 1.5
- conv_x: float32 [4, 4096], P(None, 'tensor'), may hold values from -3 to 3
- conv_bc: float32 [4, 1024], replicated, may hold values from -3 to 3
- norm_gain: float32 [4096], P('tensor'), may hold values from 0.5 to 1.5
- out_weight: bfloat16 [4096, 4096], P('tensor'), may hold values from -0.09375 to 0.09375
- cached_states: float32 [16, 128, 32, 128], P('replica', 'tensor'), may hold values from -4 to 4
- cached_tail_x: float32 [16, 3, 4096], P('replica', None, 'tensor'), may hold values from -6 to 6
- cached_tail_bc: float32 [16, 3, 1024], P('replica'), may hold values from -6 to 6
- prefix_block: int32 [16], replicated, may hold values from 0 to 15, as said below
- lengths: int32 [16], P('replica'), may hold values from 128 to 128, as said below
Outputs:
- mixed: bfloat16 [2048, 4096], P(('replica', 'tensor'))
- final_states: float32 [16, 128, 32, 128], P('replica', 'tensor')
The draws below stay inside these ranges and needn't reach their ends.
Inputs may be any that keep to these rules, and one draw needn't show every extreme that they name: A permutation: request q (on replica q // 2) starts from cached block prefix_block[q], which replica prefix_block[q] // 2 holds; every cached block feeds exactly one request. `lengths`: every request's suffix fills all 128 of its slots, so every entry is 128.
All inputs are finite; a program needn't handle non-finite values.
Results may differ from the reference program's by a relative error of at most 0.015.
Values may be sent and summed in bfloat16 or wider, within the bound.
No kernel may reach another device: no remote copies, remote signals or barrier semaphores. Data moves between devices by JAX's collectives and lax.ppermute only.
A program may use at most 64 MiB of HBM per device.

```python
import math
import jax
import jax.numpy as jnp
from jax import lax

HEADS = 128
HEAD_DIM = 32
STATE = 128
GROUPS = 4
CONV = 4
DOUT = 4096
SPAN = 128
REQ = 2
SLOT_LEN = 128
INNER = 4096
TOKENS = 2048
BLOCKS = 16
N_TENSOR = 4


def draw_lengths(key, part):
    most_blocks = SLOT_LEN // SPAN
    counts = jax.random.randint(jax.random.fold_in(key, 11), (BLOCKS,), 1, most_blocks + 1)
    fullest = jax.random.randint(jax.random.fold_in(key, 12), (), 0, BLOCKS)
    step_away = jax.random.randint(jax.random.fold_in(key, 13), (), 1, BLOCKS)
    shortest = (fullest + step_away) % BLOCKS
    places = jnp.arange(BLOCKS)
    counts = jnp.where(places == fullest, most_blocks, counts)
    counts = jnp.where(places == shortest, 1, counts)
    return (counts * SPAN).astype(jnp.int32)


def draw_prefix_block(key, part):
    replicas = BLOCKS // REQ
    shuffled = jax.random.permutation(jax.random.fold_in(key, 21), BLOCKS).astype(jnp.int32)
    chosen = jax.random.randint(jax.random.fold_in(key, 22), (), 0, BLOCKS).astype(jnp.int32)
    far_slot = jax.random.randint(jax.random.fold_in(key, 23), (), 0, REQ).astype(jnp.int32)
    target = (chosen // REQ + replicas // 2) % replicas * REQ + far_slot
    places = jnp.arange(BLOCKS, dtype=jnp.int32)
    holder = jnp.sum(jnp.where(shuffled == target, places, 0)).astype(jnp.int32)
    previous = jnp.sum(jnp.where(places == chosen, shuffled, 0)).astype(jnp.int32)
    result = jnp.where(places == chosen, target, jnp.where(places == holder, previous, shuffled))
    return result.astype(jnp.int32)


def block_levels(own_key, extent, cuts, low, top_value):
    factor_of = 1.0
    for position, parts in cuts:
        heights = jax.random.uniform(jax.random.fold_in(jax.random.fold_in(own_key, 6), position), (parts,), jnp.float32, low / len(cuts), top_value / len(cuts))
        factor_of = factor_of * jnp.repeat(jnp.exp(heights), extent[position] // parts).reshape((-1,) + (1,) * (len(extent) - 1 - position))
    return factor_of


def scatter_about(rng, dims, width, bound, cuts=(), kind=jnp.bfloat16):
    drawn = width * jax.random.normal(rng, dims, jnp.float32)
    if cuts:
        drawn = drawn * block_levels(rng, dims, cuts, -0.22, 0.18)
    return jnp.clip(drawn, -bound, bound).astype(kind)


def setup_inputs(seed: int = 0) -> dict:
    key_of = jax.random.split(jax.random.key(seed), 17)
    x_input = scatter_about(key_of[0], (TOKENS, INNER), 1.0, 6.0, ((0, 8), (1, 4)))
    z_input = scatter_about(key_of[1], (TOKENS, INNER), 1.0, 6.0, ((0, 8), (1, 4)))
    bc_input = scatter_about(key_of[2], (TOKENS, 2 * GROUPS * STATE), 1.0, 6.0, ((0, 8),))
    dt_raw = scatter_about(key_of[3], (TOKENS, HEADS), 1.0, 6.0, ((0, 8), (1, 4)), jnp.float32)
    dt_bias = jnp.clip(-3.0 + 2.0 * jax.random.uniform(key_of[4], (HEADS,), jnp.float32) ** block_levels(key_of[4], (HEADS,), ((0, 4),), -0.2, 0.2), -3.0, -1.0)
    decay_rates = jnp.clip(jnp.exp(math.log(0.5) - 4.6051702 * jax.random.uniform(key_of[5], (HEADS,), jnp.float32) ** block_levels(key_of[5], (HEADS,), ((0, 4),), -0.2, 0.2)), 0.005, 0.5)
    skip_gain = jnp.clip(0.5 + 1.0 * jax.random.uniform(key_of[6], (HEADS,), jnp.float32) ** block_levels(key_of[6], (HEADS,), ((0, 4),), -0.2, 0.2), 0.5, 1.5)
    conv_x = scatter_about(key_of[7], (CONV, INNER), CONV ** -0.5, 3.0, ((1, 4),), jnp.float32)
    conv_bc = scatter_about(key_of[8], (CONV, 2 * GROUPS * STATE), CONV ** -0.5, 3.0, (), jnp.float32)
    norm_gain = jnp.clip(1.0 + 0.1 * jax.random.normal(key_of[9], (INNER,), jnp.float32), 0.5, 1.5)
    out_weight = scatter_about(key_of[10], (INNER, DOUT), INNER ** -0.5, 0.09375, ((0, 4),))
    cached_states = scatter_about(key_of[11], (BLOCKS, HEADS, HEAD_DIM, STATE), 0.5, 4.0, ((0, 8), (1, 4)), jnp.float32)
    cached_tail_x = scatter_about(key_of[12], (BLOCKS, CONV - 1, INNER), 1.0, 6.0, ((0, 8), (2, 4)), jnp.float32)
    cached_tail_bc = scatter_about(key_of[13], (BLOCKS, CONV - 1, 2 * GROUPS * STATE), 1.0, 6.0, ((0, 8),), jnp.float32)
    prefix_block = draw_prefix_block(jax.random.fold_in(key_of[16], 71), 0)
    lengths = draw_lengths(jax.random.fold_in(key_of[16], 71), 0)
    return {"x_input": x_input, "z_input": z_input, "bc_input": bc_input, "dt_raw": dt_raw, "dt_bias": dt_bias, "decay_rates": decay_rates, "skip_gain": skip_gain, "conv_x": conv_x, "conv_bc": conv_bc, "norm_gain": norm_gain, "out_weight": out_weight, "cached_states": cached_states, "cached_tail_x": cached_tail_x, "cached_tail_bc": cached_tail_bc, "prefix_block": prefix_block, "lengths": lengths}


highest = lax.Precision.HIGHEST
epsilon = 1e-05

def causal_conv(tail_rows, sequence, kernel):
    joined = jnp.concatenate([tail_rows, sequence], axis=0)
    length = sequence.shape[0]
    total = joined[0:length] * kernel[0][None, :]
    for offset in range(1, kernel.shape[0]):
        total = total + joined[offset:offset + length] * kernel[offset][None, :]
    return jax.nn.silu(total)

def span_scan(inputs, b_heads, c_heads, step_sizes, decay_rates, skip_gain, carry_state):
    logdec = -step_sizes * decay_rates[None, :]
    cumulative = jnp.cumsum(logdec, axis=0)
    count_rows = inputs.shape[0]
    causal = jnp.arange(count_rows)[:, None] >= jnp.arange(count_rows)[None, :]
    cum_heads = jnp.transpose(cumulative)
    differ = cum_heads[:, :, None] - cum_heads[:, None, :]
    decays = jnp.where(causal[None, :, :], jnp.exp(jnp.minimum(differ, 0.0)), 0.0)
    scores = jnp.einsum('ihn,jhn->hij', c_heads, b_heads, precision=highest)
    weights = scores * decays * jnp.transpose(step_sizes)[:, None, :]
    inside = jnp.einsum('hij,jhp->ihp', weights, inputs, precision=highest)
    carried = jnp.exp(cumulative)[:, :, None] * jnp.einsum('ihn,hpn->ihp', c_heads, carry_state, precision=highest)
    output = inside + carried + skip_gain[None, :, None] * inputs
    ending = cumulative[-1]
    weigh_in = jnp.exp(ending[None, :] - cumulative) * step_sizes
    new_state = jnp.exp(ending)[:, None, None] * carry_state + jnp.einsum('jh,jhp,jhn->hpn', weigh_in, inputs, b_heads, precision=highest)
    return (output, new_state)

def request_forward(x_seq, bc_seq, dt_seq, length, carry_state, tail_x, tail_bc, conv_x, conv_bc, dt_bias, decay_rates, skip_gain, member):
    count_rows = x_seq.shape[0]
    heads_here = dt_seq.shape[1]
    inputs = causal_conv(tail_x, x_seq.astype(jnp.float32), conv_x).reshape(count_rows, heads_here, HEAD_DIM)
    bc_conv = causal_conv(tail_bc, bc_seq.astype(jnp.float32), conv_bc)
    b_groups = bc_conv[:, :GROUPS * STATE].reshape(count_rows, GROUPS, STATE)
    c_groups = bc_conv[:, GROUPS * STATE:].reshape(count_rows, GROUPS, STATE)
    b_heads = jnp.einsum('lgn,hg->lhn', b_groups, member, precision=highest)
    c_heads = jnp.einsum('lgn,hg->lhn', c_groups, member, precision=highest)
    live = (jnp.arange(count_rows) < length)[:, None]
    step_sizes = jnp.where(live, jax.nn.softplus(dt_seq + dt_bias[None, :]), 0.0)
    pieces = []
    for start in range(0, count_rows, SPAN):
        output, carry_state = span_scan(inputs[start:start + SPAN], b_heads[start:start + SPAN], c_heads[start:start + SPAN], step_sizes[start:start + SPAN], decay_rates, skip_gain, carry_state)
        pieces.append(output)
    return (jnp.concatenate(pieces, axis=0).reshape(count_rows, -1), carry_state)

def reference(x_input, z_input, bc_input, dt_raw, dt_bias, decay_rates, skip_gain, conv_x, conv_bc, norm_gain, out_weight, cached_states, cached_tail_x, cached_tail_bc, prefix_block, lengths):
    member = ((jnp.arange(HEADS) // (HEADS // GROUPS))[:, None] == jnp.arange(GROUPS)[None, :]).astype(jnp.float32)
    start_states = jnp.take(cached_states, prefix_block, axis=0)
    start_tail_x = jnp.take(cached_tail_x, prefix_block, axis=0)
    start_tail_bc = jnp.take(cached_tail_bc, prefix_block, axis=0)

    def one_request(items):
        x_seq, bc_seq, dt_seq, length, carry_state, tail_x, tail_bc = items
        return request_forward(x_seq, bc_seq, dt_seq, length, carry_state, tail_x, tail_bc, conv_x, conv_bc, dt_bias, decay_rates, skip_gain, member)
    outputs, final_states = lax.map(one_request, (x_input.reshape(BLOCKS, SLOT_LEN, INNER), bc_input.reshape(BLOCKS, SLOT_LEN, 2 * GROUPS * STATE), dt_raw.reshape(BLOCKS, SLOT_LEN, HEADS), lengths, start_states, start_tail_x, start_tail_bc))
    outputs = outputs.reshape(TOKENS, INNER)
    live = (jnp.arange(SLOT_LEN)[None, :] < lengths[:, None]).reshape(TOKENS, 1)
    gate_vals = outputs * jax.nn.silu(z_input.astype(jnp.float32))
    grouped = gate_vals.reshape(TOKENS, GROUPS, INNER // GROUPS)
    mean_sq = lax.optimization_barrier(jnp.mean(grouped * grouped, axis=2, keepdims=True))
    normed = (grouped * lax.rsqrt(mean_sq + epsilon)).reshape(TOKENS, INNER) * norm_gain[None, :]
    gated = jnp.where(live, normed, 0.0).astype(jnp.bfloat16)
    block_rows = INNER // N_TENSOR

    def add_block(number, total):
        rows_in = lax.dynamic_slice_in_dim(gated, number * block_rows, block_rows, 1)
        weight_rows = lax.dynamic_slice_in_dim(out_weight, number * block_rows, block_rows, 0)
        part = jnp.dot(rows_in, weight_rows, preferred_element_type=jnp.float32).astype(jnp.bfloat16)
        part = lax.optimization_barrier(part)
        return total + part.astype(jnp.float32)
    mixed = lax.fori_loop(0, N_TENSOR, add_block, jnp.zeros((TOKENS, DOUT), jnp.float32)).astype(jnp.bfloat16)
    return (mixed, final_states)
```

```python
import math
from functools import partial

import jax
import jax.numpy as jnp
from jax import lax
from jax.experimental import pallas as pl
from jax.experimental.pallas import tpu as pltpu
from jax.sharding import PartitionSpec as P

HEADS = 128
HEAD_DIM = 32
STATE = 128
GROUPS = 4
CONV = 4


highest = lax.Precision.HIGHEST
epsilon = 1e-05
f32 = jnp.float32
bf16 = jnp.bfloat16
LOG2E = math.log2(math.e)
VMEM_LIMIT = 40 * 1024 * 1024


def causal_conv(tail_rows, sequence, kernel):
    joined = jnp.concatenate([tail_rows, sequence], axis=0)
    length = sequence.shape[0]
    total = joined[0:length] * kernel[0][None, :]
    for offset in range(1, kernel.shape[0]):
        total = total + joined[offset : offset + length] * kernel[offset][None, :]
    return jax.nn.silu(total)


def span_scan(inputs, b_heads, c_heads, step_sizes, decay_rates, skip_gain, carry_state):
    logdec = -step_sizes * decay_rates[None, :]
    cumulative = jnp.cumsum(logdec, axis=0)
    count_rows = inputs.shape[0]
    causal = jnp.arange(count_rows)[:, None] >= jnp.arange(count_rows)[None, :]
    cum_heads = jnp.transpose(cumulative)
    differ = cum_heads[:, :, None] - cum_heads[:, None, :]
    decays = jnp.where(causal[None, :, :], jnp.exp(jnp.minimum(differ, 0.0)), 0.0)
    scores = jnp.einsum("ihn,jhn->hij", c_heads, b_heads, precision=highest)
    weights = scores * decays * jnp.transpose(step_sizes)[:, None, :]
    inside = jnp.einsum("hij,jhp->ihp", weights, inputs, precision=highest)
    carried = jnp.exp(cumulative)[:, :, None] * jnp.einsum(
        "ihn,hpn->ihp", c_heads, carry_state, precision=highest
    )
    output = inside + carried + skip_gain[None, :, None] * inputs
    ending = cumulative[-1]
    weigh_in = jnp.exp(ending[None, :] - cumulative) * step_sizes
    new_state = jnp.exp(ending)[:, None, None] * carry_state + jnp.einsum(
        "jh,jhp,jhn->hpn", weigh_in, inputs, b_heads, precision=highest
    )
    return (output, new_state)


def local_any(
    x_input,
    z_input,
    bc_input,
    dt_raw,
    dt_bias,
    decay_rates,
    skip_gain,
    conv_x,
    conv_bc,
    norm_gain,
    out_weight,
    cached_states,
    cached_tail_x,
    cached_tail_bc,
    prefix_block,
    lengths,
):
    requests = lengths.shape[0]
    local_heads = dt_raw.shape[1]
    tokens_dev = x_input.shape[0]
    slot_len = tokens_dev // requests
    wanted = lax.dynamic_slice_in_dim(prefix_block, lax.axis_index("replica") * requests, requests)

    def migrate(rows):
        rows = lax.all_gather(rows.astype(bf16), "replica", axis=0, tiled=True)
        return jnp.take(rows, wanted, axis=0).astype(f32)

    start_states = migrate(cached_states)
    start_tail_x = migrate(cached_tail_x)
    start_tail_bc = migrate(cached_tail_bc)
    head_ids = lax.axis_index("tensor") * local_heads + jnp.arange(local_heads)
    member = ((head_ids // (HEADS // GROUPS))[:, None] == jnp.arange(GROUPS)[None, :]).astype(f32)
    live = jnp.arange(slot_len)[None, :] < lengths[:, None]
    outputs = []
    finals = []
    for request in range(requests):
        row_lo = request * slot_len
        row_hi = row_lo + slot_len
        inputs = causal_conv(
            start_tail_x[request], x_input[row_lo:row_hi].astype(f32), conv_x
        ).reshape(slot_len, local_heads, HEAD_DIM)
        bc_conv = causal_conv(
            start_tail_bc[request], bc_input[row_lo:row_hi].astype(f32), conv_bc
        )
        b_groups = bc_conv[:, : GROUPS * STATE].reshape(slot_len, GROUPS, STATE)
        c_groups = bc_conv[:, GROUPS * STATE :].reshape(slot_len, GROUPS, STATE)
        b_heads = jnp.einsum("lgn,hg->lhn", b_groups, member, precision=highest)
        c_heads = jnp.einsum("lgn,hg->lhn", c_groups, member, precision=highest)
        step_sizes = jnp.where(
            live[request][:, None], jax.nn.softplus(dt_raw[row_lo:row_hi] + dt_bias[None, :]), 0.0
        )
        output, carry_state = span_scan(
            inputs, b_heads, c_heads, step_sizes, decay_rates, skip_gain, start_states[request]
        )
        outputs.append(output.reshape(slot_len, -1))
        finals.append(carry_state)
    outputs = jnp.concatenate(outputs, axis=0)
    final_states = jnp.stack(finals, axis=0)
    gate_vals = outputs * jax.nn.silu(z_input.astype(f32))
    by_head = gate_vals.reshape(tokens_dev, local_heads, HEAD_DIM)
    head_squares = jnp.sum(by_head * by_head, axis=2)
    partial_sq = jnp.dot(head_squares, member, precision=highest)
    totals = lax.psum(partial_sq, "tensor")
    mean_sq = jnp.dot(totals, jnp.transpose(member), precision=highest) / (
        HEADS * HEAD_DIM // GROUPS
    )
    normed = (by_head * lax.rsqrt(mean_sq + epsilon)[:, :, None]).reshape(
        tokens_dev, -1
    ) * norm_gain[None, :]
    gated = jnp.where(live.reshape(tokens_dev, 1), normed, 0.0).astype(bf16)
    mixed = lax.psum_scatter(
        jnp.dot(gated, out_weight, preferred_element_type=f32).astype(bf16),
        "tensor",
        scatter_dimension=0,
        tiled=True,
    )
    return (mixed, final_states)


CHIPS = 4
SLOTS = 2
ITEMS = 2 * SLOTS
ROWS = 1024
HALF = ROWS // 2
TAIL = 32
LANES = 128
COLUMN_BLOCKS = ROWS // LANES
DIRECT = (4, 2, 2)
EXTRA = 2

VMEM = pl.BlockSpec(memory_space=pltpu.VMEM)
SMEM = pl.BlockSpec(memory_space=pltpu.SMEM)


def sds(shape, dtype):
    return jax.ShapeDtypeStruct(shape, dtype)


def params(**kw):
    return pltpu.CompilerParams(vmem_limit_bytes=VMEM_LIMIT, **kw)


def cost(nbytes, flops=0):
    return pl.CostEstimate(flops=flops, bytes_accessed=nbytes, transcendentals=0)


def silu(value):
    half = 0.5 * value
    return half + half * jnp.tanh(half)


def chip_and_core():
    replica = lax.axis_index("replica")
    return replica // 2, lax.rem(replica, 2)


def pack_kernel(states, tail_x, tail_bc, keep, send, scratch):
    _, core = chip_and_core()
    group = lax.axis_index("tensor")
    for block in range(SLOTS):
        keep[block, :HALF, :] = states[block, pl.ds(core * HALF, HALF), :].astype(bf16)
        send[block, :HALF, :] = states[block, pl.ds((1 - core) * HALF, HALF), :].astype(bf16)
        for s in range(COLUMN_BLOCKS):
            scratch[3 * s : 3 * s + 3, :] = tail_x[block, :, s * LANES : (s + 1) * LANES]
        for s in range(2):
            at = pl.multiple_of((s * GROUPS + group) * STATE, STATE)
            row = 3 * (COLUMN_BLOCKS + s)
            scratch[row : row + 3, :] = tail_bc[block, :, pl.ds(at, STATE)]
        scratch[30:32, :] = jnp.zeros((2, LANES), f32)
        rows = scratch[...].astype(bf16)
        keep[block, HALF:, :] = rows
        send[block, HALF:, :] = rows


def rank_of(prefix, chip, place):
    source = prefix[chip * ITEMS + place] // ITEMS
    rank = jnp.int32(0)
    for other in range(ITEMS):
        same = prefix[chip * ITEMS + other] // ITEMS == source
        rank += jnp.where((other < place) & same, 1, 0)
    return source, rank


def copy_item(out, at, keep, recv, item, core, rows):
    slot = lax.rem(item, SLOTS)
    mine = item // SLOTS == core

    @pl.when(mine)
    def _():
        out[at] = keep[slot, rows, :]

    @pl.when(jnp.logical_not(mine))
    def _():
        out[at] = recv[slot, rows, :]


def compacted(prefix, chip, target, slot):
    item = jnp.int32(0)
    for place in range(ITEMS):
        source, rank = rank_of(prefix, target, place)
        hit = (source == chip) & (rank == slot)
        item = jnp.where(hit, lax.rem(prefix[target * ITEMS + place], ITEMS), item)
    return item


def select_kernel(prefix, keep, recv, s1, s2, s3, t0, t1, t2, t3):
    chip, core = chip_and_core()
    state_rows = pl.ds(0, HALF)
    tail_rows = pl.ds(HALF, TAIL)
    for d, tails in enumerate((t0, t1, t2, t3)):
        target = jnp.bitwise_xor(chip, d)
        for slot in range(SLOTS):
            block = prefix[target * ITEMS + core * SLOTS + slot]
            copy_item(tails, slot, keep, recv, lax.rem(block, ITEMS), core, tail_rows)
    target = jnp.bitwise_xor(chip, 1)
    for slot in range(ITEMS):
        block = prefix[target * ITEMS + slot]
        copy_item(s1, slot, keep, recv, lax.rem(block, ITEMS), core, state_rows)
    for d, out in ((2, s2), (3, s3)):
        target = jnp.bitwise_xor(chip, d)
        for slot in range(DIRECT[d - 1]):
            item = compacted(prefix, chip, target, slot)
            copy_item(out, slot, keep, recv, item, core, state_rows)


def extra_kernel(prefix, keep, recv, o2, o3):
    chip, core = chip_and_core()
    for d, out in ((2, o2), (3, o3)):
        target = jnp.bitwise_xor(chip, d)
        for slot in range(EXTRA):
            item = compacted(prefix, chip, target, DIRECT[d - 1] + slot)
            copy_item(out, slot, keep, recv, item, core, pl.ds(0, HALF))


def place_kernel(has_extra, prefix, keep, recv, r1, r2, r3, *rest):
    if has_extra:
        o2, o3, mine, other = rest
    else:
        mine, other = rest
    chip, core = chip_and_core()
    for out, owner in ((mine, core), (other, 1 - core)):
        for slot in range(SLOTS):
            place = owner * SLOTS + slot
            source, rank = rank_of(prefix, chip, place)
            d = jnp.bitwise_xor(source, chip)
            item = lax.rem(prefix[chip * ITEMS + place], ITEMS)

            @pl.when(d == 0)
            def _():
                copy_item(out, slot, keep, recv, item, core, pl.ds(0, HALF))

            @pl.when(d == 1)
            def _():
                out[slot] = r1[place]

            for e, r in ((2, r2), (3, r3)):
                few = DIRECT[e - 1]

                @pl.when((d == e) & (rank < few))
                def _():
                    out[slot] = r[jnp.minimum(rank, few - 1)]

                if has_extra:
                    o = o2 if e == 2 else o3

                    @pl.when((d == e) & (rank >= few))
                    def _():
                        out[slot] = o[jnp.clip(rank - few, 0, EXTRA - 1)]


def scan_kernel(
    prefix,
    lengths,
    x_in,
    z_in,
    bc_in,
    dt_raw,
    dt_bias,
    decay,
    skip,
    conv_x,
    conv_bc,
    t0,
    t1,
    t2,
    t3,
    y_in,
    y_scale,
    c_out,
    s_add,
    s_scale,
    u,
    tails,
):
    chip, core = chip_and_core()
    group = lax.axis_index("tensor")
    span = x_in.shape[0] // SLOTS
    heads = dt_raw.shape[1]
    row = lax.broadcasted_iota(jnp.int32, (span, span), 0)
    column = lax.broadcasted_iota(jnp.int32, (span, span), 1)
    causal = row >= column
    lower = causal.astype(f32)
    head_row = lax.broadcasted_iota(jnp.int32, (heads, ROWS), 0)
    head_column = lax.broadcasted_iota(jnp.int32, (heads, ROWS), 1) // HEAD_DIM
    expand = (head_row == head_column).astype(f32)
    skip_wide = jnp.dot(skip[...], expand, precision=highest, preferred_element_type=f32)
    per_block = LANES // HEAD_DIM
    lane_head = lax.broadcasted_iota(jnp.int32, (span, LANES), 1) // HEAD_DIM
    for r in range(SLOTS):
        rows = slice(r * span, (r + 1) * span)
        source = prefix[chip * ITEMS + core * SLOTS + r] // ITEMS
        d = jnp.bitwise_xor(source, chip)
        tail = t0[r].astype(f32)
        for e, t in ((1, t1), (2, t2), (3, t3)):
            tail = jnp.where(d == e, t[r].astype(f32), tail)
        tails[...] = tail
        for s in range(COLUMN_BLOCKS + 2):
            u[5:8, s * LANES : (s + 1) * LANES] = tails[3 * s : 3 * s + 3, :]
        u[8 : 8 + span, :ROWS] = x_in[rows, :].astype(f32)
        for s in range(2):
            at = pl.multiple_of((s * GROUPS + group) * STATE, STATE)
            lo = ROWS + s * STATE
            u[8 : 8 + span, lo : lo + STATE] = bc_in[rows, pl.ds(at, STATE)].astype(f32)

        def conv(lo, taps):
            total = u[5 : 5 + span, lo : lo + LANES] * taps(0)
            for k in range(1, CONV):
                total = total + u[5 + k : 5 + k + span, lo : lo + LANES] * taps(k)
            return silu(total)

        def bc_conv(s):
            at = pl.multiple_of((s * GROUPS + group) * STATE, STATE)
            return conv(ROWS + s * STATE, lambda k: conv_bc[k : k + 1, pl.ds(at, STATE)])

        b_mat = bc_conv(0).astype(bf16)
        c_mat = bc_conv(1).astype(bf16)
        c_out[rows, :] = c_mat
        scores = lax.dot_general(
            c_mat, b_mat, (((1,), (1,)), ((), ())), preferred_element_type=f32
        )
        scores = jnp.where(causal, scores, 0.0)

        live = lax.broadcasted_iota(jnp.int32, (span, heads), 0) < lengths[r]
        raw = dt_raw[rows, :] + dt_bias[...]
        steps = jnp.maximum(raw, 0.0) + jnp.log1p(jnp.exp(-jnp.abs(raw)))
        steps = jnp.where(live, steps, 0.0)
        logdec = steps * decay[...] * (-LOG2E)
        cum = jnp.dot(lower, logdec, precision=highest, preferred_element_type=f32)
        cum_t = lax.dot_general(
            logdec, lower, (((0,), (1,)), ((), ())), precision=highest, preferred_element_type=f32
        )
        ending = cum[span - 1 : span, :]
        s_scale[r] = jnp.broadcast_to(jnp.exp2(cum_t[:, span - 1 : span]), (heads, LANES))
        weigh = jnp.exp2(ending - cum) * steps
        wide = jnp.dot(
            jnp.concatenate([steps, weigh, jnp.exp2(cum)], axis=0),
            expand,
            precision=highest,
            preferred_element_type=f32,
        )
        for q in range(COLUMN_BLOCKS):
            lo = q * LANES
            cols = slice(lo, lo + LANES)
            xc = conv(lo, lambda k: conv_x[k : k + 1, cols])
            xdt_q = (xc * wide[:span, cols]).astype(bf16)
            xw = (xc * wide[span : 2 * span, cols]).astype(bf16)
            s_add[r, lo : lo + LANES, :] = lax.dot_general(
                xw, b_mat, (((0,), (0,)), ((), ())), preferred_element_type=f32
            )
            total = skip_wide[:, cols] * xc
            parts = []
            masked = []
            for i in range(per_block):
                h = q * per_block + i
                differ = cum[:, h : h + 1] - cum_t[h : h + 1, :]
                parts.append((jnp.exp2(jnp.minimum(differ, 0.0)) * scores).astype(bf16))
                masked.append(jnp.where(lane_head == i, xdt_q, jnp.zeros_like(xdt_q)))
            total = total + jnp.dot(
                jnp.concatenate(parts, axis=1),
                jnp.concatenate(masked, axis=0),
                preferred_element_type=f32,
            )
            gate = silu(z_in[rows, cols].astype(f32))
            y_in[rows, cols] = total * gate
            y_scale[rows, cols] = wide[2 * span :, cols] * gate


def gate_rows(lengths, y_in, y_scale, c_in, mine, other, gain, gated, start):
    _, core = chip_and_core()
    span = y_in.shape[0] // SLOTS
    for r in range(SLOTS):
        rows = slice(r * span, (r + 1) * span)
        start[pl.ds(pl.multiple_of(core * HALF, HALF), HALF), :] = mine[r]
        start[pl.ds(pl.multiple_of((1 - core) * HALF, HALF), HALF), :] = other[r]
        carried = lax.dot_general(
            c_in[rows, :], start[...], (((1,), (1,)), ((), ())), preferred_element_type=f32
        )
        value = y_in[rows, :] + y_scale[rows, :] * carried
        mean_sq = jnp.mean(value * value, axis=1, keepdims=True)
        live = lax.broadcasted_iota(jnp.int32, (span, 1), 0) < lengths[r]
        scale = jnp.where(live, lax.rsqrt(mean_sq + epsilon), 0.0)
        gated[rows, :] = (value * scale * gain[...]).astype(bf16)


def project_kernel(first, *refs):
    if first:
        lengths, y_in, y_scale, c_in, mine, other, gain, weight = refs[:8]
        gated, l_send, l_own, l_on, r_send, r_own, r_on, start = refs[8:]
    else:
        gated, weight, l_send, l_own, l_on, r_send, r_own, r_on = refs
    step = pl.program_id(0)
    half = pl.num_programs(0) // 2
    if first:

        @pl.when(step == 0)
        def _():
            gate_rows(lengths, y_in, y_scale, c_in, mine, other, gain, gated, start)

    tensor = lax.axis_index("tensor")
    x, y = lax.rem(tensor, 2), tensor // 2
    rows = gated.shape[0] // 4

    def product(at_y, at_x):
        block = gated[pl.ds(pl.multiple_of((at_y * 2 + at_x) * rows, rows), rows), :]
        return jnp.dot(block, weight[...], preferred_element_type=f32).astype(bf16)

    @pl.when(step < half)
    def _():
        l_send[0] = product(y, 1 - x)
        l_send[1] = product(1 - y, 1 - x)
        l_own[...] = product(y, x)
        l_on[...] = product(1 - y, x)

    @pl.when(step >= half)
    def _():
        r_send[0] = product(1 - y, x)
        r_send[1] = product(1 - y, 1 - x)
        r_own[...] = product(y, x)
        r_on[...] = product(y, 1 - x)


def final_kernel(mine, other, s_add, s_scale, out):
    _, core = chip_and_core()
    heads = s_scale.shape[1] // 2

    def put(half, piece):
        at = pl.ds(pl.multiple_of(half * HALF, HALF), HALF)
        scale = s_scale[0, pl.ds(pl.multiple_of(half * heads, heads), heads), :]
        state = piece[0].astype(f32).reshape(heads, HEAD_DIM, LANES)
        value = (state * scale[:, None, :]).reshape(HALF, LANES) + s_add[0, at, :]
        out[0, at, :] = value

    put(core, mine)
    put(1 - core, other)


def local_square(
    x_input,
    z_input,
    bc_input,
    dt_raw,
    dt_bias,
    decay_rates,
    skip_gain,
    conv_x,
    conv_bc,
    norm_gain,
    out_weight,
    cached_states,
    cached_tail_x,
    cached_tail_bc,
    prefix_block,
    lengths,
):
    tokens = x_input.shape[0]
    heads = dt_raw.shape[1]
    features = out_weight.shape[1]

    def over_replica(value, bits):
        pairs = [(r, r ^ bits) for r in range(2 * CHIPS)]
        return lax.ppermute(value, "replica", pairs)

    def over_tensor(value, bits):
        return lax.ppermute(value, "tensor", [(t, t ^ bits) for t in range(4)])

    half_items = sds((SLOTS, HALF, LANES), bf16)
    with jax.named_scope("pack"):
        keep, send = pl.pallas_call(
            pack_kernel,
            out_shape=(sds((SLOTS, HALF + TAIL, LANES), bf16),) * 2,
            in_specs=[VMEM] * 3,
            out_specs=(VMEM, VMEM),
            scratch_shapes=[pltpu.VMEM((TAIL, LANES), f32)],
            compiler_params=params(),
        )(cached_states.reshape(SLOTS, ROWS, LANES), cached_tail_x, cached_tail_bc)
    recv = over_replica(send, 1)

    with jax.named_scope("select"):
        s1, s2, s3, t0, t1, t2, t3 = pl.pallas_call(
            select_kernel,
            out_shape=tuple(sds((n, HALF, LANES), bf16) for n in DIRECT)
            + (sds((SLOTS, TAIL, LANES), bf16),) * 4,
            in_specs=[SMEM, VMEM, VMEM],
            out_specs=(VMEM,) * 7,
            compiler_params=params(),
        )(prefix_block, keep, recv)
    t1, t2, t3 = (over_replica(t, 2 * d) for d, t in ((1, t1), (2, t2), (3, t3)))
    r1, r2, r3 = (over_replica(s, 2 * d) for d, s in ((1, s1), (2, s2), (3, s3)))

    with jax.named_scope("scan"):
        span = tokens // SLOTS
        y_in, y_scale, c_mat, s_add, s_scale = pl.pallas_call(
            scan_kernel,
            out_shape=(
                sds((tokens, ROWS), f32),
                sds((tokens, ROWS), f32),
                sds((tokens, STATE), bf16),
                sds((SLOTS, ROWS, STATE), f32),
                sds((SLOTS, heads, LANES), f32),
            ),
            in_specs=[SMEM, SMEM] + [VMEM] * 13,
            out_specs=(VMEM,) * 5,
            scratch_shapes=[
                pltpu.VMEM((8 + span, ROWS + 2 * STATE), f32),
                pltpu.VMEM((TAIL, LANES), f32),
            ],
            compiler_params=params(),
            cost_estimate=cost(8 << 20, 1 << 30),
        )(
            prefix_block,
            lengths,
            x_input,
            z_input,
            bc_input,
            dt_raw,
            dt_bias.reshape(1, heads),
            decay_rates.reshape(1, heads),
            skip_gain.reshape(1, heads),
            conv_x,
            conv_bc,
            t0,
            t1,
            t2,
            t3,
        )

    chips = prefix_block.reshape(CHIPS, ITEMS) // ITEMS
    distance = jnp.bitwise_xor(chips, jnp.arange(CHIPS)[:, None])
    counts = jnp.stack([jnp.sum(distance == d, axis=1) for d in (2, 3)])
    overflow = jnp.any(counts > DIRECT[1])

    def place(*extra):
        return pl.pallas_call(
            partial(place_kernel, bool(extra)),
            out_shape=(half_items, half_items),
            in_specs=[SMEM] + [VMEM] * (5 + len(extra)),
            out_specs=(VMEM, VMEM),
            compiler_params=params(),
        )(prefix_block, keep, recv, r1, r2, r3, *extra)

    def place_more():
        o2, o3 = pl.pallas_call(
            extra_kernel,
            out_shape=(sds((EXTRA, HALF, LANES), bf16),) * 2,
            in_specs=[SMEM, VMEM, VMEM],
            out_specs=(VMEM, VMEM),
            compiler_params=params(),
        )(prefix_block, keep, recv)
        return place(over_replica(o2, 4), over_replica(o3, 6))

    with jax.named_scope("place"):
        mine, theirs = lax.cond(overflow, place_more, place)
    other = over_replica(theirs, 1)

    chunks = 2
    wide = features // chunks
    block = wide // 4
    quarter = tokens // 4

    def left(n):
        return jnp.minimum(n, 1)

    def right(n):
        return jnp.maximum(n - 2, 0)

    outs = []
    out_specs = []
    for index in (left, right):
        outs += [sds((2, quarter, wide // 2), bf16)] + [sds((quarter, wide // 2), bf16)] * 2
        out_specs += [
            pl.BlockSpec((2, quarter, block), lambda n, index=index: (0, 0, index(n))),
            pl.BlockSpec((quarter, block), lambda n, index=index: (0, index(n))),
            pl.BlockSpec((quarter, block), lambda n, index=index: (0, index(n))),
        ]

    def whole(*shape):
        return pl.BlockSpec(shape, lambda n: (0,) * len(shape))

    pieces = []
    gated = None
    for chunk in range(chunks):
        weight_spec = pl.BlockSpec((ROWS, block), lambda n, chunk=chunk: (0, chunk * 4 + n))
        call = partial(
            pl.pallas_call,
            partial(project_kernel, chunk == 0),
            grid=(4,),
            compiler_params=params(),
            cost_estimate=cost(ROWS * wide * 2, 2 * tokens * ROWS * wide),
        )
        with jax.named_scope("project"):
            if chunk == 0:
                gated, *parts = call(
                    out_shape=[sds((tokens, ROWS), bf16)] + outs,
                    in_specs=[
                        SMEM,
                        whole(tokens, ROWS),
                        whole(tokens, ROWS),
                        whole(tokens, STATE),
                        whole(SLOTS, HALF, LANES),
                        whole(SLOTS, HALF, LANES),
                        whole(1, ROWS),
                        weight_spec,
                    ],
                    out_specs=[whole(tokens, ROWS)] + out_specs,
                    scratch_shapes=[pltpu.VMEM((ROWS, LANES), bf16)],
                )(
                    lengths,
                    y_in,
                    y_scale,
                    c_mat,
                    mine,
                    other,
                    norm_gain.reshape(1, ROWS),
                    out_weight,
                )
            else:
                parts = call(
                    out_shape=outs,
                    in_specs=[whole(tokens, ROWS), weight_spec],
                    out_specs=out_specs,
                )(gated, out_weight)
        pieces.append(parts)

    with jax.named_scope("final_states"):
        row_block = pl.BlockSpec((1, HALF, LANES), lambda n: (n, 0, 0))
        full_block = pl.BlockSpec((1, ROWS, LANES), lambda n: (n, 0, 0))
        final_states = pl.pallas_call(
            final_kernel,
            grid=(SLOTS,),
            out_shape=sds((SLOTS, ROWS, STATE), f32),
            in_specs=[
                row_block,
                row_block,
                full_block,
                pl.BlockSpec((1, heads, LANES), lambda n: (n, 0, 0)),
            ],
            out_specs=full_block,
            compiler_params=params(),
            cost_estimate=cost(4 << 20),
        )(mine, other, s_add, s_scale)

    with jax.named_scope("sum"):
        came = []
        for l_send, _, _, r_send, _, _ in pieces:
            came.append((over_tensor(l_send, 1), over_tensor(r_send, 2)))
        passed = []
        for (l_came, r_came), (_, l_own, l_on, _, r_own, r_on) in zip(came, pieces):
            onward = (l_on.astype(f32) + l_came[1].astype(f32)).astype(bf16)
            l_last = over_tensor(onward, 2)
            onward = (r_on.astype(f32) + r_came[1].astype(f32)).astype(bf16)
            r_last = over_tensor(onward, 1)
            passed.append(
                (
                    l_own.astype(f32) + l_came[0].astype(f32) + l_last.astype(f32),
                    r_own.astype(f32) + r_came[0].astype(f32) + r_last.astype(f32),
                )
            )
        mixed = jnp.concatenate([p for pair in passed for p in pair], axis=1).astype(bf16)

    return (mixed, final_states.reshape(cached_states.shape))


def solution(mesh):
    placed = (
        P("replica", "tensor"),
        P("replica", "tensor"),
        P("replica", None),
        P("replica", "tensor"),
        P("tensor"),
        P("tensor"),
        P("tensor"),
        P(None, "tensor"),
        P(),
        P("tensor"),
        P("tensor", None),
        P("replica", "tensor", None, None),
        P("replica", None, "tensor"),
        P("replica", None, None),
        P(),
        P("replica"),
    )
    square = mesh.shape["replica"] == 2 * CHIPS and mesh.shape["tensor"] == GROUPS
    return jax.shard_map(
        local_square if square else local_any,
        mesh=mesh,
        in_specs=placed,
        out_specs=(P(("replica", "tensor"), None), P("replica", "tensor", None, None)),
        check_vma=False,
    )
```

```python
import math
from functools import partial

import jax
import jax.numpy as jnp
from jax import lax
from jax.experimental import pallas as pl
from jax.experimental.pallas import tpu as pltpu
from jax.sharding import PartitionSpec as P

HEADS = 128
HEAD_DIM = 32
STATE = 128
GROUPS = 4
CONV = 4


highest = lax.Precision.HIGHEST
epsilon = 1e-05
f32 = jnp.float32
bf16 = jnp.bfloat16
LOG2E = math.log2(math.e)
MIB = 1024 * 1024
VMEM_LIMIT = 24


def causal_conv(tail_rows, sequence, kernel):
    joined = jnp.concatenate([tail_rows, sequence], axis=0)
    length = sequence.shape[0]
    total = joined[0:length] * kernel[0][None, :]
    for offset in range(1, kernel.shape[0]):
        total = total + joined[offset : offset + length] * kernel[offset][None, :]
    return jax.nn.silu(total)


def span_scan(inputs, b_heads, c_heads, step_sizes, decay_rates, skip_gain, carry_state):
    logdec = -step_sizes * decay_rates[None, :]
    cumulative = jnp.cumsum(logdec, axis=0)
    count_rows = inputs.shape[0]
    causal = jnp.arange(count_rows)[:, None] >= jnp.arange(count_rows)[None, :]
    cum_heads = jnp.transpose(cumulative)
    differ = cum_heads[:, :, None] - cum_heads[:, None, :]
    decays = jnp.where(causal[None, :, :], jnp.exp(jnp.minimum(differ, 0.0)), 0.0)
    scores = jnp.einsum("ihn,jhn->hij", c_heads, b_heads, precision=highest)
    weights = scores * decays * jnp.transpose(step_sizes)[:, None, :]
    inside = jnp.einsum("hij,jhp->ihp", weights, inputs, precision=highest)
    carried = jnp.exp(cumulative)[:, :, None] * jnp.einsum(
        "ihn,hpn->ihp", c_heads, carry_state, precision=highest
    )
    output = inside + carried + skip_gain[None, :, None] * inputs
    ending = cumulative[-1]
    weigh_in = jnp.exp(ending[None, :] - cumulative) * step_sizes
    new_state = jnp.exp(ending)[:, None, None] * carry_state + jnp.einsum(
        "jh,jhp,jhn->hpn", weigh_in, inputs, b_heads, precision=highest
    )
    return (output, new_state)


def local_any(
    x_input,
    z_input,
    bc_input,
    dt_raw,
    dt_bias,
    decay_rates,
    skip_gain,
    conv_x,
    conv_bc,
    norm_gain,
    out_weight,
    cached_states,
    cached_tail_x,
    cached_tail_bc,
    prefix_block,
    lengths,
):
    requests = lengths.shape[0]
    local_heads = dt_raw.shape[1]
    tokens_dev = x_input.shape[0]
    slot_len = tokens_dev // requests
    wanted = lax.dynamic_slice_in_dim(prefix_block, lax.axis_index("replica") * requests, requests)

    def migrate(rows):
        rows = lax.all_gather(rows.astype(bf16), "replica", axis=0, tiled=True)
        return jnp.take(rows, wanted, axis=0).astype(f32)

    start_states = migrate(cached_states)
    start_tail_x = migrate(cached_tail_x)
    start_tail_bc = migrate(cached_tail_bc)
    head_ids = lax.axis_index("tensor") * local_heads + jnp.arange(local_heads)
    member = ((head_ids // (HEADS // GROUPS))[:, None] == jnp.arange(GROUPS)[None, :]).astype(f32)
    live = jnp.arange(slot_len)[None, :] < lengths[:, None]
    outputs = []
    finals = []
    for request in range(requests):
        row_lo = request * slot_len
        row_hi = row_lo + slot_len
        inputs = causal_conv(
            start_tail_x[request], x_input[row_lo:row_hi].astype(f32), conv_x
        ).reshape(slot_len, local_heads, HEAD_DIM)
        bc_conv = causal_conv(
            start_tail_bc[request], bc_input[row_lo:row_hi].astype(f32), conv_bc
        )
        b_groups = bc_conv[:, : GROUPS * STATE].reshape(slot_len, GROUPS, STATE)
        c_groups = bc_conv[:, GROUPS * STATE :].reshape(slot_len, GROUPS, STATE)
        b_heads = jnp.einsum("lgn,hg->lhn", b_groups, member, precision=highest)
        c_heads = jnp.einsum("lgn,hg->lhn", c_groups, member, precision=highest)
        step_sizes = jnp.where(
            live[request][:, None], jax.nn.softplus(dt_raw[row_lo:row_hi] + dt_bias[None, :]), 0.0
        )
        output, carry_state = span_scan(
            inputs, b_heads, c_heads, step_sizes, decay_rates, skip_gain, start_states[request]
        )
        outputs.append(output.reshape(slot_len, -1))
        finals.append(carry_state)
    outputs = jnp.concatenate(outputs, axis=0)
    final_states = jnp.stack(finals, axis=0)
    gate_vals = outputs * jax.nn.silu(z_input.astype(f32))
    by_head = gate_vals.reshape(tokens_dev, local_heads, HEAD_DIM)
    head_squares = jnp.sum(by_head * by_head, axis=2)
    partial_sq = jnp.dot(head_squares, member, precision=highest)
    totals = lax.psum(partial_sq, "tensor")
    mean_sq = jnp.dot(totals, jnp.transpose(member), precision=highest) / (
        HEADS * HEAD_DIM // GROUPS
    )
    normed = (by_head * lax.rsqrt(mean_sq + epsilon)[:, :, None]).reshape(
        tokens_dev, -1
    ) * norm_gain[None, :]
    gated = jnp.where(live.reshape(tokens_dev, 1), normed, 0.0).astype(bf16)
    mixed = lax.psum_scatter(
        jnp.dot(gated, out_weight, preferred_element_type=f32).astype(bf16),
        "tensor",
        scatter_dimension=0,
        tiled=True,
    )
    return (mixed, final_states)


CHIPS = 4
SLOTS = 2
ITEMS = 2 * SLOTS
ROWS = 1024
HALF = ROWS // 2
TAIL = 32
ITEM_ROWS = HALF + TAIL // 2
LANES = 128
COLUMN_BLOCKS = ROWS // LANES
WIDE = ROWS + 2 * STATE
EARLY = CONV - 1
BASE = (3, 2, 2)
EXTRAS = ((0, 0, 0), (0, 1, 0), (0, 0, 1), (1, 2, 2))
SEND_PLAN = 0
PLACE_PLAN = 3 * ITEMS
CHUNKS = ((0, 4), (4, 8))
TILE = 512

HBM = pl.BlockSpec(memory_space=pltpu.HBM)
ANYWHERE = pl.BlockSpec(memory_space=pl.ANY)
VMEM = pl.BlockSpec(memory_space=pltpu.VMEM)
SMEM = pl.BlockSpec(memory_space=pltpu.SMEM)


def sds(shape, dtype):
    return jax.ShapeDtypeStruct(shape, dtype)


def params():
    return pltpu.CompilerParams(vmem_limit_bytes=VMEM_LIMIT * MIB)


def in_hbm(value):
    return pltpu.with_memory_space_constraint(value, pltpu.HBM)


def cost(nbytes, flops=0):
    return pl.CostEstimate(flops=flops, bytes_accessed=nbytes, transcendentals=0)


def silu(value):
    half = 0.5 * value
    return half + half * jnp.tanh(half)


def chip_and_core():
    replica = lax.axis_index("replica")
    return replica // 2, lax.rem(replica, 2)


def half_at(core):
    return pl.ds(pl.multiple_of(core * HALF, HALF), HALF)


def tail_half(core):
    return pl.ds(pl.multiple_of(core * (TAIL // 2), TAIL // 2), TAIL // 2)


def pack_kernel(
    prefix,
    states,
    tail_x,
    tail_bc,
    send,
    keep,
    plan,
    variant,
    blocks,
    rows_x,
    rows_bc,
    scratch,
    sems,
):
    _, core = chip_and_core()
    group = lax.axis_index("tensor")
    copies = [
        pltpu.make_async_copy(states.at[:, half_at(1 - core)], blocks.at[0], sems.at[0]),
        pltpu.make_async_copy(tail_x, rows_x, sems.at[1]),
        pltpu.make_async_copy(tail_bc, rows_bc, sems.at[2]),
        pltpu.make_async_copy(states.at[:, half_at(core)], blocks.at[1], sems.at[3]),
    ]
    for copy in copies:
        copy.start()
    make_plan(prefix, plan, variant)
    for copy in copies:
        copy.wait()
    scratch[...] = jnp.zeros_like(scratch)
    for block in range(SLOTS):
        for k in range(CONV - 1):
            for s in range(COLUMN_BLOCKS):
                scratch[3 * s + k : 3 * s + k + 1, :] = rows_x[
                    k, block : block + 1, s * LANES : (s + 1) * LANES
                ]
            for s in range(2):
                at = pl.multiple_of((s * GROUPS + group) * STATE, STATE)
                row = 3 * (COLUMN_BLOCKS + s) + k
                scratch[row : row + 1, :] = rows_bc[k, block : block + 1, pl.ds(at, STATE)]
        for part, out in enumerate((send, keep)):
            half = jnp.bitwise_xor(core, 1 - part)
            out[block, :HALF, :] = blocks[part, block].astype(bf16)
            out[block, HALF:, :] = scratch[tail_half(half), :].astype(bf16)


def make_plan(prefix, plan, variant):
    chip, core = chip_and_core()
    need = [jnp.int32(0)] * CHIPS
    for entry in range(PLACE_PLAN):
        plan[SEND_PLAN + entry] = 0
    for target in range(CHIPS):
        blocks = [prefix[target * ITEMS + place] for place in range(ITEMS)]
        sources = [block // ITEMS for block in blocks]
        for place in range(ITEMS):
            source = sources[place]
            item = lax.rem(blocks[place], ITEMS)
            rank = jnp.int32(0)
            for other in range(place):
                rank += jnp.where(sources[other] == source, 1, 0)
            distance = jnp.bitwise_xor(source, target)
            for d in range(1, CHIPS):
                need[d] = jnp.where(distance == d, jnp.maximum(need[d], rank + 1), need[d])

            @pl.when((source == chip) & (distance > 0))
            def _():
                plan[SEND_PLAN + (distance - 1) * ITEMS + rank] = item

            @pl.when(target == chip)
            def _():
                owner = jnp.bitwise_xor(core, place // SLOTS)
                at = PLACE_PLAN + owner * SLOTS + place % SLOTS
                plan[at] = distance * ITEMS + jnp.where(distance == 0, item, rank)

    choice = jnp.int32(len(EXTRAS) - 1)
    for v in reversed(range(len(EXTRAS) - 1)):
        fits = need[1] <= BASE[0] + EXTRAS[v][0]
        for d in range(2, CHIPS):
            fits = fits & (need[d] <= BASE[d - 1] + EXTRAS[v][d - 1])
        choice = jnp.where(fits, v, choice)
    variant[0] = choice


def copy_item(out, at, keep, recv, item, core):
    slot = lax.rem(item, SLOTS)
    mine = item // SLOTS == core

    @pl.when(mine)
    def _():
        out[at] = keep[slot]

    @pl.when(jnp.logical_not(mine))
    def _():
        out[at] = recv[slot]


def select_kernel(first, counts, plan, keep, recv, *outs):
    _, core = chip_and_core()
    outs = iter(outs)
    for d in range(1, CHIPS):
        if counts[d - 1]:
            out = next(outs)
            for slot in range(counts[d - 1]):
                item = plan[SEND_PLAN + (d - 1) * ITEMS + first[d - 1] + slot]
                copy_item(out, slot, keep, recv, item, core)


def spread_kernel(counts, *refs):
    outs = refs[-(CHIPS - 1) :]
    came = iter(refs)
    for n, out in zip(counts, outs):
        if n:
            out[:n] = next(came)[...]


def place_kernel(plan, _, keep, recv, *refs):
    came, (mine, other) = refs[: 2 * (CHIPS - 1)], refs[-2:]
    _, core = chip_and_core()
    for o, out in enumerate((other, mine)):
        for slot in range(SLOTS):
            code = plan[PLACE_PLAN + (1 - o) * SLOTS + slot]
            d = code // ITEMS
            which = lax.rem(code, ITEMS)

            @pl.when(d == 0)
            def _():
                copy_item(out, slot, keep, recv, which, core)

            for e in range(1, CHIPS):
                few = BASE[e - 1]
                base, extra = came[e - 1], came[e + 2]

                @pl.when((d == e) & (which < few))
                def _():
                    out[slot] = base[jnp.minimum(which, few - 1)]

                @pl.when((d == e) & (which >= few))
                def _():
                    out[slot] = extra[jnp.maximum(which - few, 0)]


def scan_kernel(
    _,
    lengths,
    x_in,
    z_in,
    bc_in,
    dt_raw,
    dt_bias,
    decay,
    skip,
    conv_x,
    conv_bc,
    weight,
    y_in,
    y_scale,
    c_out,
    s_add,
    s_scale,
    e_scale,
    early,
    staged,
    u,
    sems,
):
    parts = sems.shape[0]
    deep = weight.shape[0] // parts
    copies = []
    for i in range(parts):
        at = slice(i * deep, (i + 1) * deep)
        copies.append(pltpu.make_async_copy(weight.at[at], staged.at[at], sems.at[i]))
        copies[-1].start()
    group = lax.axis_index("tensor")
    span = x_in.shape[0] // SLOTS
    heads = dt_raw.shape[0]
    row = lax.broadcasted_iota(jnp.int32, (span, span), 0)
    column = lax.broadcasted_iota(jnp.int32, (span, span), 1)
    causal = row >= column
    lower = causal.astype(f32)
    late = causal & (column >= EARLY)
    head_row = lax.broadcasted_iota(jnp.int32, (heads, ROWS), 0)
    head_column = lax.broadcasted_iota(jnp.int32, (heads, ROWS), 1) // HEAD_DIM
    expand = (head_row == head_column).astype(f32)
    skip_wide = jnp.dot(skip[...], expand, precision=highest, preferred_element_type=f32)
    same = lax.broadcasted_iota(jnp.int32, (heads, heads), 0) == lax.broadcasted_iota(
        jnp.int32, (heads, heads), 1
    )

    def upright(value):
        return jnp.sum(jnp.where(same, value, 0.0), axis=1, keepdims=True)

    bias = upright(dt_bias[...])
    rate = upright(decay[...]) * (-LOG2E)
    per_block = LANES // HEAD_DIM
    lane_head = lax.broadcasted_iota(jnp.int32, (span, LANES), 1) // HEAD_DIM
    token = lax.broadcasted_iota(jnp.int32, (heads, span), 1)
    over_last = (((1,), (1,)), ((), ()))
    over_first = (((0,), (0,)), ((), ()))
    u[0:8, :] = jnp.zeros((8, WIDE), f32)
    for r in range(SLOTS):
        rows = slice(r * span, (r + 1) * span)
        u[8 : 8 + span, :ROWS] = x_in[rows, :].astype(f32)
        for s in range(2):
            at = pl.multiple_of((s * GROUPS + group) * STATE, STATE)
            lo = ROWS + s * STATE
            u[8 : 8 + span, lo : lo + STATE] = bc_in[rows, pl.ds(at, STATE)].astype(f32)

        def conv(lo, taps):
            at = slice(lo, lo + LANES)
            total = u[5 : 5 + span, at] * taps(0)
            early[r, 1, 0:1, at] = taps(0)
            for k in range(1, CONV):
                total = total + u[5 + k : 5 + k + span, at] * taps(k)
                early[r, 1, k : k + 1, at] = taps(k)
            early[r, 0, :, at] = total[:8]
            return silu(total)

        def bc_conv(s):
            at = pl.multiple_of((s * GROUPS + group) * STATE, STATE)
            return conv(ROWS + s * STATE, lambda k: conv_bc[k : k + 1, pl.ds(at, STATE)])

        b_mat = bc_conv(0).astype(bf16)
        c_mat = bc_conv(1).astype(bf16)
        c_out[rows, :] = c_mat
        scores = lax.dot_general(c_mat, b_mat, over_last, preferred_element_type=f32)
        scores = jnp.where(late, scores, 0.0)

        raw = dt_raw[:, rows] + bias
        steps = jnp.maximum(raw, 0.0) + jnp.log1p(jnp.exp(-jnp.abs(raw)))
        steps = jnp.where(token < lengths[r], steps, 0.0)
        logdec = steps * rate
        cum = lax.dot_general(
            lower, logdec, over_last, precision=highest, preferred_element_type=f32
        )
        cum_t = lax.dot_general(
            logdec, lower, over_last, precision=highest, preferred_element_type=f32
        )
        begin = cum_t[:, EARLY - 1 : EARLY]
        ending = cum_t[:, span - 1 : span]
        s_scale[r] = jnp.broadcast_to(jnp.exp2(ending - begin), (heads, LANES))
        e_scale[r] = jnp.broadcast_to(jnp.exp2(begin), (heads, LANES))
        weigh = jnp.where(token >= EARLY, jnp.exp2(ending - cum_t) * steps, 0.0)
        since = jnp.exp2(jnp.minimum(cum_t - begin, 0.0))
        wide = lax.dot_general(
            jnp.concatenate([steps, weigh, since, cum_t], axis=1),
            expand,
            over_first,
            precision=highest,
            preferred_element_type=f32,
        )
        early[r, 2, :, :ROWS] = wide[:8]
        early[r, 3, :, :ROWS] = wide[3 * span : 3 * span + 8]
        early[r, 5, :, :ROWS] = jnp.broadcast_to(skip_wide, (8, ROWS))
        for q in range(COLUMN_BLOCKS):
            lo = q * LANES
            cols = slice(lo, lo + LANES)
            xc = conv(lo, lambda k: conv_x[k : k + 1, cols])
            xdt = (xc * wide[:span, cols]).astype(bf16)
            xw = (xc * wide[span : 2 * span, cols]).astype(bf16)
            s_add[r, lo : lo + LANES, :] = lax.dot_general(
                xw, b_mat, over_first, preferred_element_type=f32
            )
            total = skip_wide[:, cols] * xc
            parts = []
            masked = []
            for i in range(per_block):
                h = q * per_block + i
                differ = cum[:, h : h + 1] - cum_t[h : h + 1, :]
                parts.append((jnp.exp2(jnp.minimum(differ, 0.0)) * scores).astype(bf16))
                masked.append(jnp.where(lane_head == i, xdt, jnp.zeros_like(xdt)))
            total = total + jnp.dot(
                jnp.concatenate(parts, axis=1),
                jnp.concatenate(masked, axis=0),
                preferred_element_type=f32,
            )
            gate = silu(z_in[rows, cols].astype(f32))
            early[r, 4, :, cols] = gate[:8]
            y_in[rows, cols] = total * gate
            y_scale[rows, cols] = wide[2 * span : 3 * span, cols] * gate
    for copy in copies:
        copy.wait()


def by_head(state, scale):
    heads = scale.shape[0]
    wide = state.astype(f32).reshape(heads, HEAD_DIM, LANES) * scale[:, None, :]
    return wide.reshape(heads * HEAD_DIM, LANES)


def first_tokens(early, tails):
    row = lax.broadcasted_iota(jnp.int32, (8, WIDE), 0)
    taps = early[1]
    tail = tails[...]
    total = early[0]
    for t in range(EARLY):
        add = sum(taps[k : k + 1] * tail[t + k : t + k + 1] for k in range(EARLY - t))
        total = jnp.where(row == t, total + add, total)
    act = silu(total)
    return act[:, :ROWS], act[:, ROWS : ROWS + STATE], act[:, ROWS + STATE :]


def gate_rows(
    lengths,
    y_in,
    y_scale,
    c_in,
    e_scale,
    early,
    mine,
    other,
    gain,
    gated,
    x_first,
    b_first,
    start,
    tails,
    tail_rows,
):
    _, core = chip_and_core()
    tensor = lax.axis_index("tensor")
    x, y = lax.rem(tensor, 2), tensor // 2
    tokens = y_in.shape[0]
    span = tokens // SLOTS
    quarter = tokens // 4
    over_last = (((1,), (1,)), ((), ()))
    over_first = (((0,), (0,)), ((), ()))
    row = lax.broadcasted_iota(jnp.int32, (8, ROWS), 0)
    tail_rows[...] = jnp.zeros_like(tail_rows)
    for r in range(SLOTS):
        rows = slice(r * span, (r + 1) * span)
        start[half_at(core), :] = mine[r, :HALF]
        start[half_at(1 - core), :] = other[r, :HALF]
        tails[tail_half(core), :] = mine[r, HALF:].astype(f32)
        tails[tail_half(1 - core), :] = other[r, HALF:].astype(f32)
        for s in range(COLUMN_BLOCKS + 2):
            tail_rows[:EARLY, s * LANES : (s + 1) * LANES] = tails[3 * s : 3 * s + 3, :]

        x_8, b_8, c_8 = first_tokens(early[r], tail_rows)
        steps, cum, gate_8 = early[r, 2, :, :ROWS], early[r, 3, :, :ROWS], early[r, 4, :, :ROWS]
        skip = early[r, 5, 0:1, :ROWS]
        moved = steps * x_8
        last = cum[EARLY - 1 : EARLY]
        kept = jnp.where(row < EARLY, jnp.exp2(jnp.minimum(last - cum, 0.0)) * moved, 0.0)
        x_first[r] = kept
        b_first[r] = b_8
        after = by_head(start[...], e_scale[r]) + lax.dot_general(
            kept, b_8, over_first, preferred_element_type=f32
        )
        y_8 = skip * x_8 + jnp.exp2(cum) * lax.dot_general(
            c_8.astype(bf16), start[...], over_last, preferred_element_type=f32
        )
        scores = lax.dot_general(c_8, b_8, over_last, preferred_element_type=f32)
        for j in range(EARLY):
            decay = jnp.exp2(jnp.minimum(cum - cum[j : j + 1], 0.0))
            y_8 += jnp.where(row >= j, scores[:, j : j + 1] * decay * moved[j : j + 1], 0.0)

        carried = lax.dot_general(
            c_in[rows, :], after.astype(bf16), over_last, preferred_element_type=f32
        )
        value = y_in[rows, :] + y_scale[rows, :] * carried
        value = jnp.concatenate([jnp.where(row < EARLY, y_8 * gate_8, value[:8]), value[8:]], axis=0)
        mean_sq = jnp.mean(value * value, axis=1, keepdims=True)
        live = lax.broadcasted_iota(jnp.int32, (span, 1), 0) < lengths[r]
        scale = jnp.where(live, lax.rsqrt(mean_sq + epsilon), 0.0)
        result = (value * scale * gain[...]).astype(bf16)
        for part in range(span // quarter):
            owner = r * (span // quarter) + part
            place = jnp.bitwise_xor(owner // 2, y) + 2 * jnp.bitwise_xor(owner % 2, x)
            at = pl.ds(pl.multiple_of(place * quarter, quarter), quarter)
            gated[at, :] = result[part * quarter : (part + 1) * quarter, :]


def project_kernel(first, columns, *refs):
    if first:
        *ins, weight, gated, x_first, b_first = refs[:13]
        l_send, l_own, l_on, r_send, r_own, r_on, *scratch = refs[13:]
        gate_rows(*ins, gated, x_first, b_first, *scratch)
    else:
        gated, weight, l_send, l_own, l_on, r_send, r_own, r_on = refs
    q = gated.shape[0] // 4
    half = l_own.shape[1]
    tile = min(half, TILE)
    for lo in range(0, 2 * half, tile):
        at = slice(columns + lo, columns + lo + tile)
        product = jnp.dot(gated[...], weight[:, at], preferred_element_type=f32).astype(bf16)
        own, block_y, block_x, block_xy = (product[j * q : (j + 1) * q] for j in range(4))
        if lo < half:
            to = slice(lo, lo + tile)
            l_send[0, :, to] = block_x
            l_send[1, :, to] = block_xy
            l_own[:, to] = own
            l_on[:, to] = block_y
        else:
            to = slice(lo - half, lo - half + tile)
            r_send[0, :, to] = block_y
            r_send[1, :, to] = block_xy
            r_own[:, to] = own
            r_on[:, to] = block_x


def final_kernel(mine, other, x_first, b_first, s_add, s_scale, e_scale, out):
    _, core = chip_and_core()
    heads = s_scale.shape[1] // 2

    def put(half, piece):
        at = half_at(half)
        of = pl.ds(pl.multiple_of(half * heads, heads), heads)
        after = by_head(piece[0, :HALF], e_scale[0, of, :]) + lax.dot_general(
            x_first[0, :, at], b_first[0], (((0,), (0,)), ((), ())), preferred_element_type=f32
        )
        out[0, at, :] = by_head(after, s_scale[0, of, :]) + s_add[0, at, :]

    put(core, mine)
    put(1 - core, other)


def over_replica(value, bits):
    pairs = [(r, r ^ bits) for r in range(2 * CHIPS)]
    return lax.ppermute(value, "replica", pairs)


def over_tensor(value, bits):
    return lax.ppermute(value, "tensor", [(t, t ^ bits) for t in range(4)])


def select(first, counts, plan, keep, recv):
    with jax.named_scope("select"):
        return pl.pallas_call(
            partial(select_kernel, first, counts),
            out_shape=[sds((n, ITEM_ROWS, LANES), bf16) for n in counts if n],
            in_specs=[SMEM, VMEM, VMEM],
            out_specs=[VMEM for n in counts if n],
            compiler_params=params(),
        )(plan, keep, recv)


def exchange(counts, sends):
    bits = [2 * d for d in range(1, CHIPS) if counts[d - 1]]
    return [over_replica(value, b) for value, b in zip(sends, bits)]


def migrate_more(counts, plan, keep, recv):
    came = exchange(counts, select(BASE, counts, plan, keep, recv)) if any(counts) else []
    return pl.pallas_call(
        partial(spread_kernel, counts),
        out_shape=tuple(sds((n, ITEM_ROWS, LANES), bf16) for n in EXTRAS[-1]),
        in_specs=[VMEM] * len(came),
        out_specs=(VMEM,) * (CHIPS - 1),
        compiler_params=params(),
    )(*came)


def local_square(
    x_input,
    z_input,
    bc_input,
    dt_raw,
    dt_bias,
    decay_rates,
    skip_gain,
    conv_x,
    conv_bc,
    norm_gain,
    out_weight,
    cached_states,
    cached_tail_x,
    cached_tail_bc,
    prefix_block,
    lengths,
):
    tokens = x_input.shape[0]
    heads = dt_raw.shape[1]
    features = out_weight.shape[1]
    span = tokens // SLOTS

    with jax.named_scope("pack"):
        send, keep, plan, variant = pl.pallas_call(
            pack_kernel,
            out_shape=(sds((SLOTS, ITEM_ROWS, LANES), bf16),) * 2
            + (sds((PLACE_PLAN + ITEMS,), jnp.int32), sds((1,), jnp.int32)),
            in_specs=[SMEM, HBM, HBM, HBM],
            out_specs=(VMEM, VMEM, SMEM, SMEM),
            scratch_shapes=[
                pltpu.VMEM((2, SLOTS, HALF, LANES), f32),
                pltpu.VMEM((CONV - 1, SLOTS) + cached_tail_x.shape[2:], f32),
                pltpu.VMEM((CONV - 1, SLOTS) + cached_tail_bc.shape[2:], f32),
                pltpu.VMEM((TAIL, LANES), f32),
                pltpu.SemaphoreType.DMA((4,)),
            ],
            compiler_params=params(),
        )(
            prefix_block,
            in_hbm(cached_states.reshape(SLOTS, ROWS, LANES)),
            in_hbm(jnp.transpose(cached_tail_x, (1, 0, 2))),
            in_hbm(jnp.transpose(cached_tail_bc, (1, 0, 2))),
        )
    recv = over_replica(send, 1)
    more = lax.switch(
        variant.reshape(()),
        [partial(migrate_more, counts) for counts in EXTRAS],
        plan,
        keep,
        recv,
    )
    sends = select((0,) * (CHIPS - 1), BASE, plan, keep, recv)
    came = exchange(BASE, sends)

    with jax.named_scope("scan"):
        scale = sds((SLOTS, heads, LANES), f32)
        y_in, y_scale, c_mat, s_add, s_scale, e_scale, early, weight = pl.pallas_call(
            scan_kernel,
            out_shape=(
                sds((tokens, ROWS), f32),
                sds((tokens, ROWS), f32),
                sds((tokens, STATE), bf16),
                sds((SLOTS, ROWS, STATE), f32),
                scale,
                scale,
                sds((SLOTS, 6, 8, WIDE), f32),
                pltpu.VMEM(out_weight.shape, bf16),
            ),
            in_specs=[ANYWHERE, SMEM] + [VMEM] * 9 + [HBM],
            out_specs=(VMEM,) * 8,
            scratch_shapes=[pltpu.VMEM((8 + span, WIDE), f32), pltpu.SemaphoreType.DMA((4,))],
            compiler_params=params(),
            cost_estimate=cost(8 << 20, 1 << 30),
        )(
            sends[0],
            lengths,
            x_input,
            z_input,
            bc_input,
            jnp.transpose(dt_raw),
            dt_bias.reshape(1, heads),
            decay_rates.reshape(1, heads),
            skip_gain.reshape(1, heads),
            conv_x,
            conv_bc,
            in_hbm(out_weight),
        )

    with jax.named_scope("place"):
        mine, theirs = pl.pallas_call(
            place_kernel,
            out_shape=(sds((SLOTS, ITEM_ROWS, LANES), bf16),) * 2,
            in_specs=[SMEM, ANYWHERE] + [VMEM] * 8,
            out_specs=(VMEM, VMEM),
            compiler_params=params(),
        )(plan, c_mat, keep, recv, *came, *more)
    other = over_replica(theirs, 1)

    quarter = tokens // 4
    pieces = []
    gated = None
    for lo, hi in CHUNKS:
        lo, hi = lo * features // 8, hi * features // 8
        half = (hi - lo) // 2
        outs = [sds((2, quarter, half), bf16), sds((quarter, half), bf16), sds((quarter, half), bf16)]
        call = partial(
            pl.pallas_call,
            partial(project_kernel, gated is None, lo),
            compiler_params=params(),
            cost_estimate=cost(ROWS * (hi - lo) * 2, 2 * tokens * ROWS * (hi - lo)),
        )
        with jax.named_scope("project"):
            if gated is None:
                gated, x_first, b_first, *parts = call(
                    out_shape=[
                        sds((tokens, ROWS), bf16),
                        sds((SLOTS, 8, ROWS), f32),
                        sds((SLOTS, 8, STATE), f32),
                    ]
                    + 2 * outs,
                    in_specs=[SMEM] + [VMEM] * 9,
                    out_specs=[VMEM] * 9,
                    scratch_shapes=[
                        pltpu.VMEM((ROWS, LANES), bf16),
                        pltpu.VMEM((TAIL, LANES), f32),
                        pltpu.VMEM((8, WIDE), f32),
                    ],
                )(
                    lengths,
                    y_in,
                    y_scale,
                    c_mat,
                    e_scale,
                    early,
                    mine,
                    other,
                    norm_gain.reshape(1, ROWS),
                    weight,
                )
            else:
                parts = call(
                    out_shape=2 * outs,
                    in_specs=[VMEM, VMEM],
                    out_specs=[VMEM] * 6,
                )(gated, weight)
        pieces.append(parts)

    with jax.named_scope("final_states"):

        def of_request(*shape):
            return pl.BlockSpec((1,) + shape, lambda n: (n,) + (0,) * len(shape))

        final_states = pl.pallas_call(
            final_kernel,
            grid=(SLOTS,),
            out_shape=sds((SLOTS, ROWS, STATE), f32),
            in_specs=[
                of_request(ITEM_ROWS, LANES),
                of_request(ITEM_ROWS, LANES),
                of_request(8, ROWS),
                of_request(8, STATE),
                of_request(ROWS, STATE),
                of_request(heads, LANES),
                of_request(heads, LANES),
            ],
            out_specs=of_request(ROWS, STATE),
            compiler_params=params(),
            cost_estimate=cost(4 << 20),
        )(mine, other, x_first, b_first, s_add, s_scale, e_scale)

    with jax.named_scope("sum"):
        came = []
        for l_send, _, _, r_send, _, _ in pieces:
            came.append((over_tensor(l_send, 1), over_tensor(r_send, 2)))
        passed = []
        for (l_came, r_came), (_, l_own, l_on, _, r_own, r_on) in zip(came, pieces):
            onward = (l_on.astype(f32) + l_came[1].astype(f32)).astype(bf16)
            l_last = over_tensor(onward, 2)
            onward = (r_on.astype(f32) + r_came[1].astype(f32)).astype(bf16)
            r_last = over_tensor(onward, 1)
            passed.append(l_own.astype(f32) + l_came[0].astype(f32) + l_last.astype(f32))
            passed.append(r_own.astype(f32) + r_came[0].astype(f32) + r_last.astype(f32))
        mixed = jnp.concatenate(passed, axis=1).astype(bf16)

    return (mixed, final_states.reshape(cached_states.shape))


def solution(mesh):
    placed = (
        P("replica", "tensor"),
        P("replica", "tensor"),
        P("replica", None),
        P("replica", "tensor"),
        P("tensor"),
        P("tensor"),
        P("tensor"),
        P(None, "tensor"),
        P(),
        P("tensor"),
        P("tensor", None),
        P("replica", "tensor", None, None),
        P("replica", None, "tensor"),
        P("replica", None, None),
        P(),
        P("replica"),
    )
    square = mesh.shape["replica"] == 2 * CHIPS and mesh.shape["tensor"] == GROUPS
    return jax.shard_map(
        local_square if square else local_any,
        mesh=mesh,
        in_specs=placed,
        out_specs=(P(("replica", "tensor"), None), P("replica", "tensor", None, None)),
        check_vma=False,
    )
```

```python
import math
from functools import partial

import jax
import jax.numpy as jnp
from jax import lax
from jax.experimental import pallas as pl
from jax.experimental.pallas import tpu as pltpu
from jax.sharding import PartitionSpec as P

HEADS = 128
HEAD_DIM = 32
STATE = 128
GROUPS = 4
CONV = 4


highest = lax.Precision.HIGHEST
epsilon = 1e-05
f32 = jnp.float32
bf16 = jnp.bfloat16
LOG2E = math.log2(math.e)
MIB = 1024 * 1024
VMEM_LIMIT = 24


def causal_conv(tail_rows, sequence, kernel):
    joined = jnp.concatenate([tail_rows, sequence], axis=0)
    length = sequence.shape[0]
    total = joined[0:length] * kernel[0][None, :]
    for offset in range(1, kernel.shape[0]):
        total = total + joined[offset : offset + length] * kernel[offset][None, :]
    return jax.nn.silu(total)


def span_scan(inputs, b_heads, c_heads, step_sizes, decay_rates, skip_gain, carry_state):
    logdec = -step_sizes * decay_rates[None, :]
    cumulative = jnp.cumsum(logdec, axis=0)
    count_rows = inputs.shape[0]
    causal = jnp.arange(count_rows)[:, None] >= jnp.arange(count_rows)[None, :]
    cum_heads = jnp.transpose(cumulative)
    differ = cum_heads[:, :, None] - cum_heads[:, None, :]
    decays = jnp.where(causal[None, :, :], jnp.exp(jnp.minimum(differ, 0.0)), 0.0)
    scores = jnp.einsum("ihn,jhn->hij", c_heads, b_heads, precision=highest)
    weights = scores * decays * jnp.transpose(step_sizes)[:, None, :]
    inside = jnp.einsum("hij,jhp->ihp", weights, inputs, precision=highest)
    carried = jnp.exp(cumulative)[:, :, None] * jnp.einsum(
        "ihn,hpn->ihp", c_heads, carry_state, precision=highest
    )
    output = inside + carried + skip_gain[None, :, None] * inputs
    ending = cumulative[-1]
    weigh_in = jnp.exp(ending[None, :] - cumulative) * step_sizes
    new_state = jnp.exp(ending)[:, None, None] * carry_state + jnp.einsum(
        "jh,jhp,jhn->hpn", weigh_in, inputs, b_heads, precision=highest
    )
    return (output, new_state)


def local_any(
    x_input,
    z_input,
    bc_input,
    dt_raw,
    dt_bias,
    decay_rates,
    skip_gain,
    conv_x,
    conv_bc,
    norm_gain,
    out_weight,
    cached_states,
    cached_tail_x,
    cached_tail_bc,
    prefix_block,
    lengths,
):
    requests = lengths.shape[0]
    local_heads = dt_raw.shape[1]
    tokens_dev = x_input.shape[0]
    slot_len = tokens_dev // requests
    wanted = lax.dynamic_slice_in_dim(prefix_block, lax.axis_index("replica") * requests, requests)

    def migrate(rows):
        rows = lax.all_gather(rows.astype(bf16), "replica", axis=0, tiled=True)
        return jnp.take(rows, wanted, axis=0).astype(f32)

    start_states = migrate(cached_states)
    start_tail_x = migrate(cached_tail_x)
    start_tail_bc = migrate(cached_tail_bc)
    head_ids = lax.axis_index("tensor") * local_heads + jnp.arange(local_heads)
    member = ((head_ids // (HEADS // GROUPS))[:, None] == jnp.arange(GROUPS)[None, :]).astype(f32)
    live = jnp.arange(slot_len)[None, :] < lengths[:, None]
    outputs = []
    finals = []
    for request in range(requests):
        row_lo = request * slot_len
        row_hi = row_lo + slot_len
        inputs = causal_conv(
            start_tail_x[request], x_input[row_lo:row_hi].astype(f32), conv_x
        ).reshape(slot_len, local_heads, HEAD_DIM)
        bc_conv = causal_conv(
            start_tail_bc[request], bc_input[row_lo:row_hi].astype(f32), conv_bc
        )
        b_groups = bc_conv[:, : GROUPS * STATE].reshape(slot_len, GROUPS, STATE)
        c_groups = bc_conv[:, GROUPS * STATE :].reshape(slot_len, GROUPS, STATE)
        b_heads = jnp.einsum("lgn,hg->lhn", b_groups, member, precision=highest)
        c_heads = jnp.einsum("lgn,hg->lhn", c_groups, member, precision=highest)
        step_sizes = jnp.where(
            live[request][:, None], jax.nn.softplus(dt_raw[row_lo:row_hi] + dt_bias[None, :]), 0.0
        )
        output, carry_state = span_scan(
            inputs, b_heads, c_heads, step_sizes, decay_rates, skip_gain, start_states[request]
        )
        outputs.append(output.reshape(slot_len, -1))
        finals.append(carry_state)
    outputs = jnp.concatenate(outputs, axis=0)
    final_states = jnp.stack(finals, axis=0)
    gate_vals = outputs * jax.nn.silu(z_input.astype(f32))
    by_head = gate_vals.reshape(tokens_dev, local_heads, HEAD_DIM)
    head_squares = jnp.sum(by_head * by_head, axis=2)
    partial_sq = jnp.dot(head_squares, member, precision=highest)
    totals = lax.psum(partial_sq, "tensor")
    mean_sq = jnp.dot(totals, jnp.transpose(member), precision=highest) / (
        HEADS * HEAD_DIM // GROUPS
    )
    normed = (by_head * lax.rsqrt(mean_sq + epsilon)[:, :, None]).reshape(
        tokens_dev, -1
    ) * norm_gain[None, :]
    gated = jnp.where(live.reshape(tokens_dev, 1), normed, 0.0).astype(bf16)
    mixed = lax.psum_scatter(
        jnp.dot(gated, out_weight, preferred_element_type=f32).astype(bf16),
        "tensor",
        scatter_dimension=0,
        tiled=True,
    )
    return (mixed, final_states)


CHIPS = 4
SLOTS = 2
ITEMS = 2 * SLOTS
ROWS = 1024
HALF = ROWS // 2
TAIL = 32
ITEM_ROWS = HALF + TAIL // 2
LANES = 128
COLUMN_BLOCKS = ROWS // LANES
WIDE = ROWS + 2 * STATE
EARLY = CONV - 1
BASE = (3, 2, 2)
EXTRAS = ((0, 0, 0), (0, 1, 0), (0, 0, 1), (1, 2, 2))
SEND_PLAN = 0
PLACE_PLAN = 3 * ITEMS
CHUNKS = ((0, 4), (4, 8))
TILE = 512

HBM = pl.BlockSpec(memory_space=pltpu.HBM)
ANYWHERE = pl.BlockSpec(memory_space=pl.ANY)
VMEM = pl.BlockSpec(memory_space=pltpu.VMEM)
SMEM = pl.BlockSpec(memory_space=pltpu.SMEM)


def sds(shape, dtype):
    return jax.ShapeDtypeStruct(shape, dtype)


def params():
    return pltpu.CompilerParams(vmem_limit_bytes=VMEM_LIMIT * MIB)


def in_hbm(value):
    return pltpu.with_memory_space_constraint(value, pltpu.HBM)


def cost(nbytes, flops=0):
    return pl.CostEstimate(flops=flops, bytes_accessed=nbytes, transcendentals=0)


def silu(value):
    half = 0.5 * value
    return half + half * jnp.tanh(half)


def chip_and_core():
    replica = lax.axis_index("replica")
    return replica // 2, lax.rem(replica, 2)


def half_at(core):
    return pl.ds(pl.multiple_of(core * HALF, HALF), HALF)


def tail_half(core):
    return pl.ds(pl.multiple_of(core * (TAIL // 2), TAIL // 2), TAIL // 2)


def pack_kernel(
    states,
    tail_x,
    tail_bc,
    send,
    keep,
    blocks,
    rows_x,
    rows_bc,
    scratch,
    sems,
):
    _, core = chip_and_core()
    group = lax.axis_index("tensor")
    copies = [
        pltpu.make_async_copy(states.at[:, half_at(1 - core)], blocks.at[0], sems.at[0]),
        pltpu.make_async_copy(tail_x, rows_x, sems.at[1]),
        pltpu.make_async_copy(tail_bc, rows_bc, sems.at[2]),
        pltpu.make_async_copy(states.at[:, half_at(core)], blocks.at[1], sems.at[3]),
    ]
    for copy in copies:
        copy.start()
    for copy in copies:
        copy.wait()
    scratch[...] = jnp.zeros_like(scratch)
    for block in range(SLOTS):
        for k in range(CONV - 1):
            for s in range(COLUMN_BLOCKS):
                scratch[3 * s + k : 3 * s + k + 1, :] = rows_x[
                    k, block : block + 1, s * LANES : (s + 1) * LANES
                ]
            for s in range(2):
                at = pl.multiple_of((s * GROUPS + group) * STATE, STATE)
                row = 3 * (COLUMN_BLOCKS + s) + k
                scratch[row : row + 1, :] = rows_bc[k, block : block + 1, pl.ds(at, STATE)]
        for part, out in enumerate((send, keep)):
            half = jnp.bitwise_xor(core, 1 - part)
            out[block, :HALF, :] = blocks[part, block].astype(bf16)
            out[block, HALF:, :] = scratch[tail_half(half), :].astype(bf16)


def plan_kernel(prefix, plan, variant):
    chip, core = chip_and_core()
    need = [jnp.int32(0)] * CHIPS
    for entry in range(PLACE_PLAN):
        plan[SEND_PLAN + entry] = 0
    for target in range(CHIPS):
        blocks = [prefix[target * ITEMS + place] for place in range(ITEMS)]
        sources = [block // ITEMS for block in blocks]
        for place in range(ITEMS):
            source = sources[place]
            item = lax.rem(blocks[place], ITEMS)
            rank = jnp.int32(0)
            for other in range(place):
                rank += jnp.where(sources[other] == source, 1, 0)
            distance = jnp.bitwise_xor(source, target)
            for d in range(1, CHIPS):
                need[d] = jnp.where(distance == d, jnp.maximum(need[d], rank + 1), need[d])

            @pl.when((source == chip) & (distance > 0))
            def _():
                plan[SEND_PLAN + (distance - 1) * ITEMS + rank] = item

            @pl.when(target == chip)
            def _():
                owner = jnp.bitwise_xor(core, place // SLOTS)
                at = PLACE_PLAN + owner * SLOTS + place % SLOTS
                plan[at] = distance * ITEMS + jnp.where(distance == 0, item, rank)

    choice = jnp.int32(len(EXTRAS) - 1)
    for v in reversed(range(len(EXTRAS) - 1)):
        fits = need[1] <= BASE[0] + EXTRAS[v][0]
        for d in range(2, CHIPS):
            fits = fits & (need[d] <= BASE[d - 1] + EXTRAS[v][d - 1])
        choice = jnp.where(fits, v, choice)
    variant[0] = choice


def copy_item(out, at, keep, recv, item, core):
    slot = lax.rem(item, SLOTS)
    mine = item // SLOTS == core

    @pl.when(mine)
    def _():
        out[at] = keep[slot]

    @pl.when(jnp.logical_not(mine))
    def _():
        out[at] = recv[slot]


def select_kernel(first, counts, plan, _, keep, recv, *outs):
    _, core = chip_and_core()
    outs = iter(outs)
    for d in range(1, CHIPS):
        if counts[d - 1]:
            out = next(outs)
            for slot in range(counts[d - 1]):
                item = plan[SEND_PLAN + (d - 1) * ITEMS + first[d - 1] + slot]
                copy_item(out, slot, keep, recv, item, core)


def spread_kernel(counts, *refs):
    outs = refs[-(CHIPS - 1) :]
    came = iter(refs)
    for n, out in zip(counts, outs):
        if n:
            out[:n] = next(came)[...]


def place_kernel(owner, plan, _, keep, recv, *refs):
    came, out = refs[: 2 * (CHIPS - 1)], refs[-1]
    _, core = chip_and_core()
    for slot in range(SLOTS):
        code = plan[PLACE_PLAN + owner * SLOTS + slot]
        d = code // ITEMS
        which = lax.rem(code, ITEMS)

        @pl.when(d == 0)
        def _():
            copy_item(out, slot, keep, recv, which, core)

        for e in range(1, CHIPS):
            few = BASE[e - 1]
            base, extra = came[e - 1], came[e + 2]

            @pl.when((d == e) & (which < few))
            def _():
                out[slot] = base[jnp.minimum(which, few - 1)]

            @pl.when((d == e) & (which >= few))
            def _():
                out[slot] = extra[jnp.maximum(which - few, 0)]


def scan_kernel(
    _,
    lengths,
    x_in,
    z_in,
    bc_in,
    dt_raw,
    dt_bias,
    decay,
    skip,
    conv_x,
    conv_bc,
    weight,
    y_in,
    y_scale,
    c_out,
    s_add,
    s_scale,
    e_scale,
    early,
    staged,
    u,
    sems,
):
    parts = sems.shape[0]
    deep = weight.shape[0] // parts
    copies = []
    for i in range(parts):
        at = slice(i * deep, (i + 1) * deep)
        copies.append(pltpu.make_async_copy(weight.at[at], staged.at[at], sems.at[i]))
        copies[-1].start()
    group = lax.axis_index("tensor")
    span = x_in.shape[0] // SLOTS
    heads = dt_raw.shape[0]
    row = lax.broadcasted_iota(jnp.int32, (span, span), 0)
    column = lax.broadcasted_iota(jnp.int32, (span, span), 1)
    causal = row >= column
    lower = causal.astype(f32)
    late = causal & (column >= EARLY)
    head_row = lax.broadcasted_iota(jnp.int32, (heads, ROWS), 0)
    head_column = lax.broadcasted_iota(jnp.int32, (heads, ROWS), 1) // HEAD_DIM
    expand = (head_row == head_column).astype(f32)
    skip_wide = jnp.dot(skip[...], expand, precision=highest, preferred_element_type=f32)
    same = lax.broadcasted_iota(jnp.int32, (heads, heads), 0) == lax.broadcasted_iota(
        jnp.int32, (heads, heads), 1
    )

    def upright(value):
        return jnp.sum(jnp.where(same, value, 0.0), axis=1, keepdims=True)

    bias = upright(dt_bias[...])
    rate = upright(decay[...]) * (-LOG2E)
    per_block = LANES // HEAD_DIM
    lane_head = lax.broadcasted_iota(jnp.int32, (span, LANES), 1) // HEAD_DIM
    token = lax.broadcasted_iota(jnp.int32, (heads, span), 1)
    over_last = (((1,), (1,)), ((), ()))
    over_first = (((0,), (0,)), ((), ()))
    u[0:8, :] = jnp.zeros((8, WIDE), f32)
    for r in range(SLOTS):
        rows = slice(r * span, (r + 1) * span)
        u[8 : 8 + span, :ROWS] = x_in[rows, :].astype(f32)
        for s in range(2):
            at = pl.multiple_of((s * GROUPS + group) * STATE, STATE)
            lo = ROWS + s * STATE
            u[8 : 8 + span, lo : lo + STATE] = bc_in[rows, pl.ds(at, STATE)].astype(f32)

        def conv(lo, taps):
            at = slice(lo, lo + LANES)
            total = u[5 : 5 + span, at] * taps(0)
            early[r, 1, 0:1, at] = taps(0)
            for k in range(1, CONV):
                total = total + u[5 + k : 5 + k + span, at] * taps(k)
                early[r, 1, k : k + 1, at] = taps(k)
            early[r, 0, :, at] = total[:8]
            return silu(total)

        def bc_conv(s):
            at = pl.multiple_of((s * GROUPS + group) * STATE, STATE)
            return conv(ROWS + s * STATE, lambda k: conv_bc[k : k + 1, pl.ds(at, STATE)])

        b_mat = bc_conv(0).astype(bf16)
        c_mat = bc_conv(1).astype(bf16)
        c_out[rows, :] = c_mat
        scores = lax.dot_general(c_mat, b_mat, over_last, preferred_element_type=f32)
        scores = jnp.where(late, scores, 0.0)

        raw = dt_raw[:, rows] + bias
        steps = jnp.maximum(raw, 0.0) + jnp.log1p(jnp.exp(-jnp.abs(raw)))
        steps = jnp.where(token < lengths[r], steps, 0.0)
        logdec = steps * rate
        cum = lax.dot_general(
            lower, logdec, over_last, precision=highest, preferred_element_type=f32
        )
        cum_t = lax.dot_general(
            logdec, lower, over_last, precision=highest, preferred_element_type=f32
        )
        begin = cum_t[:, EARLY - 1 : EARLY]
        ending = cum_t[:, span - 1 : span]
        s_scale[r] = jnp.broadcast_to(jnp.exp2(ending - begin), (heads, LANES))
        e_scale[r] = jnp.broadcast_to(jnp.exp2(begin), (heads, LANES))
        weigh = jnp.where(token >= EARLY, jnp.exp2(ending - cum_t) * steps, 0.0)
        since = jnp.exp2(jnp.minimum(cum_t - begin, 0.0))
        wide = lax.dot_general(
            jnp.concatenate([steps, weigh, since, cum_t], axis=1),
            expand,
            over_first,
            precision=highest,
            preferred_element_type=f32,
        )
        early[r, 2, :, :ROWS] = wide[:8]
        early[r, 3, :, :ROWS] = wide[3 * span : 3 * span + 8]
        early[r, 5, :, :ROWS] = jnp.broadcast_to(skip_wide, (8, ROWS))
        for q in range(COLUMN_BLOCKS):
            lo = q * LANES
            cols = slice(lo, lo + LANES)
            xc = conv(lo, lambda k: conv_x[k : k + 1, cols])
            xdt = (xc * wide[:span, cols]).astype(bf16)
            xw = (xc * wide[span : 2 * span, cols]).astype(bf16)
            s_add[r, lo : lo + LANES, :] = lax.dot_general(
                xw, b_mat, over_first, preferred_element_type=f32
            )
            total = skip_wide[:, cols] * xc
            parts = []
            masked = []
            for i in range(per_block):
                h = q * per_block + i
                differ = cum[:, h : h + 1] - cum_t[h : h + 1, :]
                parts.append((jnp.exp2(jnp.minimum(differ, 0.0)) * scores).astype(bf16))
                masked.append(jnp.where(lane_head == i, xdt, jnp.zeros_like(xdt)))
            total = total + jnp.dot(
                jnp.concatenate(parts, axis=1),
                jnp.concatenate(masked, axis=0),
                preferred_element_type=f32,
            )
            gate = silu(z_in[rows, cols].astype(f32))
            early[r, 4, :, cols] = gate[:8]
            y_in[rows, cols] = total * gate
            y_scale[rows, cols] = wide[2 * span : 3 * span, cols] * gate
    for copy in copies:
        copy.wait()


def by_head(state, scale):
    heads = scale.shape[0]
    wide = state.astype(f32).reshape(heads, HEAD_DIM, LANES) * scale[:, None, :]
    return wide.reshape(heads * HEAD_DIM, LANES)


def first_tokens(early, tail):
    row = lax.broadcasted_iota(jnp.int32, (8, WIDE), 0)
    taps = early[1]
    total = early[0]
    for t in range(EARLY):
        add = sum(taps[k : k + 1] * tail[t + k : t + k + 1] for k in range(EARLY - t))
        total = jnp.where(row == t, total + add, total)
    act = silu(total)
    return act[:, :ROWS], act[:, ROWS : ROWS + STATE], act[:, ROWS + STATE :]


def gate_rows(
    lengths,
    y_in,
    y_scale,
    c_in,
    e_scale,
    early,
    mine,
    other,
    gain,
    gated,
    x_first,
    b_first,
    start,
    tails,
    tail_rows,
):
    _, core = chip_and_core()
    tensor = lax.axis_index("tensor")
    x, y = lax.rem(tensor, 2), tensor // 2
    tokens = y_in.shape[0]
    span = tokens // SLOTS
    quarter = tokens // 4
    over_last = (((1,), (1,)), ((), ()))
    over_first = (((0,), (0,)), ((), ()))
    row = lax.broadcasted_iota(jnp.int32, (8, ROWS), 0)
    tail_rows[...] = jnp.zeros_like(tail_rows)
    for r in range(SLOTS):
        rows = slice(r * span, (r + 1) * span)
        start[r, half_at(core), :] = mine[r, :HALF]
        start[r, half_at(1 - core), :] = other[r, :HALF]
        tails[r, tail_half(core), :] = mine[r, HALF:].astype(f32)
        tails[r, tail_half(1 - core), :] = other[r, HALF:].astype(f32)
        for s in range(COLUMN_BLOCKS + 2):
            tail_rows[r, :EARLY, s * LANES : (s + 1) * LANES] = tails[r, 3 * s : 3 * s + 3, :]

        x_8, b_8, c_8 = first_tokens(early[r], tail_rows[r])
        steps, cum, gate_8 = early[r, 2, :, :ROWS], early[r, 3, :, :ROWS], early[r, 4, :, :ROWS]
        skip = early[r, 5, 0:1, :ROWS]
        moved = steps * x_8
        last = cum[EARLY - 1 : EARLY]
        kept = jnp.where(row < EARLY, jnp.exp2(jnp.minimum(last - cum, 0.0)) * moved, 0.0)
        x_first[r] = kept
        b_first[r] = b_8
        after = by_head(start[r], e_scale[r]) + lax.dot_general(
            kept, b_8, over_first, preferred_element_type=f32
        )
        y_8 = skip * x_8 + jnp.exp2(cum) * lax.dot_general(
            c_8.astype(bf16), start[r], over_last, preferred_element_type=f32
        )
        scores = lax.dot_general(c_8, b_8, over_last, preferred_element_type=f32)
        for j in range(EARLY):
            decay = jnp.exp2(jnp.minimum(cum - cum[j : j + 1], 0.0))
            y_8 += jnp.where(row >= j, scores[:, j : j + 1] * decay * moved[j : j + 1], 0.0)

        carried = lax.dot_general(
            c_in[rows, :], after.astype(bf16), over_last, preferred_element_type=f32
        )
        value = y_in[rows, :] + y_scale[rows, :] * carried
        value = jnp.concatenate([jnp.where(row < EARLY, y_8 * gate_8, value[:8]), value[8:]], axis=0)
        mean_sq = jnp.mean(value * value, axis=1, keepdims=True)
        live = lax.broadcasted_iota(jnp.int32, (span, 1), 0) < lengths[r]
        scale = jnp.where(live, lax.rsqrt(mean_sq + epsilon), 0.0)
        result = (value * scale * gain[...]).astype(bf16)
        for part in range(span // quarter):
            owner = r * (span // quarter) + part
            place = jnp.bitwise_xor(owner // 2, y) + 2 * jnp.bitwise_xor(owner % 2, x)
            at = pl.ds(pl.multiple_of(place * quarter, quarter), quarter)
            gated[at, :] = result[part * quarter : (part + 1) * quarter, :]


def project_kernel(first, columns, *refs):
    if first:
        *ins, weight, gated, x_first, b_first = refs[:13]
        l_send, l_own, l_on, r_send, r_own, r_on, *scratch = refs[13:]
        gate_rows(*ins, gated, x_first, b_first, *scratch)
    else:
        gated, weight, l_send, l_own, l_on, r_send, r_own, r_on = refs
    q = gated.shape[0] // 4
    half = l_own.shape[1]
    tile = min(half, TILE)
    for lo in range(0, 2 * half, tile):
        at = slice(columns + lo, columns + lo + tile)
        product = jnp.dot(gated[...], weight[:, at], preferred_element_type=f32).astype(bf16)
        own, block_y, block_x, block_xy = (product[j * q : (j + 1) * q] for j in range(4))
        if lo < half:
            to = slice(lo, lo + tile)
            l_send[0, :, to] = block_x
            l_send[1, :, to] = block_xy
            l_own[:, to] = own
            l_on[:, to] = block_y
        else:
            to = slice(lo - half, lo - half + tile)
            r_send[0, :, to] = block_y
            r_send[1, :, to] = block_xy
            r_own[:, to] = own
            r_on[:, to] = block_x


def final_kernel(mine, other, x_first, b_first, s_add, s_scale, e_scale, out):
    _, core = chip_and_core()
    heads = s_scale.shape[1] // 2

    def put(half, piece):
        at = half_at(half)
        of = pl.ds(pl.multiple_of(half * heads, heads), heads)
        after = by_head(piece[0, :HALF], e_scale[0, of, :]) + lax.dot_general(
            x_first[0, :, at], b_first[0], (((0,), (0,)), ((), ())), preferred_element_type=f32
        )
        out[0, at, :] = by_head(after, s_scale[0, of, :]) + s_add[0, at, :]

    put(core, mine)
    put(1 - core, other)


def over_replica(value, bits):
    pairs = [(r, r ^ bits) for r in range(2 * CHIPS)]
    return lax.ppermute(value, "replica", pairs)


def over_tensor(value, bits):
    return lax.ppermute(value, "tensor", [(t, t ^ bits) for t in range(4)])


def select(first, counts, plan, after, keep, recv):
    with jax.named_scope("select"):
        return pl.pallas_call(
            partial(select_kernel, first, counts),
            out_shape=[sds((n, ITEM_ROWS, LANES), bf16) for n in counts if n],
            in_specs=[SMEM, ANYWHERE, VMEM, VMEM],
            out_specs=[VMEM for n in counts if n],
            compiler_params=params(),
        )(plan, after, keep, recv)


def exchange(counts, sends):
    bits = [2 * d for d in range(1, CHIPS) if counts[d - 1]]
    return [over_replica(value, b) for value, b in zip(sends, bits)]


def migrate_more(counts, plan, keep, recv):
    came = exchange(counts, select(BASE, counts, plan, keep, keep, recv)) if any(counts) else []
    return pl.pallas_call(
        partial(spread_kernel, counts),
        out_shape=tuple(sds((n, ITEM_ROWS, LANES), bf16) for n in EXTRAS[-1]),
        in_specs=[VMEM] * len(came),
        out_specs=(VMEM,) * (CHIPS - 1),
        compiler_params=params(),
    )(*came)


def local_square(
    x_input,
    z_input,
    bc_input,
    dt_raw,
    dt_bias,
    decay_rates,
    skip_gain,
    conv_x,
    conv_bc,
    norm_gain,
    out_weight,
    cached_states,
    cached_tail_x,
    cached_tail_bc,
    prefix_block,
    lengths,
):
    tokens = x_input.shape[0]
    heads = dt_raw.shape[1]
    features = out_weight.shape[1]
    span = tokens // SLOTS

    with jax.named_scope("pack"):
        send, keep = pl.pallas_call(
            pack_kernel,
            out_shape=(sds((SLOTS, ITEM_ROWS, LANES), bf16),) * 2,
            in_specs=[HBM] * 3,
            out_specs=(VMEM, VMEM),
            scratch_shapes=[
                pltpu.VMEM((2, SLOTS, HALF, LANES), f32),
                pltpu.VMEM((CONV - 1, SLOTS) + cached_tail_x.shape[2:], f32),
                pltpu.VMEM((CONV - 1, SLOTS) + cached_tail_bc.shape[2:], f32),
                pltpu.VMEM((TAIL, LANES), f32),
                pltpu.SemaphoreType.DMA((4,)),
            ],
            compiler_params=params(),
        )(
            in_hbm(cached_states.reshape(SLOTS, ROWS, LANES)),
            in_hbm(jnp.transpose(cached_tail_x, (1, 0, 2))),
            in_hbm(jnp.transpose(cached_tail_bc, (1, 0, 2))),
        )
    recv = over_replica(send, 1)
    with jax.named_scope("plan"):
        plan, variant = pl.pallas_call(
            plan_kernel,
            out_shape=(sds((PLACE_PLAN + ITEMS,), jnp.int32), sds((1,), jnp.int32)),
            in_specs=[SMEM],
            out_specs=(SMEM, SMEM),
            compiler_params=params(),
        )(in_hbm(prefix_block))

    more = lax.switch(
        variant.reshape(()),
        [partial(migrate_more, counts) for counts in EXTRAS],
        plan,
        keep,
        recv,
    )
    sends = select((0,) * (CHIPS - 1), BASE, plan, more[0], keep, recv)
    came = exchange(BASE, sends)

    with jax.named_scope("scan"):
        scale = sds((SLOTS, heads, LANES), f32)
        y_in, y_scale, c_mat, s_add, s_scale, e_scale, early, weight = pl.pallas_call(
            scan_kernel,
            out_shape=(
                sds((tokens, ROWS), f32),
                sds((tokens, ROWS), f32),
                sds((tokens, STATE), bf16),
                sds((SLOTS, ROWS, STATE), f32),
                scale,
                scale,
                sds((SLOTS, 6, 8, WIDE), f32),
                pltpu.VMEM(out_weight.shape, bf16),
            ),
            in_specs=[ANYWHERE, SMEM] + [VMEM] * 9 + [HBM],
            out_specs=(VMEM,) * 8,
            scratch_shapes=[pltpu.VMEM((8 + span, WIDE), f32), pltpu.SemaphoreType.DMA((4,))],
            compiler_params=params(),
            cost_estimate=cost(8 << 20, 1 << 30),
        )(
            sends[0],
            lengths,
            x_input,
            z_input,
            bc_input,
            jnp.transpose(dt_raw),
            dt_bias.reshape(1, heads),
            decay_rates.reshape(1, heads),
            skip_gain.reshape(1, heads),
            conv_x,
            conv_bc,
            in_hbm(out_weight),
        )

    def place(owner, after):
        with jax.named_scope("place"):
            return pl.pallas_call(
                partial(place_kernel, owner),
                out_shape=sds((SLOTS, ITEM_ROWS, LANES), bf16),
                in_specs=[SMEM, ANYWHERE] + [VMEM] * 8,
                out_specs=VMEM,
                compiler_params=params(),
            )(plan, after, keep, recv, *came, *more)

    theirs = place(1, c_mat)
    other = over_replica(theirs, 1)
    mine = place(0, theirs)

    quarter = tokens // 4
    pieces = []
    gated = None
    for lo, hi in CHUNKS:
        lo, hi = lo * features // 8, hi * features // 8
        half = (hi - lo) // 2
        outs = [sds((2, quarter, half), bf16), sds((quarter, half), bf16), sds((quarter, half), bf16)]
        call = partial(
            pl.pallas_call,
            partial(project_kernel, gated is None, lo),
            compiler_params=params(),
            cost_estimate=cost(ROWS * (hi - lo) * 2, 2 * tokens * ROWS * (hi - lo)),
        )
        with jax.named_scope("project"):
            if gated is None:
                gated, x_first, b_first, *parts = call(
                    out_shape=[
                        sds((tokens, ROWS), bf16),
                        sds((SLOTS, 8, ROWS), f32),
                        sds((SLOTS, 8, STATE), f32),
                    ]
                    + 2 * outs,
                    in_specs=[SMEM] + [VMEM] * 9,
                    out_specs=[VMEM] * 9,
                    scratch_shapes=[
                        pltpu.VMEM((SLOTS, ROWS, LANES), bf16),
                        pltpu.VMEM((SLOTS, TAIL, LANES), f32),
                        pltpu.VMEM((SLOTS, 8, WIDE), f32),
                    ],
                )(
                    lengths,
                    y_in,
                    y_scale,
                    c_mat,
                    e_scale,
                    early,
                    mine,
                    other,
                    norm_gain.reshape(1, ROWS),
                    weight,
                )
            else:
                parts = call(
                    out_shape=2 * outs,
                    in_specs=[VMEM, VMEM],
                    out_specs=[VMEM] * 6,
                )(gated, weight)
        pieces.append(parts)

    with jax.named_scope("final_states"):

        def of_request(*shape):
            return pl.BlockSpec((1,) + shape, lambda n: (n,) + (0,) * len(shape))

        final_states = pl.pallas_call(
            final_kernel,
            grid=(SLOTS,),
            out_shape=sds((SLOTS, ROWS, STATE), f32),
            in_specs=[
                of_request(ITEM_ROWS, LANES),
                of_request(ITEM_ROWS, LANES),
                of_request(8, ROWS),
                of_request(8, STATE),
                of_request(ROWS, STATE),
                of_request(heads, LANES),
                of_request(heads, LANES),
            ],
            out_specs=of_request(ROWS, STATE),
            compiler_params=params(),
            cost_estimate=cost(4 << 20),
        )(mine, other, x_first, b_first, s_add, s_scale, e_scale)

    with jax.named_scope("sum"):
        came = []
        for l_send, _, _, r_send, _, _ in pieces:
            came.append((over_tensor(l_send, 1), over_tensor(r_send, 2)))
        passed = []
        for (l_came, r_came), (_, l_own, l_on, _, r_own, r_on) in zip(came, pieces):
            onward = (l_on.astype(f32) + l_came[1].astype(f32)).astype(bf16)
            l_last = over_tensor(onward, 2)
            onward = (r_on.astype(f32) + r_came[1].astype(f32)).astype(bf16)
            r_last = over_tensor(onward, 1)
            passed.append(l_own.astype(f32) + l_came[0].astype(f32) + l_last.astype(f32))
            passed.append(r_own.astype(f32) + r_came[0].astype(f32) + r_last.astype(f32))
        mixed = jnp.concatenate(passed, axis=1).astype(bf16)

    return (mixed, final_states.reshape(cached_states.shape))


def solution(mesh):
    placed = (
        P("replica", "tensor"),
        P("replica", "tensor"),
        P("replica", None),
        P("replica", "tensor"),
        P("tensor"),
        P("tensor"),
        P("tensor"),
        P(None, "tensor"),
        P(),
        P("tensor"),
        P("tensor", None),
        P("replica", "tensor", None, None),
        P("replica", None, "tensor"),
        P("replica", None, None),
        P(),
        P("replica"),
    )
    square = mesh.shape["replica"] == 2 * CHIPS and mesh.shape["tensor"] == GROUPS
    return jax.shard_map(
        local_square if square else local_any,
        mesh=mesh,
        in_specs=placed,
        out_specs=(P(("replica", "tensor"), None), P("replica", "tensor", None, None)),
        check_vma=False,
    )
```

```python
import math
from functools import partial

import jax
import jax.numpy as jnp
from jax import lax
from jax.experimental import pallas as pl
from jax.experimental.pallas import tpu as pltpu
from jax.sharding import PartitionSpec as P

HEADS = 128
HEAD_DIM = 32
STATE = 128
GROUPS = 4
CONV = 4


highest = lax.Precision.HIGHEST
epsilon = 1e-05
f32 = jnp.float32
bf16 = jnp.bfloat16
LOG2E = math.log2(math.e)
MIB = 1024 * 1024
VMEM_LIMIT = 24


def causal_conv(tail_rows, sequence, kernel):
    joined = jnp.concatenate([tail_rows, sequence], axis=0)
    length = sequence.shape[0]
    total = joined[0:length] * kernel[0][None, :]
    for offset in range(1, kernel.shape[0]):
        total = total + joined[offset : offset + length] * kernel[offset][None, :]
    return jax.nn.silu(total)


def span_scan(inputs, b_heads, c_heads, step_sizes, decay_rates, skip_gain, carry_state):
    logdec = -step_sizes * decay_rates[None, :]
    cumulative = jnp.cumsum(logdec, axis=0)
    count_rows = inputs.shape[0]
    causal = jnp.arange(count_rows)[:, None] >= jnp.arange(count_rows)[None, :]
    cum_heads = jnp.transpose(cumulative)
    differ = cum_heads[:, :, None] - cum_heads[:, None, :]
    decays = jnp.where(causal[None, :, :], jnp.exp(jnp.minimum(differ, 0.0)), 0.0)
    scores = jnp.einsum("ihn,jhn->hij", c_heads, b_heads, precision=highest)
    weights = scores * decays * jnp.transpose(step_sizes)[:, None, :]
    inside = jnp.einsum("hij,jhp->ihp", weights, inputs, precision=highest)
    carried = jnp.exp(cumulative)[:, :, None] * jnp.einsum(
        "ihn,hpn->ihp", c_heads, carry_state, precision=highest
    )
    output = inside + carried + skip_gain[None, :, None] * inputs
    ending = cumulative[-1]
    weigh_in = jnp.exp(ending[None, :] - cumulative) * step_sizes
    new_state = jnp.exp(ending)[:, None, None] * carry_state + jnp.einsum(
        "jh,jhp,jhn->hpn", weigh_in, inputs, b_heads, precision=highest
    )
    return (output, new_state)


def local_any(
    x_input,
    z_input,
    bc_input,
    dt_raw,
    dt_bias,
    decay_rates,
    skip_gain,
    conv_x,
    conv_bc,
    norm_gain,
    out_weight,
    cached_states,
    cached_tail_x,
    cached_tail_bc,
    prefix_block,
    lengths,
):
    requests = lengths.shape[0]
    local_heads = dt_raw.shape[1]
    tokens_dev = x_input.shape[0]
    slot_len = tokens_dev // requests
    wanted = lax.dynamic_slice_in_dim(prefix_block, lax.axis_index("replica") * requests, requests)

    def migrate(rows):
        rows = lax.all_gather(rows.astype(bf16), "replica", axis=0, tiled=True)
        return jnp.take(rows, wanted, axis=0).astype(f32)

    start_states = migrate(cached_states)
    start_tail_x = migrate(cached_tail_x)
    start_tail_bc = migrate(cached_tail_bc)
    head_ids = lax.axis_index("tensor") * local_heads + jnp.arange(local_heads)
    member = ((head_ids // (HEADS // GROUPS))[:, None] == jnp.arange(GROUPS)[None, :]).astype(f32)
    live = jnp.arange(slot_len)[None, :] < lengths[:, None]
    outputs = []
    finals = []
    for request in range(requests):
        row_lo = request * slot_len
        row_hi = row_lo + slot_len
        inputs = causal_conv(
            start_tail_x[request], x_input[row_lo:row_hi].astype(f32), conv_x
        ).reshape(slot_len, local_heads, HEAD_DIM)
        bc_conv = causal_conv(
            start_tail_bc[request], bc_input[row_lo:row_hi].astype(f32), conv_bc
        )
        b_groups = bc_conv[:, : GROUPS * STATE].reshape(slot_len, GROUPS, STATE)
        c_groups = bc_conv[:, GROUPS * STATE :].reshape(slot_len, GROUPS, STATE)
        b_heads = jnp.einsum("lgn,hg->lhn", b_groups, member, precision=highest)
        c_heads = jnp.einsum("lgn,hg->lhn", c_groups, member, precision=highest)
        step_sizes = jnp.where(
            live[request][:, None], jax.nn.softplus(dt_raw[row_lo:row_hi] + dt_bias[None, :]), 0.0
        )
        output, carry_state = span_scan(
            inputs, b_heads, c_heads, step_sizes, decay_rates, skip_gain, start_states[request]
        )
        outputs.append(output.reshape(slot_len, -1))
        finals.append(carry_state)
    outputs = jnp.concatenate(outputs, axis=0)
    final_states = jnp.stack(finals, axis=0)
    gate_vals = outputs * jax.nn.silu(z_input.astype(f32))
    by_head = gate_vals.reshape(tokens_dev, local_heads, HEAD_DIM)
    head_squares = jnp.sum(by_head * by_head, axis=2)
    partial_sq = jnp.dot(head_squares, member, precision=highest)
    totals = lax.psum(partial_sq, "tensor")
    mean_sq = jnp.dot(totals, jnp.transpose(member), precision=highest) / (
        HEADS * HEAD_DIM // GROUPS
    )
    normed = (by_head * lax.rsqrt(mean_sq + epsilon)[:, :, None]).reshape(
        tokens_dev, -1
    ) * norm_gain[None, :]
    gated = jnp.where(live.reshape(tokens_dev, 1), normed, 0.0).astype(bf16)
    mixed = lax.psum_scatter(
        jnp.dot(gated, out_weight, preferred_element_type=f32).astype(bf16),
        "tensor",
        scatter_dimension=0,
        tiled=True,
    )
    return (mixed, final_states)


CHIPS = 4
SLOTS = 2
ITEMS = 2 * SLOTS
ROWS = 1024
HALF = ROWS // 2
TAIL = 32
ITEM_ROWS = HALF + TAIL // 2
LANES = 128
COLUMN_BLOCKS = ROWS // LANES
WIDE = ROWS + 2 * STATE
EARLY = CONV - 1
BASE = (3, 2, 2)
EXTRAS = ((0, 0, 0), (0, 1, 0), (0, 0, 1), (1, 2, 2))
SEND_PLAN = 0
PLACE_PLAN = 3 * ITEMS
CHUNKS = ((0, 4), (4, 8))
TILE = 512

HBM = pl.BlockSpec(memory_space=pltpu.HBM)
ANYWHERE = pl.BlockSpec(memory_space=pl.ANY)
VMEM = pl.BlockSpec(memory_space=pltpu.VMEM)
SMEM = pl.BlockSpec(memory_space=pltpu.SMEM)


def sds(shape, dtype):
    return jax.ShapeDtypeStruct(shape, dtype)


def params():
    return pltpu.CompilerParams(vmem_limit_bytes=VMEM_LIMIT * MIB)


def in_hbm(value):
    return pltpu.with_memory_space_constraint(value, pltpu.HBM)


def cost(nbytes, flops=0):
    return pl.CostEstimate(flops=flops, bytes_accessed=nbytes, transcendentals=0)


def silu(value):
    half = 0.5 * value
    return half + half * jnp.tanh(half)


def chip_and_core():
    replica = lax.axis_index("replica")
    return replica // 2, lax.rem(replica, 2)


def half_at(core):
    return pl.ds(pl.multiple_of(core * HALF, HALF), HALF)


def tail_half(core):
    return pl.ds(pl.multiple_of(core * (TAIL // 2), TAIL // 2), TAIL // 2)


def pack_kernel(
    states,
    tail_x,
    tail_bc,
    send,
    keep,
    blocks,
    rows_x,
    rows_bc,
    scratch,
    sems,
):
    _, core = chip_and_core()
    group = lax.axis_index("tensor")
    copies = [
        pltpu.make_async_copy(states.at[:, half_at(1 - core)], blocks.at[0], sems.at[0]),
        pltpu.make_async_copy(tail_x, rows_x, sems.at[1]),
        pltpu.make_async_copy(tail_bc, rows_bc, sems.at[2]),
        pltpu.make_async_copy(states.at[:, half_at(core)], blocks.at[1], sems.at[3]),
    ]
    for copy in copies:
        copy.start()
    for copy in copies:
        copy.wait()
    scratch[...] = jnp.zeros_like(scratch)
    for block in range(SLOTS):
        for k in range(CONV - 1):
            for s in range(COLUMN_BLOCKS):
                scratch[3 * s + k : 3 * s + k + 1, :] = rows_x[
                    k, block : block + 1, s * LANES : (s + 1) * LANES
                ]
            for s in range(2):
                at = pl.multiple_of((s * GROUPS + group) * STATE, STATE)
                row = 3 * (COLUMN_BLOCKS + s) + k
                scratch[row : row + 1, :] = rows_bc[k, block : block + 1, pl.ds(at, STATE)]
        for part, out in enumerate((send, keep)):
            half = jnp.bitwise_xor(core, 1 - part)
            out[block, :HALF, :] = blocks[part, block].astype(bf16)
            out[block, HALF:, :] = scratch[tail_half(half), :].astype(bf16)


def plan_kernel(prefix, plan, variant):
    chip, core = chip_and_core()
    need = [jnp.int32(0)] * CHIPS
    for entry in range(PLACE_PLAN):
        plan[SEND_PLAN + entry] = 0
    for target in range(CHIPS):
        blocks = [prefix[target * ITEMS + place] for place in range(ITEMS)]
        sources = [block // ITEMS for block in blocks]
        for place in range(ITEMS):
            source = sources[place]
            item = lax.rem(blocks[place], ITEMS)
            rank = jnp.int32(0)
            for other in range(place):
                rank += jnp.where(sources[other] == source, 1, 0)
            distance = jnp.bitwise_xor(source, target)
            for d in range(1, CHIPS):
                need[d] = jnp.where(distance == d, jnp.maximum(need[d], rank + 1), need[d])

            @pl.when((source == chip) & (distance > 0))
            def _():
                plan[SEND_PLAN + (distance - 1) * ITEMS + rank] = item

            @pl.when(target == chip)
            def _():
                owner = jnp.bitwise_xor(core, place // SLOTS)
                at = PLACE_PLAN + owner * SLOTS + place % SLOTS
                plan[at] = distance * ITEMS + jnp.where(distance == 0, item, rank)

    choice = jnp.int32(len(EXTRAS) - 1)
    for v in reversed(range(len(EXTRAS) - 1)):
        fits = need[1] <= BASE[0] + EXTRAS[v][0]
        for d in range(2, CHIPS):
            fits = fits & (need[d] <= BASE[d - 1] + EXTRAS[v][d - 1])
        choice = jnp.where(fits, v, choice)
    variant[0] = choice


def copy_item(out, at, keep, recv, item, core):
    slot = lax.rem(item, SLOTS)
    mine = item // SLOTS == core

    @pl.when(mine)
    def _():
        out[at] = keep[slot]

    @pl.when(jnp.logical_not(mine))
    def _():
        out[at] = recv[slot]


def select_kernel(first, counts, plan, _, keep, recv, *outs):
    _, core = chip_and_core()
    outs = iter(outs)
    for d in range(1, CHIPS):
        if counts[d - 1]:
            out = next(outs)
            for slot in range(counts[d - 1]):
                item = plan[SEND_PLAN + (d - 1) * ITEMS + first[d - 1] + slot]
                copy_item(out, slot, keep, recv, item, core)


def spread_kernel(counts, *refs):
    outs = refs[-(CHIPS - 1) :]
    came = iter(refs)
    for n, out in zip(counts, outs):
        if n:
            out[:n] = next(came)[...]


def place_kernel(owner, plan, _, keep, recv, *refs):
    came, out = refs[: 2 * (CHIPS - 1)], refs[-1]
    _, core = chip_and_core()
    for slot in range(SLOTS):
        code = plan[PLACE_PLAN + owner * SLOTS + slot]
        d = code // ITEMS
        which = lax.rem(code, ITEMS)

        @pl.when(d == 0)
        def _():
            copy_item(out, slot, keep, recv, which, core)

        for e in range(1, CHIPS):
            few = BASE[e - 1]
            base, extra = came[e - 1], came[e + 2]

            @pl.when((d == e) & (which < few))
            def _():
                out[slot] = base[jnp.minimum(which, few - 1)]

            @pl.when((d == e) & (which >= few))
            def _():
                out[slot] = extra[jnp.maximum(which - few, 0)]


def scan_kernel(
    _,
    lengths,
    x_in,
    z_in,
    bc_in,
    dt_raw,
    dt_bias,
    decay,
    skip,
    conv_x,
    conv_bc,
    weight,
    y_in,
    y_scale,
    c_out,
    s_add,
    s_scale,
    e_scale,
    early,
    staged,
    u,
    sems,
):
    parts = sems.shape[0]
    deep = weight.shape[0] // parts
    copies = []
    for i in range(parts):
        at = slice(i * deep, (i + 1) * deep)
        copies.append(pltpu.make_async_copy(weight.at[at], staged.at[at], sems.at[i]))
        copies[-1].start()
    group = lax.axis_index("tensor")
    span = x_in.shape[0] // SLOTS
    heads = dt_raw.shape[0]
    row = lax.broadcasted_iota(jnp.int32, (span, span), 0)
    column = lax.broadcasted_iota(jnp.int32, (span, span), 1)
    causal = row >= column
    lower = causal.astype(f32)
    late = causal & (column >= EARLY)
    head_row = lax.broadcasted_iota(jnp.int32, (heads, ROWS), 0)
    head_column = lax.broadcasted_iota(jnp.int32, (heads, ROWS), 1) // HEAD_DIM
    expand = (head_row == head_column).astype(f32)
    skip_wide = jnp.dot(skip[...], expand, precision=highest, preferred_element_type=f32)
    same = lax.broadcasted_iota(jnp.int32, (heads, heads), 0) == lax.broadcasted_iota(
        jnp.int32, (heads, heads), 1
    )

    def upright(value):
        return jnp.sum(jnp.where(same, value, 0.0), axis=1, keepdims=True)

    bias = upright(dt_bias[...])
    rate = upright(decay[...]) * (-LOG2E)
    per_block = LANES // HEAD_DIM
    lane_head = lax.broadcasted_iota(jnp.int32, (span, LANES), 1) // HEAD_DIM
    token = lax.broadcasted_iota(jnp.int32, (heads, span), 1)
    over_last = (((1,), (1,)), ((), ()))
    over_first = (((0,), (0,)), ((), ()))
    u[0:8, :] = jnp.zeros((8, WIDE), f32)
    for r in range(SLOTS):
        rows = slice(r * span, (r + 1) * span)
        u[8 : 8 + span, :ROWS] = x_in[rows, :].astype(f32)
        for s in range(2):
            at = pl.multiple_of((s * GROUPS + group) * STATE, STATE)
            lo = ROWS + s * STATE
            u[8 : 8 + span, lo : lo + STATE] = bc_in[rows, pl.ds(at, STATE)].astype(f32)

        def conv(lo, taps):
            at = slice(lo, lo + LANES)
            total = u[5 : 5 + span, at] * taps(0)
            early[r, 1, 0:1, at] = taps(0)
            for k in range(1, CONV):
                total = total + u[5 + k : 5 + k + span, at] * taps(k)
                early[r, 1, k : k + 1, at] = taps(k)
            early[r, 0, :, at] = total[:8]
            return silu(total)

        def bc_conv(s):
            at = pl.multiple_of((s * GROUPS + group) * STATE, STATE)
            return conv(ROWS + s * STATE, lambda k: conv_bc[k : k + 1, pl.ds(at, STATE)])

        b_mat = bc_conv(0).astype(bf16)
        c_mat = bc_conv(1).astype(bf16)
        c_out[rows, :] = c_mat
        scores = lax.dot_general(c_mat, b_mat, over_last, preferred_element_type=f32)
        scores = jnp.where(late, scores, 0.0)

        live = lax.broadcasted_iota(jnp.int32, (span, 1), 0) < lengths[r]
        raw = dt_raw[:, rows] + bias
        steps = jnp.maximum(raw, 0.0) + jnp.log1p(jnp.exp(-jnp.abs(raw)))
        steps = jnp.where(token < lengths[r], steps, 0.0)
        logdec = steps * rate
        cum = lax.dot_general(
            lower, logdec, over_last, precision=highest, preferred_element_type=f32
        )
        cum_t = lax.dot_general(
            logdec, lower, over_last, precision=highest, preferred_element_type=f32
        )
        begin = cum_t[:, EARLY - 1 : EARLY]
        ending = cum_t[:, span - 1 : span]
        s_scale[r] = jnp.broadcast_to(jnp.exp2(ending - begin), (heads, LANES))
        e_scale[r] = jnp.broadcast_to(jnp.exp2(begin), (heads, LANES))
        weigh = jnp.where(token >= EARLY, jnp.exp2(ending - cum_t) * steps, 0.0)
        since = jnp.exp2(jnp.minimum(cum_t - begin, 0.0))
        wide = lax.dot_general(
            jnp.concatenate([steps, weigh, since, cum_t], axis=1),
            expand,
            over_first,
            precision=highest,
            preferred_element_type=f32,
        )
        early[r, 2, :, :ROWS] = wide[:8]
        early[r, 3, :, :ROWS] = wide[3 * span : 3 * span + 8]
        early[r, 5, :, :ROWS] = jnp.broadcast_to(skip_wide, (8, ROWS))
        for q in range(COLUMN_BLOCKS):
            lo = q * LANES
            cols = slice(lo, lo + LANES)
            xc = conv(lo, lambda k: conv_x[k : k + 1, cols])
            xdt = (xc * wide[:span, cols]).astype(bf16)
            xw = (xc * wide[span : 2 * span, cols]).astype(bf16)
            s_add[r, lo : lo + LANES, :] = lax.dot_general(
                xw, b_mat, over_first, preferred_element_type=f32
            )
            total = skip_wide[:, cols] * xc
            parts = []
            masked = []
            for i in range(per_block):
                h = q * per_block + i
                differ = cum[:, h : h + 1] - cum_t[h : h + 1, :]
                parts.append((jnp.exp2(jnp.minimum(differ, 0.0)) * scores).astype(bf16))
                masked.append(jnp.where(lane_head == i, xdt, jnp.zeros_like(xdt)))
            total = total + jnp.dot(
                jnp.concatenate(parts, axis=1),
                jnp.concatenate(masked, axis=0),
                preferred_element_type=f32,
            )
            gate = jnp.where(live, silu(z_in[rows, cols].astype(f32)), 0.0)
            early[r, 4, :, cols] = gate[:8]
            y_in[rows, cols] = total * gate
            y_scale[rows, cols] = wide[2 * span : 3 * span, cols] * gate
    for copy in copies:
        copy.wait()


def by_head(state, scale):
    heads = scale.shape[0]
    wide = state.astype(f32).reshape(heads, HEAD_DIM, LANES) * scale[:, None, :]
    return wide.reshape(heads * HEAD_DIM, LANES)


def first_tokens(early, tail):
    row = lax.broadcasted_iota(jnp.int32, (8, WIDE), 0)
    taps = early[1]
    total = early[0]
    for t in range(EARLY):
        add = sum(taps[k : k + 1] * tail[t + k : t + k + 1] for k in range(EARLY - t))
        total = jnp.where(row == t, total + add, total)
    act = silu(total)
    return act[:, :ROWS], act[:, ROWS : ROWS + STATE], act[:, ROWS + STATE :]


def gate_rows(
    y_in,
    y_scale,
    c_in,
    early,
    mine,
    other,
    gain,
    gated,
    x_first,
    b_first,
    start,
    tails,
    tail_rows,
):
    _, core = chip_and_core()
    tensor = lax.axis_index("tensor")
    x, y = lax.rem(tensor, 2), tensor // 2
    tokens = y_in.shape[0]
    span = tokens // SLOTS
    quarter = tokens // 4
    over_last = (((1,), (1,)), ((), ()))
    row = lax.broadcasted_iota(jnp.int32, (8, ROWS), 0)
    row_16 = lax.broadcasted_iota(jnp.int32, (16, LANES), 0)
    tail_rows[...] = jnp.zeros_like(tail_rows)
    for r in range(SLOTS):
        rows = slice(r * span, (r + 1) * span)
        start[r, half_at(core), :] = mine[r, :HALF]
        start[r, half_at(1 - core), :] = other[r, :HALF]
        tails[r, tail_half(core), :] = mine[r, HALF:].astype(f32)
        tails[r, tail_half(1 - core), :] = other[r, HALF:].astype(f32)
        for s in range(COLUMN_BLOCKS + 2):
            tail_rows[r, :EARLY, s * LANES : (s + 1) * LANES] = tails[r, 3 * s : 3 * s + 3, :]

        x_8, b_8, c_8 = first_tokens(early[r], tail_rows[r])
        steps, cum, gate_8 = early[r, 2, :, :ROWS], early[r, 3, :, :ROWS], early[r, 4, :, :ROWS]
        skip = early[r, 5, 0:1, :ROWS]
        moved = steps * x_8
        last = cum[EARLY - 1 : EARLY]
        kept = jnp.where(row < EARLY, jnp.exp2(jnp.minimum(last - cum, 0.0)) * moved, 0.0)
        x_first[r] = kept
        b_first[r] = b_8
        c_first = jnp.concatenate([c_8, jnp.zeros_like(c_8)], axis=0).astype(bf16)
        c_rows = jnp.concatenate(
            [jnp.where(row_16 < EARLY, c_first, c_in[r * span : r * span + 16, :]),
             c_in[r * span + 16 : (r + 1) * span, :]],
            axis=0,
        )
        carried = lax.dot_general(c_rows, start[r], over_last, preferred_element_type=f32)
        scores = lax.dot_general(
            c_rows.astype(f32), b_8, over_last, preferred_element_type=f32
        )
        y_8 = skip * x_8 + jnp.exp2(cum) * carried[:8]
        for j in range(EARLY):
            decay = jnp.exp2(jnp.minimum(cum - cum[j : j + 1], 0.0))
            y_8 += jnp.where(row >= j, scores[:8, j : j + 1] * decay * moved[j : j + 1], 0.0)
        from_first = jnp.dot(scores, kept, preferred_element_type=f32)
        value = y_in[rows, :] + y_scale[rows, :] * (jnp.exp2(last) * carried + from_first)
        value = jnp.concatenate([jnp.where(row < EARLY, y_8 * gate_8, value[:8]), value[8:]], axis=0)
        mean_sq = jnp.mean(value * value, axis=1, keepdims=True)
        result = (value * lax.rsqrt(mean_sq + epsilon) * gain[...]).astype(bf16)
        for part in range(span // quarter):
            owner = r * (span // quarter) + part
            place = jnp.bitwise_xor(owner // 2, y) + 2 * jnp.bitwise_xor(owner % 2, x)
            at = pl.ds(pl.multiple_of(place * quarter, quarter), quarter)
            gated[at, :] = result[part * quarter : (part + 1) * quarter, :]


def project_kernel(first, columns, *refs):
    if first:
        *ins, weight, gated, x_first, b_first = refs[:11]
        l_send, l_own, l_on, r_send, r_own, r_on, *scratch = refs[11:]
        gate_rows(*ins, gated, x_first, b_first, *scratch)
    else:
        gated, weight, l_send, l_own, l_on, r_send, r_own, r_on = refs
    q = gated.shape[0] // 4
    half = l_own.shape[1]
    tile = min(half, TILE)
    for lo in range(0, 2 * half, tile):
        at = slice(columns + lo, columns + lo + tile)
        product = jnp.dot(gated[...], weight[:, at], preferred_element_type=f32).astype(bf16)
        own, block_y, block_x, block_xy = (product[j * q : (j + 1) * q] for j in range(4))
        if lo < half:
            to = slice(lo, lo + tile)
            l_send[0, :, to] = block_x
            l_send[1, :, to] = block_xy
            l_own[:, to] = own
            l_on[:, to] = block_y
        else:
            to = slice(lo - half, lo - half + tile)
            r_send[0, :, to] = block_y
            r_send[1, :, to] = block_xy
            r_own[:, to] = own
            r_on[:, to] = block_x


def final_kernel(mine, other, x_first, b_first, s_add, s_scale, e_scale, out):
    _, core = chip_and_core()
    heads = s_scale.shape[1] // 2

    def put(half, piece):
        at = half_at(half)
        of = pl.ds(pl.multiple_of(half * heads, heads), heads)
        after = by_head(piece[0, :HALF], e_scale[0, of, :]) + lax.dot_general(
            x_first[0, :, at], b_first[0], (((0,), (0,)), ((), ())), preferred_element_type=f32
        )
        out[0, at, :] = by_head(after, s_scale[0, of, :]) + s_add[0, at, :]

    put(core, mine)
    put(1 - core, other)


def over_replica(value, bits):
    pairs = [(r, r ^ bits) for r in range(2 * CHIPS)]
    return lax.ppermute(value, "replica", pairs)


def over_tensor(value, bits):
    return lax.ppermute(value, "tensor", [(t, t ^ bits) for t in range(4)])


def select(first, counts, plan, after, keep, recv):
    with jax.named_scope("select"):
        return pl.pallas_call(
            partial(select_kernel, first, counts),
            out_shape=[sds((n, ITEM_ROWS, LANES), bf16) for n in counts if n],
            in_specs=[SMEM, ANYWHERE, VMEM, VMEM],
            out_specs=[VMEM for n in counts if n],
            compiler_params=params(),
        )(plan, after, keep, recv)


def exchange(counts, sends):
    bits = [2 * d for d in range(1, CHIPS) if counts[d - 1]]
    return [over_replica(value, b) for value, b in zip(sends, bits)]


def migrate_more(counts, plan, keep, recv):
    came = exchange(counts, select(BASE, counts, plan, keep, keep, recv)) if any(counts) else []
    return pl.pallas_call(
        partial(spread_kernel, counts),
        out_shape=tuple(sds((n, ITEM_ROWS, LANES), bf16) for n in EXTRAS[-1]),
        in_specs=[VMEM] * len(came),
        out_specs=(VMEM,) * (CHIPS - 1),
        compiler_params=params(),
    )(*came)


def local_square(
    x_input,
    z_input,
    bc_input,
    dt_raw,
    dt_bias,
    decay_rates,
    skip_gain,
    conv_x,
    conv_bc,
    norm_gain,
    out_weight,
    cached_states,
    cached_tail_x,
    cached_tail_bc,
    prefix_block,
    lengths,
):
    tokens = x_input.shape[0]
    heads = dt_raw.shape[1]
    features = out_weight.shape[1]
    span = tokens // SLOTS

    with jax.named_scope("pack"):
        send, keep = pl.pallas_call(
            pack_kernel,
            out_shape=(sds((SLOTS, ITEM_ROWS, LANES), bf16),) * 2,
            in_specs=[HBM] * 3,
            out_specs=(VMEM, VMEM),
            scratch_shapes=[
                pltpu.VMEM((2, SLOTS, HALF, LANES), f32),
                pltpu.VMEM((CONV - 1, SLOTS) + cached_tail_x.shape[2:], f32),
                pltpu.VMEM((CONV - 1, SLOTS) + cached_tail_bc.shape[2:], f32),
                pltpu.VMEM((TAIL, LANES), f32),
                pltpu.SemaphoreType.DMA((4,)),
            ],
            compiler_params=params(),
        )(
            in_hbm(cached_states.reshape(SLOTS, ROWS, LANES)),
            in_hbm(jnp.transpose(cached_tail_x, (1, 0, 2))),
            in_hbm(jnp.transpose(cached_tail_bc, (1, 0, 2))),
        )
    recv = over_replica(send, 1)
    with jax.named_scope("plan"):
        plan, variant = pl.pallas_call(
            plan_kernel,
            out_shape=(pltpu.SMEM((PLACE_PLAN + ITEMS,), jnp.int32), pltpu.SMEM((1,), jnp.int32)),
            in_specs=[SMEM],
            out_specs=(SMEM, SMEM),
            compiler_params=params(),
        )(in_hbm(prefix_block))

    more = lax.switch(
        variant.reshape(()),
        [partial(migrate_more, counts) for counts in EXTRAS],
        plan,
        keep,
        recv,
    )
    sends = select((0,) * (CHIPS - 1), BASE, plan, more[0], keep, recv)
    came = exchange(BASE, sends)

    with jax.named_scope("scan"):
        scale = sds((SLOTS, heads, LANES), f32)
        y_in, y_scale, c_mat, s_add, s_scale, e_scale, early, weight = pl.pallas_call(
            scan_kernel,
            out_shape=(
                sds((tokens, ROWS), f32),
                sds((tokens, ROWS), f32),
                sds((tokens, STATE), bf16),
                sds((SLOTS, ROWS, STATE), f32),
                scale,
                scale,
                sds((SLOTS, 6, 8, WIDE), f32),
                pltpu.VMEM(out_weight.shape, bf16),
            ),
            in_specs=[ANYWHERE, SMEM] + [VMEM] * 9 + [HBM],
            out_specs=(VMEM,) * 8,
            scratch_shapes=[pltpu.VMEM((8 + span, WIDE), f32), pltpu.SemaphoreType.DMA((4,))],
            compiler_params=params(),
            cost_estimate=cost(8 << 20, 1 << 30),
        )(
            sends[0],
            lengths,
            x_input,
            z_input,
            bc_input,
            jnp.transpose(dt_raw),
            dt_bias.reshape(1, heads),
            decay_rates.reshape(1, heads),
            skip_gain.reshape(1, heads),
            conv_x,
            conv_bc,
            in_hbm(out_weight),
        )

    def place(owner, after):
        with jax.named_scope("place"):
            return pl.pallas_call(
                partial(place_kernel, owner),
                out_shape=sds((SLOTS, ITEM_ROWS, LANES), bf16),
                in_specs=[SMEM, ANYWHERE] + [VMEM] * 8,
                out_specs=VMEM,
                compiler_params=params(),
            )(plan, after, keep, recv, *came, *more)

    theirs = place(1, c_mat)
    other = over_replica(theirs, 1)
    mine = place(0, theirs)

    quarter = tokens // 4
    pieces = []
    gated = None
    for lo, hi in CHUNKS:
        lo, hi = lo * features // 8, hi * features // 8
        half = (hi - lo) // 2
        outs = [sds((2, quarter, half), bf16), sds((quarter, half), bf16), sds((quarter, half), bf16)]
        call = partial(
            pl.pallas_call,
            partial(project_kernel, gated is None, lo),
            compiler_params=params(),
            cost_estimate=cost(ROWS * (hi - lo) * 2, 2 * tokens * ROWS * (hi - lo)),
        )
        with jax.named_scope("project"):
            if gated is None:
                gated, x_first, b_first, *parts = call(
                    out_shape=[
                        sds((tokens, ROWS), bf16),
                        sds((SLOTS, 8, ROWS), f32),
                        sds((SLOTS, 8, STATE), f32),
                    ]
                    + 2 * outs,
                    in_specs=[VMEM] * 8,
                    out_specs=[VMEM] * 9,
                    scratch_shapes=[
                        pltpu.VMEM((SLOTS, ROWS, LANES), bf16),
                        pltpu.VMEM((SLOTS, TAIL, LANES), f32),
                        pltpu.VMEM((SLOTS, 8, WIDE), f32),
                    ],
                )(
                    y_in,
                    y_scale,
                    c_mat,
                    early,
                    mine,
                    other,
                    norm_gain.reshape(1, ROWS),
                    weight,
                )
            else:
                parts = call(
                    out_shape=2 * outs,
                    in_specs=[VMEM, VMEM],
                    out_specs=[VMEM] * 6,
                )(gated, weight)
        pieces.append(parts)

    with jax.named_scope("final_states"):

        def of_request(*shape):
            return pl.BlockSpec((1,) + shape, lambda n: (n,) + (0,) * len(shape))

        final_states = pl.pallas_call(
            final_kernel,
            grid=(SLOTS,),
            out_shape=sds((SLOTS, ROWS, STATE), f32),
            in_specs=[
                of_request(ITEM_ROWS, LANES),
                of_request(ITEM_ROWS, LANES),
                of_request(8, ROWS),
                of_request(8, STATE),
                of_request(ROWS, STATE),
                of_request(heads, LANES),
                of_request(heads, LANES),
            ],
            out_specs=of_request(ROWS, STATE),
            compiler_params=params(),
            cost_estimate=cost(4 << 20),
        )(mine, other, x_first, b_first, s_add, s_scale, e_scale)

    with jax.named_scope("sum"):
        came = []
        for l_send, _, _, r_send, _, _ in pieces:
            came.append((over_tensor(l_send, 1), over_tensor(r_send, 2)))
        passed = []
        for (l_came, r_came), (_, l_own, l_on, _, r_own, r_on) in zip(came, pieces):
            onward = (l_on.astype(f32) + l_came[1].astype(f32)).astype(bf16)
            l_last = over_tensor(onward, 2)
            onward = (r_on.astype(f32) + r_came[1].astype(f32)).astype(bf16)
            r_last = over_tensor(onward, 1)
            passed.append(l_own.astype(f32) + l_came[0].astype(f32) + l_last.astype(f32))
            passed.append(r_own.astype(f32) + r_came[0].astype(f32) + r_last.astype(f32))
        mixed = jnp.concatenate(passed, axis=1).astype(bf16)

    return (mixed, final_states.reshape(cached_states.shape))


def solution(mesh):
    placed = (
        P("replica", "tensor"),
        P("replica", "tensor"),
        P("replica", None),
        P("replica", "tensor"),
        P("tensor"),
        P("tensor"),
        P("tensor"),
        P(None, "tensor"),
        P(),
        P("tensor"),
        P("tensor", None),
        P("replica", "tensor", None, None),
        P("replica", None, "tensor"),
        P("replica", None, None),
        P(),
        P("replica"),
    )
    square = mesh.shape["replica"] == 2 * CHIPS and mesh.shape["tensor"] == GROUPS
    return jax.shard_map(
        local_square if square else local_any,
        mesh=mesh,
        in_specs=placed,
        out_specs=(P(("replica", "tensor"), None), P("replica", "tensor", None, None)),
        check_vma=False,
    )
```

```python
import math
from functools import partial

import jax
import jax.numpy as jnp
from jax import lax
from jax.experimental import pallas as pl
from jax.experimental.pallas import tpu as pltpu
from jax.sharding import PartitionSpec as P

HEADS = 128
HEAD_DIM = 32
STATE = 128
GROUPS = 4
CONV = 4


highest = lax.Precision.HIGHEST
epsilon = 1e-05
f32 = jnp.float32
bf16 = jnp.bfloat16
LOG2E = math.log2(math.e)
MIB = 1024 * 1024
VMEM_LIMIT = 24


def causal_conv(tail_rows, sequence, kernel):
    joined = jnp.concatenate([tail_rows, sequence], axis=0)
    length = sequence.shape[0]
    total = joined[0:length] * kernel[0][None, :]
    for offset in range(1, kernel.shape[0]):
        total = total + joined[offset : offset + length] * kernel[offset][None, :]
    return jax.nn.silu(total)


def span_scan(inputs, b_heads, c_heads, step_sizes, decay_rates, skip_gain, carry_state):
    logdec = -step_sizes * decay_rates[None, :]
    cumulative = jnp.cumsum(logdec, axis=0)
    count_rows = inputs.shape[0]
    causal = jnp.arange(count_rows)[:, None] >= jnp.arange(count_rows)[None, :]
    cum_heads = jnp.transpose(cumulative)
    differ = cum_heads[:, :, None] - cum_heads[:, None, :]
    decays = jnp.where(causal[None, :, :], jnp.exp(jnp.minimum(differ, 0.0)), 0.0)
    scores = jnp.einsum("ihn,jhn->hij", c_heads, b_heads, precision=highest)
    weights = scores * decays * jnp.transpose(step_sizes)[:, None, :]
    inside = jnp.einsum("hij,jhp->ihp", weights, inputs, precision=highest)
    carried = jnp.exp(cumulative)[:, :, None] * jnp.einsum(
        "ihn,hpn->ihp", c_heads, carry_state, precision=highest
    )
    output = inside + carried + skip_gain[None, :, None] * inputs
    ending = cumulative[-1]
    weigh_in = jnp.exp(ending[None, :] - cumulative) * step_sizes
    new_state = jnp.exp(ending)[:, None, None] * carry_state + jnp.einsum(
        "jh,jhp,jhn->hpn", weigh_in, inputs, b_heads, precision=highest
    )
    return (output, new_state)


def local_any(
    x_input,
    z_input,
    bc_input,
    dt_raw,
    dt_bias,
    decay_rates,
    skip_gain,
    conv_x,
    conv_bc,
    norm_gain,
    out_weight,
    cached_states,
    cached_tail_x,
    cached_tail_bc,
    prefix_block,
    lengths,
):
    requests = lengths.shape[0]
    local_heads = dt_raw.shape[1]
    tokens_dev = x_input.shape[0]
    slot_len = tokens_dev // requests
    wanted = lax.dynamic_slice_in_dim(prefix_block, lax.axis_index("replica") * requests, requests)

    def migrate(rows):
        rows = lax.all_gather(rows.astype(bf16), "replica", axis=0, tiled=True)
        return jnp.take(rows, wanted, axis=0).astype(f32)

    start_states = migrate(cached_states)
    start_tail_x = migrate(cached_tail_x)
    start_tail_bc = migrate(cached_tail_bc)
    head_ids = lax.axis_index("tensor") * local_heads + jnp.arange(local_heads)
    member = ((head_ids // (HEADS // GROUPS))[:, None] == jnp.arange(GROUPS)[None, :]).astype(f32)
    live = jnp.arange(slot_len)[None, :] < lengths[:, None]
    outputs = []
    finals = []
    for request in range(requests):
        row_lo = request * slot_len
        row_hi = row_lo + slot_len
        inputs = causal_conv(
            start_tail_x[request], x_input[row_lo:row_hi].astype(f32), conv_x
        ).reshape(slot_len, local_heads, HEAD_DIM)
        bc_conv = causal_conv(
            start_tail_bc[request], bc_input[row_lo:row_hi].astype(f32), conv_bc
        )
        b_groups = bc_conv[:, : GROUPS * STATE].reshape(slot_len, GROUPS, STATE)
        c_groups = bc_conv[:, GROUPS * STATE :].reshape(slot_len, GROUPS, STATE)
        b_heads = jnp.einsum("lgn,hg->lhn", b_groups, member, precision=highest)
        c_heads = jnp.einsum("lgn,hg->lhn", c_groups, member, precision=highest)
        step_sizes = jnp.where(
            live[request][:, None], jax.nn.softplus(dt_raw[row_lo:row_hi] + dt_bias[None, :]), 0.0
        )
        output, carry_state = span_scan(
            inputs, b_heads, c_heads, step_sizes, decay_rates, skip_gain, start_states[request]
        )
        outputs.append(output.reshape(slot_len, -1))
        finals.append(carry_state)
    outputs = jnp.concatenate(outputs, axis=0)
    final_states = jnp.stack(finals, axis=0)
    gate_vals = outputs * jax.nn.silu(z_input.astype(f32))
    by_head = gate_vals.reshape(tokens_dev, local_heads, HEAD_DIM)
    head_squares = jnp.sum(by_head * by_head, axis=2)
    partial_sq = jnp.dot(head_squares, member, precision=highest)
    totals = lax.psum(partial_sq, "tensor")
    mean_sq = jnp.dot(totals, jnp.transpose(member), precision=highest) / (
        HEADS * HEAD_DIM // GROUPS
    )
    normed = (by_head * lax.rsqrt(mean_sq + epsilon)[:, :, None]).reshape(
        tokens_dev, -1
    ) * norm_gain[None, :]
    gated = jnp.where(live.reshape(tokens_dev, 1), normed, 0.0).astype(bf16)
    mixed = lax.psum_scatter(
        jnp.dot(gated, out_weight, preferred_element_type=f32).astype(bf16),
        "tensor",
        scatter_dimension=0,
        tiled=True,
    )
    return (mixed, final_states)


CHIPS = 4
SLOTS = 2
ITEMS = 2 * SLOTS
ROWS = 1024
HALF = ROWS // 2
TAIL = 32
ITEM_ROWS = HALF + TAIL // 2
LANES = 128
COLUMN_BLOCKS = ROWS // LANES
WIDE = ROWS + 2 * STATE
EARLY = CONV - 1
BASE = (3, 2, 2)
EXTRAS = ((0, 0, 0), (0, 1, 0), (0, 0, 1), (1, 2, 2))
SEND_PLAN = 0
PLACE_PLAN = 3 * ITEMS
CHUNKS = ((0, 4), (4, 8))
TILE = 512

HBM = pl.BlockSpec(memory_space=pltpu.HBM)
ANYWHERE = pl.BlockSpec(memory_space=pl.ANY)
VMEM = pl.BlockSpec(memory_space=pltpu.VMEM)
SMEM = pl.BlockSpec(memory_space=pltpu.SMEM)


def sds(shape, dtype):
    return jax.ShapeDtypeStruct(shape, dtype)


def params():
    return pltpu.CompilerParams(vmem_limit_bytes=VMEM_LIMIT * MIB)


def in_hbm(value):
    return pltpu.with_memory_space_constraint(value, pltpu.HBM)


def cost(nbytes, flops=0):
    return pl.CostEstimate(flops=flops, bytes_accessed=nbytes, transcendentals=0)


def silu(value):
    half = 0.5 * value
    return half + half * jnp.tanh(half)


def chip_and_core():
    replica = lax.axis_index("replica")
    return replica // 2, lax.rem(replica, 2)


def half_at(core):
    return pl.ds(pl.multiple_of(core * HALF, HALF), HALF)


def tail_half(core):
    return pl.ds(pl.multiple_of(core * (TAIL // 2), TAIL // 2), TAIL // 2)


def pack_kernel(
    states,
    tail_x,
    tail_bc,
    send,
    keep,
    blocks,
    rows_x,
    rows_bc,
    scratch,
    sems,
):
    _, core = chip_and_core()
    group = lax.axis_index("tensor")
    copies = [
        pltpu.make_async_copy(states.at[:, half_at(1 - core)], blocks.at[0], sems.at[0]),
        pltpu.make_async_copy(tail_x, rows_x, sems.at[1]),
        pltpu.make_async_copy(tail_bc, rows_bc, sems.at[2]),
        pltpu.make_async_copy(states.at[:, half_at(core)], blocks.at[1], sems.at[3]),
    ]
    for copy in copies:
        copy.start()
    for copy in copies:
        copy.wait()
    scratch[...] = jnp.zeros_like(scratch)
    for block in range(SLOTS):
        for k in range(CONV - 1):
            for s in range(COLUMN_BLOCKS):
                scratch[3 * s + k : 3 * s + k + 1, :] = rows_x[
                    k, block : block + 1, s * LANES : (s + 1) * LANES
                ]
            for s in range(2):
                at = pl.multiple_of((s * GROUPS + group) * STATE, STATE)
                row = 3 * (COLUMN_BLOCKS + s) + k
                scratch[row : row + 1, :] = rows_bc[k, block : block + 1, pl.ds(at, STATE)]
        for part, out in enumerate((send, keep)):
            half = jnp.bitwise_xor(core, 1 - part)
            out[block, :HALF, :] = blocks[part, block].astype(bf16)
            out[block, HALF:, :] = scratch[tail_half(half), :].astype(bf16)


def plan_kernel(prefix, plan, variant):
    chip, core = chip_and_core()
    need = [jnp.int32(0)] * CHIPS
    for entry in range(PLACE_PLAN):
        plan[SEND_PLAN + entry] = 0
    for target in range(CHIPS):
        blocks = [prefix[target * ITEMS + place] for place in range(ITEMS)]
        sources = [block // ITEMS for block in blocks]
        for place in range(ITEMS):
            source = sources[place]
            item = lax.rem(blocks[place], ITEMS)
            rank = jnp.int32(0)
            for other in range(place):
                rank += jnp.where(sources[other] == source, 1, 0)
            distance = jnp.bitwise_xor(source, target)
            for d in range(1, CHIPS):
                need[d] = jnp.where(distance == d, jnp.maximum(need[d], rank + 1), need[d])

            @pl.when((source == chip) & (distance > 0))
            def _():
                plan[SEND_PLAN + (distance - 1) * ITEMS + rank] = item

            @pl.when(target == chip)
            def _():
                owner = jnp.bitwise_xor(core, place // SLOTS)
                at = PLACE_PLAN + owner * SLOTS + place % SLOTS
                plan[at] = distance * ITEMS + jnp.where(distance == 0, item, rank)

    choice = jnp.int32(len(EXTRAS) - 1)
    for v in reversed(range(len(EXTRAS) - 1)):
        fits = need[1] <= BASE[0] + EXTRAS[v][0]
        for d in range(2, CHIPS):
            fits = fits & (need[d] <= BASE[d - 1] + EXTRAS[v][d - 1])
        choice = jnp.where(fits, v, choice)
    variant[0] = choice


def copy_item(out, at, keep, recv, item, core):
    slot = lax.rem(item, SLOTS)
    mine = item // SLOTS == core

    @pl.when(mine)
    def _():
        out[at] = keep[slot]

    @pl.when(jnp.logical_not(mine))
    def _():
        out[at] = recv[slot]


def select_kernel(first, counts, plan, _, keep, recv, *outs):
    _, core = chip_and_core()
    outs = iter(outs)
    for d in range(1, CHIPS):
        if counts[d - 1]:
            out = next(outs)
            for slot in range(counts[d - 1]):
                item = plan[SEND_PLAN + (d - 1) * ITEMS + first[d - 1] + slot]
                copy_item(out, slot, keep, recv, item, core)


def spread_kernel(counts, *refs):
    outs = refs[-(CHIPS - 1) :]
    came = iter(refs)
    for n, out in zip(counts, outs):
        if n:
            out[:n] = next(came)[...]


def place_kernel(owner, plan, _, keep, recv, *refs):
    came, out = refs[: 2 * (CHIPS - 1)], refs[-1]
    _, core = chip_and_core()
    for slot in range(SLOTS):
        code = plan[PLACE_PLAN + owner * SLOTS + slot]
        d = code // ITEMS
        which = lax.rem(code, ITEMS)

        @pl.when(d == 0)
        def _():
            copy_item(out, slot, keep, recv, which, core)

        for e in range(1, CHIPS):
            few = BASE[e - 1]
            base, extra = came[e - 1], came[e + 2]

            @pl.when((d == e) & (which < few))
            def _():
                out[slot] = base[jnp.minimum(which, few - 1)]

            @pl.when((d == e) & (which >= few))
            def _():
                out[slot] = extra[jnp.maximum(which - few, 0)]


def scan_kernel(
    _,
    lengths,
    x_in,
    z_in,
    bc_in,
    dt_raw,
    dt_bias,
    decay,
    skip,
    conv_x,
    conv_bc,
    weight,
    y_in,
    y_scale,
    c_out,
    s_add,
    s_scale,
    e_scale,
    early,
    staged,
    u,
    sems,
):
    parts = sems.shape[0]
    deep = weight.shape[0] // parts
    copies = []
    for i in range(parts):
        at = slice(i * deep, (i + 1) * deep)
        copies.append(pltpu.make_async_copy(weight.at[at], staged.at[at], sems.at[i]))
        copies[-1].start()
    group = lax.axis_index("tensor")
    span = x_in.shape[0] // SLOTS
    heads = dt_raw.shape[0]
    row = lax.broadcasted_iota(jnp.int32, (span, span), 0)
    column = lax.broadcasted_iota(jnp.int32, (span, span), 1)
    causal = row >= column
    lower = causal.astype(f32)
    late = causal & (column >= EARLY)
    head_row = lax.broadcasted_iota(jnp.int32, (heads, ROWS), 0)
    head_column = lax.broadcasted_iota(jnp.int32, (heads, ROWS), 1) // HEAD_DIM
    expand = (head_row == head_column).astype(f32)
    skip_wide = jnp.dot(skip[...], expand, precision=highest, preferred_element_type=f32)
    same = lax.broadcasted_iota(jnp.int32, (heads, heads), 0) == lax.broadcasted_iota(
        jnp.int32, (heads, heads), 1
    )

    def upright(value):
        return jnp.sum(jnp.where(same, value, 0.0), axis=1, keepdims=True)

    bias = upright(dt_bias[...])
    rate = upright(decay[...]) * (-LOG2E)
    per_block = LANES // HEAD_DIM
    lane_head = lax.broadcasted_iota(jnp.int32, (span, LANES), 1) // HEAD_DIM
    token = lax.broadcasted_iota(jnp.int32, (heads, span), 1)
    over_last = (((1,), (1,)), ((), ()))
    over_first = (((0,), (0,)), ((), ()))
    u[0:8, :] = jnp.zeros((8, WIDE), f32)
    for r in range(SLOTS):
        rows = slice(r * span, (r + 1) * span)
        u[8 : 8 + span, :ROWS] = x_in[rows, :].astype(f32)
        for s in range(2):
            at = pl.multiple_of((s * GROUPS + group) * STATE, STATE)
            lo = ROWS + s * STATE
            u[8 : 8 + span, lo : lo + STATE] = bc_in[rows, pl.ds(at, STATE)].astype(f32)

        def conv(lo, taps):
            at = slice(lo, lo + LANES)
            total = u[5 : 5 + span, at] * taps(0)
            early[r, 1, 0:1, at] = taps(0)
            for k in range(1, CONV):
                total = total + u[5 + k : 5 + k + span, at] * taps(k)
                early[r, 1, k : k + 1, at] = taps(k)
            early[r, 0, :, at] = total[:8]
            return silu(total)

        def bc_conv(s):
            at = pl.multiple_of((s * GROUPS + group) * STATE, STATE)
            return conv(ROWS + s * STATE, lambda k: conv_bc[k : k + 1, pl.ds(at, STATE)])

        b_mat = bc_conv(0).astype(bf16)
        c_mat = bc_conv(1).astype(bf16)
        c_out[rows, :] = c_mat
        scores = lax.dot_general(c_mat, b_mat, over_last, preferred_element_type=f32)
        scores = jnp.where(late, scores, 0.0)

        live = lax.broadcasted_iota(jnp.int32, (span, 1), 0) < lengths[r]
        raw = dt_raw[:, rows] + bias
        steps = jnp.maximum(raw, 0.0) + jnp.log1p(jnp.exp(-jnp.abs(raw)))
        steps = jnp.where(token < lengths[r], steps, 0.0)
        logdec = steps * rate
        cum = lax.dot_general(
            lower, logdec, over_last, precision=highest, preferred_element_type=f32
        )
        cum_t = lax.dot_general(
            logdec, lower, over_last, precision=highest, preferred_element_type=f32
        )
        begin = cum_t[:, EARLY - 1 : EARLY]
        ending = cum_t[:, span - 1 : span]
        s_scale[r] = jnp.broadcast_to(jnp.exp2(ending - begin), (heads, LANES))
        e_scale[r] = jnp.broadcast_to(jnp.exp2(begin), (heads, LANES))
        weigh = jnp.where(token >= EARLY, jnp.exp2(ending - cum_t) * steps, 0.0)
        since = jnp.exp2(jnp.minimum(cum_t - begin, 0.0))
        wide = lax.dot_general(
            jnp.concatenate([steps, weigh, since, cum_t], axis=1),
            expand,
            over_first,
            precision=highest,
            preferred_element_type=f32,
        )
        early[r, 2, :, :ROWS] = wide[:8]
        early[r, 3, :, :ROWS] = wide[3 * span : 3 * span + 8]
        early[r, 5, :, :ROWS] = jnp.broadcast_to(skip_wide, (8, ROWS))
        for q in range(COLUMN_BLOCKS):
            lo = q * LANES
            cols = slice(lo, lo + LANES)
            xc = conv(lo, lambda k: conv_x[k : k + 1, cols])
            xdt = (xc * wide[:span, cols]).astype(bf16)
            xw = (xc * wide[span : 2 * span, cols]).astype(bf16)
            s_add[r, lo : lo + LANES, :] = lax.dot_general(
                xw, b_mat, over_first, preferred_element_type=f32
            )
            total = skip_wide[:, cols] * xc
            parts = []
            masked = []
            for i in range(per_block):
                h = q * per_block + i
                differ = cum[:, h : h + 1] - cum_t[h : h + 1, :]
                parts.append((jnp.exp2(jnp.minimum(differ, 0.0)) * scores).astype(bf16))
                masked.append(jnp.where(lane_head == i, xdt, jnp.zeros_like(xdt)))
            total = total + jnp.dot(
                jnp.concatenate(parts, axis=1),
                jnp.concatenate(masked, axis=0),
                preferred_element_type=f32,
            )
            gate = jnp.where(live, silu(z_in[rows, cols].astype(f32)), 0.0)
            early[r, 4, :, cols] = gate[:8]
            y_in[rows, cols] = total * gate
            y_scale[rows, cols] = wide[2 * span : 3 * span, cols] * gate
    for copy in copies:
        copy.wait()


def by_head(state, scale):
    heads = scale.shape[0]
    wide = state.astype(f32).reshape(heads, HEAD_DIM, LANES) * scale[:, None, :]
    return wide.reshape(heads * HEAD_DIM, LANES)


def first_tokens(early, tail):
    row = lax.broadcasted_iota(jnp.int32, (8, WIDE), 0)
    taps = early[1]
    total = early[0]
    for t in range(EARLY):
        add = sum(taps[k : k + 1] * tail[t + k : t + k + 1] for k in range(EARLY - t))
        total = jnp.where(row == t, total + add, total)
    act = silu(total)
    return act[:, :ROWS], act[:, ROWS : ROWS + STATE], act[:, ROWS + STATE :]


def gate_rows(
    y_in,
    y_scale,
    c_in,
    early,
    mine,
    other,
    gain,
    gated,
    x_first,
    b_first,
    start,
    tails,
    tail_rows,
):
    _, core = chip_and_core()
    tensor = lax.axis_index("tensor")
    x, y = lax.rem(tensor, 2), tensor // 2
    tokens = y_in.shape[0]
    span = tokens // SLOTS
    quarter = tokens // 4
    over_last = (((1,), (1,)), ((), ()))
    row = lax.broadcasted_iota(jnp.int32, (8, ROWS), 0)
    row_16 = lax.broadcasted_iota(jnp.int32, (16, LANES), 0)
    tail_rows[...] = jnp.zeros_like(tail_rows)
    for r in range(SLOTS):
        rows = slice(r * span, (r + 1) * span)
        start[r, half_at(core), :] = mine[r, :HALF]
        start[r, half_at(1 - core), :] = other[r, :HALF]
        tails[r, tail_half(core), :] = mine[r, HALF:].astype(f32)
        tails[r, tail_half(1 - core), :] = other[r, HALF:].astype(f32)
        for s in range(COLUMN_BLOCKS + 2):
            tail_rows[r, :EARLY, s * LANES : (s + 1) * LANES] = tails[r, 3 * s : 3 * s + 3, :]

        x_8, b_8, c_8 = first_tokens(early[r], tail_rows[r])
        steps, cum, gate_8 = early[r, 2, :, :ROWS], early[r, 3, :, :ROWS], early[r, 4, :, :ROWS]
        skip = early[r, 5, 0:1, :ROWS]
        moved = steps * x_8
        last = cum[EARLY - 1 : EARLY]
        kept = jnp.where(row < EARLY, jnp.exp2(jnp.minimum(last - cum, 0.0)) * moved, 0.0)
        x_first[r] = kept
        b_first[r] = b_8
        c_first = jnp.concatenate([c_8, jnp.zeros_like(c_8)], axis=0).astype(bf16)
        c_rows = jnp.concatenate(
            [jnp.where(row_16 < EARLY, c_first, c_in[r * span : r * span + 16, :]),
             c_in[r * span + 16 : (r + 1) * span, :]],
            axis=0,
        )
        carried = lax.dot_general(c_rows, start[r], over_last, preferred_element_type=f32)
        scores = lax.dot_general(
            c_rows.astype(f32), b_8, over_last, preferred_element_type=f32
        )
        y_8 = skip * x_8 + jnp.exp2(cum) * carried[:8]
        for j in range(EARLY):
            decay = jnp.exp2(jnp.minimum(cum - cum[j : j + 1], 0.0))
            y_8 += jnp.where(row >= j, scores[:8, j : j + 1] * decay * moved[j : j + 1], 0.0)
        from_first = jnp.dot(scores, kept, preferred_element_type=f32)
        value = y_in[rows, :] + y_scale[rows, :] * (jnp.exp2(last) * carried + from_first)
        value = jnp.concatenate([jnp.where(row < EARLY, y_8 * gate_8, value[:8]), value[8:]], axis=0)
        mean_sq = jnp.mean(value * value, axis=1, keepdims=True)
        result = (value * lax.rsqrt(mean_sq + epsilon) * gain[...]).astype(bf16)
        for part in range(span // quarter):
            owner = r * (span // quarter) + part
            place = jnp.bitwise_xor(owner // 2, y) + 2 * jnp.bitwise_xor(owner % 2, x)
            at = pl.ds(pl.multiple_of(place * quarter, quarter), quarter)
            gated[at, :] = result[part * quarter : (part + 1) * quarter, :]


def rows_of(gated, places):
    q = gated.shape[0] // 4
    return jnp.concatenate([gated[p * q : (p + 1) * q, :] for p in places], axis=0)


def product(rows, weight, lo, hi, put):
    for begin in range(lo, hi, TILE):
        end = min(begin + TILE, hi)
        value = jnp.dot(rows, weight[:, begin:end], preferred_element_type=f32)
        put(slice(begin - lo, end - lo), value.astype(bf16))


def send_kernel(first, lo, *refs):
    if first:
        *ins, weight, gated, x_first, b_first, l_send, r_send = refs[:13]
        gate_rows(*ins, gated, x_first, b_first, *refs[13:])
    else:
        gated, weight, l_send, r_send = refs
    q = gated.shape[0] // 4
    half = l_send.shape[2]
    for places, send, begin in (((2, 3), l_send, lo), ((1, 3), r_send, lo + half)):

        def put(to, value, send=send):
            send[0, :, to] = value[:q]
            send[1, :, to] = value[q:]

        product(rows_of(gated, places), weight, begin, begin + half, put)


def keep_kernel(chunks, _, gated, weight, *outs):
    q = gated.shape[0] // 4
    outs = iter(outs)
    for lo, half in chunks:
        for places, begin in (((0, 1), lo), ((0, 2), lo + half)):
            own, onward = next(outs), next(outs)

            def put(to, value, own=own, onward=onward):
                own[:, to] = value[:q]
                onward[:, to] = value[q:]

            product(rows_of(gated, places), weight, begin, begin + half, put)


def final_kernel(mine, other, x_first, b_first, s_add, s_scale, e_scale, out):
    _, core = chip_and_core()
    heads = s_scale.shape[1] // 2

    def put(half, piece):
        at = half_at(half)
        of = pl.ds(pl.multiple_of(half * heads, heads), heads)
        after = by_head(piece[0, :HALF], e_scale[0, of, :]) + lax.dot_general(
            x_first[0, :, at], b_first[0], (((0,), (0,)), ((), ())), preferred_element_type=f32
        )
        out[0, at, :] = by_head(after, s_scale[0, of, :]) + s_add[0, at, :]

    put(core, mine)
    put(1 - core, other)


def over_replica(value, bits):
    pairs = [(r, r ^ bits) for r in range(2 * CHIPS)]
    return lax.ppermute(value, "replica", pairs)


def over_tensor(value, bits):
    return lax.ppermute(value, "tensor", [(t, t ^ bits) for t in range(4)])


def select(first, counts, plan, after, keep, recv):
    with jax.named_scope("select"):
        return pl.pallas_call(
            partial(select_kernel, first, counts),
            out_shape=[sds((n, ITEM_ROWS, LANES), bf16) for n in counts if n],
            in_specs=[SMEM, ANYWHERE, VMEM, VMEM],
            out_specs=[VMEM for n in counts if n],
            compiler_params=params(),
        )(plan, after, keep, recv)


def exchange(counts, sends):
    bits = [2 * d for d in range(1, CHIPS) if counts[d - 1]]
    return [over_replica(value, b) for value, b in zip(sends, bits)]


def migrate_more(counts, plan, keep, recv):
    came = exchange(counts, select(BASE, counts, plan, keep, keep, recv)) if any(counts) else []
    return pl.pallas_call(
        partial(spread_kernel, counts),
        out_shape=tuple(sds((n, ITEM_ROWS, LANES), bf16) for n in EXTRAS[-1]),
        in_specs=[VMEM] * len(came),
        out_specs=(VMEM,) * (CHIPS - 1),
        compiler_params=params(),
    )(*came)


def local_square(
    x_input,
    z_input,
    bc_input,
    dt_raw,
    dt_bias,
    decay_rates,
    skip_gain,
    conv_x,
    conv_bc,
    norm_gain,
    out_weight,
    cached_states,
    cached_tail_x,
    cached_tail_bc,
    prefix_block,
    lengths,
):
    tokens = x_input.shape[0]
    heads = dt_raw.shape[1]
    features = out_weight.shape[1]
    span = tokens // SLOTS

    with jax.named_scope("pack"):
        send, keep = pl.pallas_call(
            pack_kernel,
            out_shape=(sds((SLOTS, ITEM_ROWS, LANES), bf16),) * 2,
            in_specs=[HBM] * 3,
            out_specs=(VMEM, VMEM),
            scratch_shapes=[
                pltpu.VMEM((2, SLOTS, HALF, LANES), f32),
                pltpu.VMEM((CONV - 1, SLOTS) + cached_tail_x.shape[2:], f32),
                pltpu.VMEM((CONV - 1, SLOTS) + cached_tail_bc.shape[2:], f32),
                pltpu.VMEM((TAIL, LANES), f32),
                pltpu.SemaphoreType.DMA((4,)),
            ],
            compiler_params=params(),
        )(
            in_hbm(cached_states.reshape(SLOTS, ROWS, LANES)),
            in_hbm(jnp.transpose(cached_tail_x, (1, 0, 2))),
            in_hbm(jnp.transpose(cached_tail_bc, (1, 0, 2))),
        )
    recv = over_replica(send, 1)
    with jax.named_scope("plan"):
        plan, variant = pl.pallas_call(
            plan_kernel,
            out_shape=(pltpu.SMEM((PLACE_PLAN + ITEMS,), jnp.int32), pltpu.SMEM((1,), jnp.int32)),
            in_specs=[SMEM],
            out_specs=(SMEM, SMEM),
            compiler_params=params(),
        )(in_hbm(prefix_block))

    more = lax.switch(
        variant.reshape(()),
        [partial(migrate_more, counts) for counts in EXTRAS],
        plan,
        keep,
        recv,
    )
    sends = select((0,) * (CHIPS - 1), BASE, plan, more[0], keep, recv)
    came = exchange(BASE, sends)

    with jax.named_scope("scan"):
        scale = sds((SLOTS, heads, LANES), f32)
        y_in, y_scale, c_mat, s_add, s_scale, e_scale, early, weight = pl.pallas_call(
            scan_kernel,
            out_shape=(
                sds((tokens, ROWS), f32),
                sds((tokens, ROWS), f32),
                sds((tokens, STATE), bf16),
                sds((SLOTS, ROWS, STATE), f32),
                scale,
                scale,
                sds((SLOTS, 6, 8, WIDE), f32),
                pltpu.VMEM(out_weight.shape, bf16),
            ),
            in_specs=[ANYWHERE, SMEM] + [VMEM] * 9 + [HBM],
            out_specs=(VMEM,) * 8,
            scratch_shapes=[pltpu.VMEM((8 + span, WIDE), f32), pltpu.SemaphoreType.DMA((4,))],
            compiler_params=params(),
            cost_estimate=cost(8 << 20, 1 << 30),
        )(
            sends[0],
            lengths,
            x_input,
            z_input,
            bc_input,
            jnp.transpose(dt_raw),
            dt_bias.reshape(1, heads),
            decay_rates.reshape(1, heads),
            skip_gain.reshape(1, heads),
            conv_x,
            conv_bc,
            in_hbm(out_weight),
        )

    def place(owner, after):
        with jax.named_scope("place"):
            return pl.pallas_call(
                partial(place_kernel, owner),
                out_shape=sds((SLOTS, ITEM_ROWS, LANES), bf16),
                in_specs=[SMEM, ANYWHERE] + [VMEM] * 8,
                out_specs=VMEM,
                compiler_params=params(),
            )(plan, after, keep, recv, *came, *more)

    theirs = place(1, c_mat)
    other = over_replica(theirs, 1)
    mine = place(0, theirs)

    quarter = tokens // 4
    spans = [(lo * features // 8, (hi - lo) * features // 16) for lo, hi in CHUNKS]
    sends = []
    gated = None
    for lo, half in spans:
        outs = [sds((2, quarter, half), bf16)] * 2
        call = partial(
            pl.pallas_call,
            partial(send_kernel, gated is None, lo),
            compiler_params=params(),
            cost_estimate=cost(ROWS * half * 4, 2 * tokens * ROWS * half),
        )
        with jax.named_scope("project"):
            if gated is None:
                gated, x_first, b_first, *parts = call(
                    out_shape=[
                        sds((tokens, ROWS), bf16),
                        sds((SLOTS, 8, ROWS), f32),
                        sds((SLOTS, 8, STATE), f32),
                    ]
                    + outs,
                    in_specs=[VMEM] * 8,
                    out_specs=[VMEM] * 5,
                    scratch_shapes=[
                        pltpu.VMEM((SLOTS, ROWS, LANES), bf16),
                        pltpu.VMEM((SLOTS, TAIL, LANES), f32),
                        pltpu.VMEM((SLOTS, 8, WIDE), f32),
                    ],
                )(
                    y_in,
                    y_scale,
                    c_mat,
                    early,
                    mine,
                    other,
                    norm_gain.reshape(1, ROWS),
                    weight,
                )
            else:
                parts = call(
                    out_shape=outs,
                    in_specs=[VMEM] * 2,
                    out_specs=[VMEM] * 2,
                )(gated, weight)
        sends.append(parts)
    with jax.named_scope("project"):
        kept = pl.pallas_call(
            partial(keep_kernel, spans),
            out_shape=[sds((quarter, half), bf16) for _, half in spans for _ in range(4)],
            in_specs=[ANYWHERE] + [VMEM] * 2,
            out_specs=[VMEM] * (4 * len(spans)),
            compiler_params=params(),
            cost_estimate=cost(ROWS * features * 2, tokens * ROWS * features),
        )(sends[-1][0], gated, weight)

    with jax.named_scope("final_states"):

        def of_request(*shape):
            return pl.BlockSpec((1,) + shape, lambda n: (n,) + (0,) * len(shape))

        final_states = pl.pallas_call(
            final_kernel,
            grid=(SLOTS,),
            out_shape=sds((SLOTS, ROWS, STATE), f32),
            in_specs=[
                of_request(ITEM_ROWS, LANES),
                of_request(ITEM_ROWS, LANES),
                of_request(8, ROWS),
                of_request(8, STATE),
                of_request(ROWS, STATE),
                of_request(heads, LANES),
                of_request(heads, LANES),
            ],
            out_specs=of_request(ROWS, STATE),
            compiler_params=params(),
            cost_estimate=cost(4 << 20),
        )(mine, other, x_first, b_first, s_add, s_scale, e_scale)

    with jax.named_scope("sum"):
        came = [(over_tensor(l_send, 1), over_tensor(r_send, 2)) for l_send, r_send in sends]
        passed = []
        for n, (l_came, r_came) in enumerate(came):
            l_own, l_on, r_own, r_on = kept[4 * n : 4 * n + 4]
            onward = (l_on.astype(f32) + l_came[1].astype(f32)).astype(bf16)
            l_last = over_tensor(onward, 2)
            onward = (r_on.astype(f32) + r_came[1].astype(f32)).astype(bf16)
            r_last = over_tensor(onward, 1)
            passed.append(l_own.astype(f32) + l_came[0].astype(f32) + l_last.astype(f32))
            passed.append(r_own.astype(f32) + r_came[0].astype(f32) + r_last.astype(f32))
        mixed = jnp.concatenate(passed, axis=1).astype(bf16)

    return (mixed, final_states.reshape(cached_states.shape))


def solution(mesh):
    placed = (
        P("replica", "tensor"),
        P("replica", "tensor"),
        P("replica", None),
        P("replica", "tensor"),
        P("tensor"),
        P("tensor"),
        P("tensor"),
        P(None, "tensor"),
        P(),
        P("tensor"),
        P("tensor", None),
        P("replica", "tensor", None, None),
        P("replica", None, "tensor"),
        P("replica", None, None),
        P(),
        P("replica"),
    )
    square = mesh.shape["replica"] == 2 * CHIPS and mesh.shape["tensor"] == GROUPS
    return jax.shard_map(
        local_square if square else local_any,
        mesh=mesh,
        in_specs=placed,
        out_specs=(P(("replica", "tensor"), None), P("replica", "tensor", None, None)),
        check_vma=False,
    )
```

```python
import math
from functools import partial

import jax
import jax.numpy as jnp
from jax import lax
from jax.experimental import pallas as pl
from jax.experimental.pallas import tpu as pltpu
from jax.sharding import PartitionSpec as P

HEADS = 128
HEAD_DIM = 32
STATE = 128
GROUPS = 4
CONV = 4


highest = lax.Precision.HIGHEST
epsilon = 1e-05
f32 = jnp.float32
bf16 = jnp.bfloat16
LOG2E = math.log2(math.e)
MIB = 1024 * 1024
VMEM_LIMIT = 24


def causal_conv(tail_rows, sequence, kernel):
    joined = jnp.concatenate([tail_rows, sequence], axis=0)
    length = sequence.shape[0]
    total = joined[0:length] * kernel[0][None, :]
    for offset in range(1, kernel.shape[0]):
        total = total + joined[offset : offset + length] * kernel[offset][None, :]
    return jax.nn.silu(total)


def span_scan(inputs, b_heads, c_heads, step_sizes, decay_rates, skip_gain, carry_state):
    logdec = -step_sizes * decay_rates[None, :]
    cumulative = jnp.cumsum(logdec, axis=0)
    count_rows = inputs.shape[0]
    causal = jnp.arange(count_rows)[:, None] >= jnp.arange(count_rows)[None, :]
    cum_heads = jnp.transpose(cumulative)
    differ = cum_heads[:, :, None] - cum_heads[:, None, :]
    decays = jnp.where(causal[None, :, :], jnp.exp(jnp.minimum(differ, 0.0)), 0.0)
    scores = jnp.einsum("ihn,jhn->hij", c_heads, b_heads, precision=highest)
    weights = scores * decays * jnp.transpose(step_sizes)[:, None, :]
    inside = jnp.einsum("hij,jhp->ihp", weights, inputs, precision=highest)
    carried = jnp.exp(cumulative)[:, :, None] * jnp.einsum(
        "ihn,hpn->ihp", c_heads, carry_state, precision=highest
    )
    output = inside + carried + skip_gain[None, :, None] * inputs
    ending = cumulative[-1]
    weigh_in = jnp.exp(ending[None, :] - cumulative) * step_sizes
    new_state = jnp.exp(ending)[:, None, None] * carry_state + jnp.einsum(
        "jh,jhp,jhn->hpn", weigh_in, inputs, b_heads, precision=highest
    )
    return (output, new_state)


def local_any(
    x_input,
    z_input,
    bc_input,
    dt_raw,
    dt_bias,
    decay_rates,
    skip_gain,
    conv_x,
    conv_bc,
    norm_gain,
    out_weight,
    cached_states,
    cached_tail_x,
    cached_tail_bc,
    prefix_block,
    lengths,
):
    requests = lengths.shape[0]
    local_heads = dt_raw.shape[1]
    tokens_dev = x_input.shape[0]
    slot_len = tokens_dev // requests
    wanted = lax.dynamic_slice_in_dim(prefix_block, lax.axis_index("replica") * requests, requests)

    def migrate(rows):
        rows = lax.all_gather(rows.astype(bf16), "replica", axis=0, tiled=True)
        return jnp.take(rows, wanted, axis=0).astype(f32)

    start_states = migrate(cached_states)
    start_tail_x = migrate(cached_tail_x)
    start_tail_bc = migrate(cached_tail_bc)
    head_ids = lax.axis_index("tensor") * local_heads + jnp.arange(local_heads)
    member = ((head_ids // (HEADS // GROUPS))[:, None] == jnp.arange(GROUPS)[None, :]).astype(f32)
    live = jnp.arange(slot_len)[None, :] < lengths[:, None]
    outputs = []
    finals = []
    for request in range(requests):
        row_lo = request * slot_len
        row_hi = row_lo + slot_len
        inputs = causal_conv(
            start_tail_x[request], x_input[row_lo:row_hi].astype(f32), conv_x
        ).reshape(slot_len, local_heads, HEAD_DIM)
        bc_conv = causal_conv(
            start_tail_bc[request], bc_input[row_lo:row_hi].astype(f32), conv_bc
        )
        b_groups = bc_conv[:, : GROUPS * STATE].reshape(slot_len, GROUPS, STATE)
        c_groups = bc_conv[:, GROUPS * STATE :].reshape(slot_len, GROUPS, STATE)
        b_heads = jnp.einsum("lgn,hg->lhn", b_groups, member, precision=highest)
        c_heads = jnp.einsum("lgn,hg->lhn", c_groups, member, precision=highest)
        step_sizes = jnp.where(
            live[request][:, None], jax.nn.softplus(dt_raw[row_lo:row_hi] + dt_bias[None, :]), 0.0
        )
        output, carry_state = span_scan(
            inputs, b_heads, c_heads, step_sizes, decay_rates, skip_gain, start_states[request]
        )
        outputs.append(output.reshape(slot_len, -1))
        finals.append(carry_state)
    outputs = jnp.concatenate(outputs, axis=0)
    final_states = jnp.stack(finals, axis=0)
    gate_vals = outputs * jax.nn.silu(z_input.astype(f32))
    by_head = gate_vals.reshape(tokens_dev, local_heads, HEAD_DIM)
    head_squares = jnp.sum(by_head * by_head, axis=2)
    partial_sq = jnp.dot(head_squares, member, precision=highest)
    totals = lax.psum(partial_sq, "tensor")
    mean_sq = jnp.dot(totals, jnp.transpose(member), precision=highest) / (
        HEADS * HEAD_DIM // GROUPS
    )
    normed = (by_head * lax.rsqrt(mean_sq + epsilon)[:, :, None]).reshape(
        tokens_dev, -1
    ) * norm_gain[None, :]
    gated = jnp.where(live.reshape(tokens_dev, 1), normed, 0.0).astype(bf16)
    mixed = lax.psum_scatter(
        jnp.dot(gated, out_weight, preferred_element_type=f32).astype(bf16),
        "tensor",
        scatter_dimension=0,
        tiled=True,
    )
    return (mixed, final_states)


CHIPS = 4
SLOTS = 2
ITEMS = 2 * SLOTS
ROWS = 1024
HALF = ROWS // 2
TAIL = 32
ITEM_ROWS = HALF + TAIL // 2
LANES = 128
COLUMN_BLOCKS = ROWS // LANES
WIDE = ROWS + 2 * STATE
EARLY = CONV - 1
BASE = (3, 2, 2)
EXTRAS = ((0, 0, 0), (0, 1, 0), (0, 0, 1), (0, 1, 1), (1, 2, 2))
SEND_PLAN = 0
PLACE_PLAN = 3 * ITEMS
CHUNKS = ((0, 4), (4, 8))
TILE = 1024

HBM = pl.BlockSpec(memory_space=pltpu.HBM)
ANYWHERE = pl.BlockSpec(memory_space=pl.ANY)
VMEM = pl.BlockSpec(memory_space=pltpu.VMEM)
SMEM = pl.BlockSpec(memory_space=pltpu.SMEM)


def sds(shape, dtype):
    return jax.ShapeDtypeStruct(shape, dtype)


def params():
    return pltpu.CompilerParams(vmem_limit_bytes=VMEM_LIMIT * MIB)


def in_hbm(value):
    return pltpu.with_memory_space_constraint(value, pltpu.HBM)


def cost(nbytes, flops=0):
    return pl.CostEstimate(flops=flops, bytes_accessed=nbytes, transcendentals=0)


def silu(value):
    half = 0.5 * value
    return half + half * jnp.tanh(half)


def chip_and_core():
    replica = lax.axis_index("replica")
    return replica // 2, lax.rem(replica, 2)


def half_at(core):
    return pl.ds(pl.multiple_of(core * HALF, HALF), HALF)


def tail_half(core):
    return pl.ds(pl.multiple_of(core * (TAIL // 2), TAIL // 2), TAIL // 2)


def pack_kernel(
    states,
    tail_x,
    tail_bc,
    send,
    keep,
    blocks,
    rows_x,
    rows_bc,
    scratch,
    sems,
):
    _, core = chip_and_core()
    group = lax.axis_index("tensor")
    copies = [
        pltpu.make_async_copy(states.at[:, half_at(1 - core)], blocks.at[0], sems.at[0]),
        pltpu.make_async_copy(tail_x, rows_x, sems.at[1]),
        pltpu.make_async_copy(tail_bc, rows_bc, sems.at[2]),
        pltpu.make_async_copy(states.at[:, half_at(core)], blocks.at[1], sems.at[3]),
    ]
    for copy in copies:
        copy.start()
    for copy in copies:
        copy.wait()
    scratch[...] = jnp.zeros_like(scratch)
    for block in range(SLOTS):
        for k in range(CONV - 1):
            for s in range(COLUMN_BLOCKS):
                scratch[3 * s + k : 3 * s + k + 1, :] = rows_x[
                    k, block : block + 1, s * LANES : (s + 1) * LANES
                ]
            for s in range(2):
                at = pl.multiple_of((s * GROUPS + group) * STATE, STATE)
                row = 3 * (COLUMN_BLOCKS + s) + k
                scratch[row : row + 1, :] = rows_bc[k, block : block + 1, pl.ds(at, STATE)]
        for part, out in enumerate((send, keep)):
            half = jnp.bitwise_xor(core, 1 - part)
            out[block, :HALF, :] = blocks[part, block].astype(bf16)
            out[block, HALF:, :] = scratch[tail_half(half), :].astype(bf16)


def plan_kernel(prefix, plan, variant):
    chip, core = chip_and_core()
    need = [jnp.int32(0)] * CHIPS
    for entry in range(PLACE_PLAN):
        plan[SEND_PLAN + entry] = 0
    for target in range(CHIPS):
        blocks = [prefix[target * ITEMS + place] for place in range(ITEMS)]
        sources = [block // ITEMS for block in blocks]
        for place in range(ITEMS):
            source = sources[place]
            item = lax.rem(blocks[place], ITEMS)
            rank = jnp.int32(0)
            for other in range(place):
                rank += jnp.where(sources[other] == source, 1, 0)
            distance = jnp.bitwise_xor(source, target)
            for d in range(1, CHIPS):
                need[d] = jnp.where(distance == d, jnp.maximum(need[d], rank + 1), need[d])

            @pl.when((source == chip) & (distance > 0))
            def _():
                plan[SEND_PLAN + (distance - 1) * ITEMS + rank] = item

            @pl.when(target == chip)
            def _():
                owner = jnp.bitwise_xor(core, place // SLOTS)
                at = PLACE_PLAN + owner * SLOTS + place % SLOTS
                plan[at] = distance * ITEMS + jnp.where(distance == 0, item, rank)

    choice = jnp.int32(len(EXTRAS) - 1)
    for v in reversed(range(len(EXTRAS) - 1)):
        fits = need[1] <= BASE[0] + EXTRAS[v][0]
        for d in range(2, CHIPS):
            fits = fits & (need[d] <= BASE[d - 1] + EXTRAS[v][d - 1])
        choice = jnp.where(fits, v, choice)
    variant[0] = choice


def copy_item(out, at, keep, recv, item, core):
    slot = lax.rem(item, SLOTS)
    mine = item // SLOTS == core

    @pl.when(mine)
    def _():
        out[at] = keep[slot]

    @pl.when(jnp.logical_not(mine))
    def _():
        out[at] = recv[slot]


def select_kernel(first, counts, plan, _, keep, recv, *outs):
    _, core = chip_and_core()
    outs = iter(outs)
    for d in range(1, CHIPS):
        if counts[d - 1]:
            out = next(outs)
            for slot in range(counts[d - 1]):
                item = plan[SEND_PLAN + (d - 1) * ITEMS + first[d - 1] + slot]
                copy_item(out, slot, keep, recv, item, core)


def spread_kernel(counts, *refs):
    outs = refs[-(CHIPS - 1) :]
    came = iter(refs)
    for n, out in zip(counts, outs):
        if n:
            out[:n] = next(came)[...]


def place_kernel(owner, plan, _, keep, recv, *refs):
    came, out = refs[: 2 * (CHIPS - 1)], refs[-1]
    _, core = chip_and_core()
    for slot in range(SLOTS):
        code = plan[PLACE_PLAN + owner * SLOTS + slot]
        d = code // ITEMS
        which = lax.rem(code, ITEMS)

        @pl.when(d == 0)
        def _():
            copy_item(out, slot, keep, recv, which, core)

        for e in range(1, CHIPS):
            few = BASE[e - 1]
            base, extra = came[e - 1], came[e + 2]

            @pl.when((d == e) & (which < few))
            def _():
                out[slot] = base[jnp.minimum(which, few - 1)]

            @pl.when((d == e) & (which >= few))
            def _():
                out[slot] = extra[jnp.maximum(which - few, 0)]


def scan_kernel(
    _,
    lengths,
    x_in,
    z_in,
    bc_in,
    dt_raw,
    dt_bias,
    decay,
    skip,
    conv_x,
    conv_bc,
    weight,
    y_in,
    y_scale,
    c_out,
    s_add,
    s_scale,
    e_scale,
    early,
    staged,
    u,
    sems,
):
    parts = sems.shape[0]
    deep = weight.shape[0] // parts
    copies = []
    for i in range(parts):
        at = slice(i * deep, (i + 1) * deep)
        copies.append(pltpu.make_async_copy(weight.at[at], staged.at[at], sems.at[i]))
        copies[-1].start()
    group = lax.axis_index("tensor")
    span = x_in.shape[0] // SLOTS
    heads = dt_raw.shape[0]
    row = lax.broadcasted_iota(jnp.int32, (span, span), 0)
    column = lax.broadcasted_iota(jnp.int32, (span, span), 1)
    causal = row >= column
    lower = causal.astype(f32)
    late = causal & (column >= EARLY)
    head_row = lax.broadcasted_iota(jnp.int32, (heads, ROWS), 0)
    head_column = lax.broadcasted_iota(jnp.int32, (heads, ROWS), 1) // HEAD_DIM
    expand = (head_row == head_column).astype(f32)
    skip_wide = jnp.dot(skip[...], expand, precision=highest, preferred_element_type=f32)
    same = lax.broadcasted_iota(jnp.int32, (heads, heads), 0) == lax.broadcasted_iota(
        jnp.int32, (heads, heads), 1
    )

    def upright(value):
        return jnp.sum(jnp.where(same, value, 0.0), axis=1, keepdims=True)

    bias = upright(dt_bias[...])
    rate = upright(decay[...]) * (-LOG2E)
    per_block = LANES // HEAD_DIM
    lane_head = lax.broadcasted_iota(jnp.int32, (span, LANES), 1) // HEAD_DIM
    token = lax.broadcasted_iota(jnp.int32, (heads, span), 1)
    over_last = (((1,), (1,)), ((), ()))
    over_first = (((0,), (0,)), ((), ()))
    u[0:8, :] = jnp.zeros((8, WIDE), f32)
    for r in range(SLOTS):
        rows = slice(r * span, (r + 1) * span)
        u[8 : 8 + span, :ROWS] = x_in[rows, :].astype(f32)
        for s in range(2):
            at = pl.multiple_of((s * GROUPS + group) * STATE, STATE)
            lo = ROWS + s * STATE
            u[8 : 8 + span, lo : lo + STATE] = bc_in[rows, pl.ds(at, STATE)].astype(f32)

        def conv(lo, taps):
            at = slice(lo, lo + LANES)
            total = u[5 : 5 + span, at] * taps(0)
            early[r, 1, 0:1, at] = taps(0)
            for k in range(1, CONV):
                total = total + u[5 + k : 5 + k + span, at] * taps(k)
                early[r, 1, k : k + 1, at] = taps(k)
            early[r, 0, :, at] = total[:8]
            return silu(total)

        def bc_conv(s):
            at = pl.multiple_of((s * GROUPS + group) * STATE, STATE)
            return conv(ROWS + s * STATE, lambda k: conv_bc[k : k + 1, pl.ds(at, STATE)])

        b_mat = bc_conv(0).astype(bf16)
        c_mat = bc_conv(1).astype(bf16)
        c_out[rows, :] = c_mat
        scores = lax.dot_general(c_mat, b_mat, over_last, preferred_element_type=f32)
        scores = jnp.where(late, scores, 0.0)

        live = lax.broadcasted_iota(jnp.int32, (span, 1), 0) < lengths[r]
        raw = dt_raw[:, rows] + bias
        steps = jnp.maximum(raw, 0.0) + jnp.log1p(jnp.exp(-jnp.abs(raw)))
        steps = jnp.where(token < lengths[r], steps, 0.0)
        logdec = steps * rate
        cum = lax.dot_general(
            lower, logdec, over_last, precision=highest, preferred_element_type=f32
        )
        cum_t = lax.dot_general(
            logdec, lower, over_last, precision=highest, preferred_element_type=f32
        )
        begin = cum_t[:, EARLY - 1 : EARLY]
        ending = cum_t[:, span - 1 : span]
        s_scale[r] = jnp.broadcast_to(jnp.exp2(ending - begin), (heads, LANES))
        e_scale[r] = jnp.broadcast_to(jnp.exp2(begin), (heads, LANES))
        weigh = jnp.where(token >= EARLY, jnp.exp2(ending - cum_t) * steps, 0.0)
        since = jnp.exp2(jnp.minimum(cum_t - begin, 0.0))
        wide = lax.dot_general(
            jnp.concatenate([steps, weigh, since, cum_t], axis=1),
            expand,
            over_first,
            precision=highest,
            preferred_element_type=f32,
        )
        early[r, 2, :, :ROWS] = wide[:8]
        early[r, 3, :, :ROWS] = wide[3 * span : 3 * span + 8]
        early[r, 5, :, :ROWS] = jnp.broadcast_to(skip_wide, (8, ROWS))
        for q in range(COLUMN_BLOCKS):
            lo = q * LANES
            cols = slice(lo, lo + LANES)
            xc = conv(lo, lambda k: conv_x[k : k + 1, cols])
            xdt = (xc * wide[:span, cols]).astype(bf16)
            xw = (xc * wide[span : 2 * span, cols]).astype(bf16)
            s_add[r, lo : lo + LANES, :] = lax.dot_general(
                xw, b_mat, over_first, preferred_element_type=f32
            )
            total = skip_wide[:, cols] * xc
            parts = []
            masked = []
            for i in range(per_block):
                h = q * per_block + i
                differ = cum[:, h : h + 1] - cum_t[h : h + 1, :]
                parts.append((jnp.exp2(jnp.minimum(differ, 0.0)) * scores).astype(bf16))
                masked.append(jnp.where(lane_head == i, xdt, jnp.zeros_like(xdt)))
            total = total + jnp.dot(
                jnp.concatenate(parts, axis=1),
                jnp.concatenate(masked, axis=0),
                preferred_element_type=f32,
            )
            gate = jnp.where(live, silu(z_in[rows, cols].astype(f32)), 0.0)
            early[r, 4, :, cols] = gate[:8]
            y_in[rows, cols] = total * gate
            y_scale[rows, cols] = wide[2 * span : 3 * span, cols] * gate
    for copy in copies:
        copy.wait()


def by_head(state, scale):
    heads = scale.shape[0]
    wide = state.astype(f32).reshape(heads, HEAD_DIM, LANES) * scale[:, None, :]
    return wide.reshape(heads * HEAD_DIM, LANES)


def first_tokens(early, tail):
    row = lax.broadcasted_iota(jnp.int32, (8, WIDE), 0)
    taps = early[1]
    total = early[0]
    for t in range(EARLY):
        add = sum(taps[k : k + 1] * tail[t + k : t + k + 1] for k in range(EARLY - t))
        total = jnp.where(row == t, total + add, total)
    act = silu(total)
    return act[:, :ROWS], act[:, ROWS : ROWS + STATE], act[:, ROWS + STATE :]


def gate_rows(
    y_in,
    y_scale,
    c_in,
    early,
    mine,
    other,
    gain,
    gated,
    x_first,
    b_first,
    start,
    tails,
    tail_rows,
):
    _, core = chip_and_core()
    tensor = lax.axis_index("tensor")
    x, y = lax.rem(tensor, 2), tensor // 2
    tokens = y_in.shape[0]
    span = tokens // SLOTS
    quarter = tokens // 4
    over_last = (((1,), (1,)), ((), ()))
    row = lax.broadcasted_iota(jnp.int32, (8, ROWS), 0)
    row_16 = lax.broadcasted_iota(jnp.int32, (16, LANES), 0)
    tail_rows[...] = jnp.zeros_like(tail_rows)
    for r in range(SLOTS):
        rows = slice(r * span, (r + 1) * span)
        start[r, half_at(core), :] = mine[r, :HALF]
        start[r, half_at(1 - core), :] = other[r, :HALF]
        tails[r, tail_half(core), :] = mine[r, HALF:].astype(f32)
        tails[r, tail_half(1 - core), :] = other[r, HALF:].astype(f32)
        for s in range(COLUMN_BLOCKS + 2):
            tail_rows[r, :EARLY, s * LANES : (s + 1) * LANES] = tails[r, 3 * s : 3 * s + 3, :]

        x_8, b_8, c_8 = first_tokens(early[r], tail_rows[r])
        steps, cum, gate_8 = early[r, 2, :, :ROWS], early[r, 3, :, :ROWS], early[r, 4, :, :ROWS]
        skip = early[r, 5, 0:1, :ROWS]
        moved = steps * x_8
        last = cum[EARLY - 1 : EARLY]
        kept = jnp.where(row < EARLY, jnp.exp2(jnp.minimum(last - cum, 0.0)) * moved, 0.0)
        x_first[r] = kept
        b_first[r] = b_8
        c_first = jnp.concatenate([c_8, jnp.zeros_like(c_8)], axis=0).astype(bf16)
        c_rows = jnp.concatenate(
            [jnp.where(row_16 < EARLY, c_first, c_in[r * span : r * span + 16, :]),
             c_in[r * span + 16 : (r + 1) * span, :]],
            axis=0,
        )
        carried = lax.dot_general(c_rows, start[r], over_last, preferred_element_type=f32)
        scores = lax.dot_general(
            c_rows.astype(f32), b_8, over_last, preferred_element_type=f32
        )
        y_8 = skip * x_8 + jnp.exp2(cum) * carried[:8]
        for j in range(EARLY):
            decay = jnp.exp2(jnp.minimum(cum - cum[j : j + 1], 0.0))
            y_8 += jnp.where(row >= j, scores[:8, j : j + 1] * decay * moved[j : j + 1], 0.0)
        from_first = jnp.dot(scores, kept, preferred_element_type=f32)
        value = y_in[rows, :] + y_scale[rows, :] * (jnp.exp2(last) * carried + from_first)
        value = jnp.concatenate([jnp.where(row < EARLY, y_8 * gate_8, value[:8]), value[8:]], axis=0)
        mean_sq = jnp.mean(value * value, axis=1, keepdims=True)
        result = (value * lax.rsqrt(mean_sq + epsilon) * gain[...]).astype(bf16)
        for part in range(span // quarter):
            owner = r * (span // quarter) + part
            place = jnp.bitwise_xor(owner // 2, y) + 2 * jnp.bitwise_xor(owner % 2, x)
            at = pl.ds(pl.multiple_of(place * quarter, quarter), quarter)
            gated[at, :] = result[part * quarter : (part + 1) * quarter, :]


def rows_of(gated, places):
    q = gated.shape[0] // 4
    return jnp.concatenate([gated[p * q : (p + 1) * q, :] for p in places], axis=0)


def product(rows, weight, lo, hi, put):
    for begin in range(lo, hi, TILE):
        end = min(begin + TILE, hi)
        value = jnp.dot(rows, weight[:, begin:end], preferred_element_type=f32)
        put(slice(begin - lo, end - lo), value.astype(bf16))


def send_kernel(first, lo, *refs):
    if first:
        *ins, weight, gated, x_first, b_first, l_send, r_send = refs[:13]
        gate_rows(*ins, gated, x_first, b_first, *refs[13:])
    else:
        gated, weight, l_send, r_send = refs
    q = gated.shape[0] // 4
    half = l_send.shape[2]
    for places, send, begin in (((2, 3), l_send, lo), ((1, 3), r_send, lo + half)):

        def put(to, value, send=send):
            send[0, :, to] = value[:q]
            send[1, :, to] = value[q:]

        product(rows_of(gated, places), weight, begin, begin + half, put)


def keep_kernel(chunks, _, gated, weight, *outs):
    q = gated.shape[0] // 4
    outs = iter(outs)
    for lo, half in chunks:
        for places, begin in (((0, 1), lo), ((0, 2), lo + half)):
            own, onward = next(outs), next(outs)

            def put(to, value, own=own, onward=onward):
                own[:, to] = value[:q]
                onward[:, to] = value[q:]

            product(rows_of(gated, places), weight, begin, begin + half, put)


def final_kernel(mine, other, x_first, b_first, s_add, s_scale, e_scale, out):
    _, core = chip_and_core()
    heads = s_scale.shape[1] // 2

    def put(half, piece):
        at = half_at(half)
        of = pl.ds(pl.multiple_of(half * heads, heads), heads)
        after = by_head(piece[0, :HALF], e_scale[0, of, :]) + lax.dot_general(
            x_first[0, :, at], b_first[0], (((0,), (0,)), ((), ())), preferred_element_type=f32
        )
        out[0, at, :] = by_head(after, s_scale[0, of, :]) + s_add[0, at, :]

    put(core, mine)
    put(1 - core, other)


def over_replica(value, bits):
    pairs = [(r, r ^ bits) for r in range(2 * CHIPS)]
    return lax.ppermute(value, "replica", pairs)


def over_tensor(value, bits):
    return lax.ppermute(value, "tensor", [(t, t ^ bits) for t in range(4)])


def select(first, counts, plan, after, keep, recv):
    with jax.named_scope("select"):
        return pl.pallas_call(
            partial(select_kernel, first, counts),
            out_shape=[sds((n, ITEM_ROWS, LANES), bf16) for n in counts if n],
            in_specs=[SMEM, ANYWHERE, VMEM, VMEM],
            out_specs=[VMEM for n in counts if n],
            compiler_params=params(),
        )(plan, after, keep, recv)


def exchange(counts, sends):
    bits = [2 * d for d in range(1, CHIPS) if counts[d - 1]]
    return [over_replica(value, b) for value, b in zip(sends, bits)]


def migrate_more(counts, plan, keep, recv):
    came = exchange(counts, select(BASE, counts, plan, keep, keep, recv)) if any(counts) else []
    return pl.pallas_call(
        partial(spread_kernel, counts),
        out_shape=tuple(sds((n, ITEM_ROWS, LANES), bf16) for n in EXTRAS[-1]),
        in_specs=[VMEM] * len(came),
        out_specs=(VMEM,) * (CHIPS - 1),
        compiler_params=params(),
    )(*came)


def local_square(
    x_input,
    z_input,
    bc_input,
    dt_raw,
    dt_bias,
    decay_rates,
    skip_gain,
    conv_x,
    conv_bc,
    norm_gain,
    out_weight,
    cached_states,
    cached_tail_x,
    cached_tail_bc,
    prefix_block,
    lengths,
):
    tokens = x_input.shape[0]
    heads = dt_raw.shape[1]
    features = out_weight.shape[1]
    span = tokens // SLOTS

    with jax.named_scope("pack"):
        send, keep = pl.pallas_call(
            pack_kernel,
            out_shape=(sds((SLOTS, ITEM_ROWS, LANES), bf16),) * 2,
            in_specs=[HBM] * 3,
            out_specs=(VMEM, VMEM),
            scratch_shapes=[
                pltpu.VMEM((2, SLOTS, HALF, LANES), f32),
                pltpu.VMEM((CONV - 1, SLOTS) + cached_tail_x.shape[2:], f32),
                pltpu.VMEM((CONV - 1, SLOTS) + cached_tail_bc.shape[2:], f32),
                pltpu.VMEM((TAIL, LANES), f32),
                pltpu.SemaphoreType.DMA((4,)),
            ],
            compiler_params=params(),
        )(
            in_hbm(cached_states.reshape(SLOTS, ROWS, LANES)),
            in_hbm(jnp.transpose(cached_tail_x, (1, 0, 2))),
            in_hbm(jnp.transpose(cached_tail_bc, (1, 0, 2))),
        )
    recv = over_replica(send, 1)
    with jax.named_scope("plan"):
        plan, variant = pl.pallas_call(
            plan_kernel,
            out_shape=(pltpu.SMEM((PLACE_PLAN + ITEMS,), jnp.int32), pltpu.SMEM((1,), jnp.int32)),
            in_specs=[SMEM],
            out_specs=(SMEM, SMEM),
            compiler_params=params(),
        )(in_hbm(prefix_block))

    more = lax.switch(
        variant.reshape(()),
        [partial(migrate_more, counts) for counts in EXTRAS],
        plan,
        keep,
        recv,
    )
    sends = select((0,) * (CHIPS - 1), BASE, plan, more[0], keep, recv)
    came = exchange(BASE, sends)

    with jax.named_scope("scan"):
        scale = sds((SLOTS, heads, LANES), f32)
        y_in, y_scale, c_mat, s_add, s_scale, e_scale, early, weight = pl.pallas_call(
            scan_kernel,
            out_shape=(
                sds((tokens, ROWS), f32),
                sds((tokens, ROWS), f32),
                sds((tokens, STATE), bf16),
                sds((SLOTS, ROWS, STATE), f32),
                scale,
                scale,
                sds((SLOTS, 6, 8, WIDE), f32),
                pltpu.VMEM(out_weight.shape, bf16),
            ),
            in_specs=[ANYWHERE, SMEM] + [VMEM] * 9 + [HBM],
            out_specs=(VMEM,) * 8,
            scratch_shapes=[pltpu.VMEM((8 + span, WIDE), f32), pltpu.SemaphoreType.DMA((4,))],
            compiler_params=params(),
            cost_estimate=cost(8 << 20, 1 << 30),
        )(
            sends[0],
            lengths,
            x_input,
            z_input,
            bc_input,
            jnp.transpose(dt_raw),
            dt_bias.reshape(1, heads),
            decay_rates.reshape(1, heads),
            skip_gain.reshape(1, heads),
            conv_x,
            conv_bc,
            in_hbm(out_weight),
        )

    def place(owner, after):
        with jax.named_scope("place"):
            return pl.pallas_call(
                partial(place_kernel, owner),
                out_shape=sds((SLOTS, ITEM_ROWS, LANES), bf16),
                in_specs=[SMEM, ANYWHERE] + [VMEM] * 8,
                out_specs=VMEM,
                compiler_params=params(),
            )(plan, after, keep, recv, *came, *more)

    theirs = place(1, c_mat)
    other = over_replica(theirs, 1)
    mine = place(0, theirs)

    quarter = tokens // 4
    spans = [(lo * features // 8, (hi - lo) * features // 16) for lo, hi in CHUNKS]
    sends = []
    gated = None
    for lo, half in spans:
        outs = [sds((2, quarter, half), bf16)] * 2
        call = partial(
            pl.pallas_call,
            partial(send_kernel, gated is None, lo),
            compiler_params=params(),
            cost_estimate=cost(ROWS * half * 4, 2 * tokens * ROWS * half),
        )
        with jax.named_scope("project"):
            if gated is None:
                gated, x_first, b_first, *parts = call(
                    out_shape=[
                        sds((tokens, ROWS), bf16),
                        sds((SLOTS, 8, ROWS), f32),
                        sds((SLOTS, 8, STATE), f32),
                    ]
                    + outs,
                    in_specs=[VMEM] * 8,
                    out_specs=[VMEM] * 5,
                    scratch_shapes=[
                        pltpu.VMEM((SLOTS, ROWS, LANES), bf16),
                        pltpu.VMEM((SLOTS, TAIL, LANES), f32),
                        pltpu.VMEM((SLOTS, 8, WIDE), f32),
                    ],
                )(
                    y_in,
                    y_scale,
                    c_mat,
                    early,
                    mine,
                    other,
                    norm_gain.reshape(1, ROWS),
                    weight,
                )
            else:
                parts = call(
                    out_shape=outs,
                    in_specs=[VMEM] * 2,
                    out_specs=[VMEM] * 2,
                )(gated, weight)
        sends.append(parts)
    with jax.named_scope("project"):
        kept = pl.pallas_call(
            partial(keep_kernel, spans),
            out_shape=[sds((quarter, half), bf16) for _, half in spans for _ in range(4)],
            in_specs=[ANYWHERE] + [VMEM] * 2,
            out_specs=[VMEM] * (4 * len(spans)),
            compiler_params=params(),
            cost_estimate=cost(ROWS * features * 2, tokens * ROWS * features),
        )(sends[-1][0], gated, weight)

    with jax.named_scope("final_states"):

        def of_request(*shape):
            return pl.BlockSpec((1,) + shape, lambda n: (n,) + (0,) * len(shape))

        final_states = pl.pallas_call(
            final_kernel,
            grid=(SLOTS,),
            out_shape=sds((SLOTS, ROWS, STATE), f32),
            in_specs=[
                of_request(ITEM_ROWS, LANES),
                of_request(ITEM_ROWS, LANES),
                of_request(8, ROWS),
                of_request(8, STATE),
                of_request(ROWS, STATE),
                of_request(heads, LANES),
                of_request(heads, LANES),
            ],
            out_specs=of_request(ROWS, STATE),
            compiler_params=params(),
            cost_estimate=cost(4 << 20),
        )(mine, other, x_first, b_first, s_add, s_scale, e_scale)

    with jax.named_scope("sum"):
        came = [(over_tensor(l_send, 1), over_tensor(r_send, 2)) for l_send, r_send in sends]
        passed = []
        for n, (l_came, r_came) in enumerate(came):
            l_own, l_on, r_own, r_on = kept[4 * n : 4 * n + 4]
            onward = (l_on.astype(f32) + l_came[1].astype(f32)).astype(bf16)
            l_last = over_tensor(onward, 2)
            onward = (r_on.astype(f32) + r_came[1].astype(f32)).astype(bf16)
            r_last = over_tensor(onward, 1)
            passed.append(l_own.astype(f32) + l_came[0].astype(f32) + l_last.astype(f32))
            passed.append(r_own.astype(f32) + r_came[0].astype(f32) + r_last.astype(f32))
        mixed = jnp.concatenate(passed, axis=1).astype(bf16)

    return (mixed, final_states.reshape(cached_states.shape))


def solution(mesh):
    placed = (
        P("replica", "tensor"),
        P("replica", "tensor"),
        P("replica", None),
        P("replica", "tensor"),
        P("tensor"),
        P("tensor"),
        P("tensor"),
        P(None, "tensor"),
        P(),
        P("tensor"),
        P("tensor", None),
        P("replica", "tensor", None, None),
        P("replica", None, "tensor"),
        P("replica", None, None),
        P(),
        P("replica"),
    )
    square = mesh.shape["replica"] == 2 * CHIPS and mesh.shape["tensor"] == GROUPS
    return jax.shard_map(
        local_square if square else local_any,
        mesh=mesh,
        in_specs=placed,
        out_specs=(P(("replica", "tensor"), None), P("replica", "tensor", None, None)),
        check_vma=False,
    )
```
